32 devices in a mesh: img: 8 (over z, x), blk: 4 (over y, core).
Axes of the slice: x: 2, y: 2, z: 4, core: 2. Of those that a mesh axis runs over, the one named last changes fastest.
Arguments:
- visible: bfloat16 [404, 8, 768], P('blk', 'img'), may hold values from -6 to 6
- masked_queries: bfloat16 [348, 8, 768], P('blk', 'img'), may hold values from -6 to 6
- visible_counts: int32 [8], P('img'), may hold values from 229 to 403, as said below
- attention_matrices: bfloat16 [2, 4, 768, 768], replicated
- up_projection_weights: bfloat16 [2, 768, 3072], replicated, may hold values from -0.21875 to 0.21875
- down_projection_weights: bfloat16 [2, 3072, 768], replicated, may hold values from -0.109375 to 0.109375
- vectors: float32 [2, 10, 768], replicated
- up_projection_bias: float32 [2, 3072], replicated, may hold values from -3 to 3
- encoder_cotangent: bfloat16 [404, 8, 768], P('blk', 'img'), may hold values from -6 to 6
- cot_regressor: bfloat16 [348, 8, 768], P('blk', 'img'), may hold values from -6 to 6
Outputs:
- encoder_out: bfloat16 [404, 8, 768], P('blk', 'img')
- regressor_out: bfloat16 [348, 8, 768], P('blk', 'img')
- grad_visible: float32 [404, 8, 768], P('blk', 'img')
- grad_masked: float32 [348, 8, 768], P('blk', 'img')
- grad_attn: float32 [2, 4, 768, 768], P(None, None, 'img', 'blk')
- grad_up: float32 [2, 768, 3072], P(None, 'img', 'blk')
- grad_down: float32 [2, 3072, 768], P(None, 'img', 'blk')
- grad_vectors: float32 [2, 10, 768], P(None, None, 'img')
- grad_up_bias: float32 [2, 3072], P(None, 'img')
The draws below stay inside these ranges and needn't reach their ends.
Inputs may be any that keep to these rules, and one draw needn't show every extreme that they name: `visible_counts`: some image has exactly 403 visible patches and some exactly 229.
All inputs are finite; a program needn't handle non-finite values.
Results may differ from the reference program's by a relative error of at most 0.013.
Values may be sent and summed in bfloat16 or wider, within the bound.
No kernel may reach another device: no remote copies, remote signals or barrier semaphores. Data moves between devices by JAX's collectives and lax.ppermute only.
A program may use at most 256 MiB of HBM per device.

```python
import math
import jax
import jax.numpy as jnp
from jax import lax

MODEL_WIDTH = 768
HEADS = 12
HEAD = 64
FF = 3072
NPATCH = 576
VIS_LO = 229
VIS_HI = 403
NVEC = 10
IMG_DEV = 1
VISIBLE_SLOTS = 404
MPAD = 348
IMAGE_TOTAL = 8
N_IMG = 8


def draw_visible_counts(key, part):
    key = jax.random.fold_in(key, 5)
    key_base, key_order = jax.random.split(key)
    counts_base = jax.random.randint(key_base, (IMAGE_TOTAL,), VIS_LO, VIS_HI + 1, dtype=jnp.int32)
    image_order = jax.random.permutation(key_order, IMAGE_TOTAL)
    counts_base = counts_base.at[image_order[0]].set(VIS_HI)
    return counts_base.at[image_order[1]].set(VIS_LO)


def draw_attention_matrices(key, part):
    key = jax.random.fold_in(key, 3)
    base_draw = jax.random.normal(key, (2, 4, MODEL_WIDTH, MODEL_WIDTH), jnp.float32)
    matrix_index = jnp.arange(4)[None, :, None, None]
    factor = jnp.where(matrix_index == 3, 6.0, 1.0) / math.sqrt(MODEL_WIDTH)
    return (base_draw * factor).astype(jnp.bfloat16)


def draw_vectors(key, part):
    key = jax.random.fold_in(key, 7)
    key_spread, key_noise = jax.random.split(key)
    spread = jax.random.uniform(key_spread, (2, NVEC, MODEL_WIDTH), jnp.float32, -1.0, 1.0)
    noise_draw = 0.2 * jax.random.normal(key_noise, (2, NVEC, MODEL_WIDTH), jnp.float32)
    row_index = jnp.arange(NVEC)[None, :, None]
    gain_rows = (row_index == 0) | (row_index == 6)
    scale_rows = (row_index == 5) | (row_index == 9)
    return jnp.where(gain_rows, 1.0 + 0.4 * spread, jnp.where(scale_rows, 1.0 + 0.5 * spread, noise_draw))


def block_scale(own_key, shape, pieces, least, largest):
    factor_of, own = 1.0, jax.random.fold_in(own_key, 6)
    for position, blocks in pieces:
        draws = jnp.exp(jax.random.uniform(jax.random.fold_in(own, position), (blocks,), jnp.float32, least / len(pieces), largest / len(pieces)))
        factor_of = factor_of * jnp.repeat(draws, shape[position] // blocks).reshape([-1 if axis == position else 1 for axis in range(len(shape))])
    return factor_of


def normal_values(rng, shape, deviation, reach, cuts=(), kind=jnp.bfloat16):
    drawn = deviation * jax.random.normal(rng, shape, jnp.float32)
    if cuts:
        drawn = drawn * block_scale(rng, shape, cuts, -0.22, 0.18)
    return jnp.clip(drawn, -reach, reach).astype(kind)


def setup_inputs(seed: int = 0) -> dict:
    keys = jax.random.split(jax.random.key(seed), 11)
    return {
        "visible": normal_values(keys[0], (VISIBLE_SLOTS, IMAGE_TOTAL, MODEL_WIDTH), 1.0, 6.0, ((0, 4), (1, 8))),
        "masked_queries": normal_values(keys[1], (MPAD, IMAGE_TOTAL, MODEL_WIDTH), 1.0, 6.0, ((0, 4), (1, 8))),
        "visible_counts": draw_visible_counts(jax.random.fold_in(keys[10], 71), 0),
        "attention_matrices": draw_attention_matrices(jax.random.fold_in(keys[10], 71), 0),
        "up_projection_weights": normal_values(keys[4], (2, MODEL_WIDTH, FF), MODEL_WIDTH ** -0.5, 0.21875),
        "down_projection_weights": normal_values(keys[5], (2, FF, MODEL_WIDTH), FF ** -0.5, 0.109375),
        "vectors": draw_vectors(jax.random.fold_in(keys[10], 71), 0),
        "up_projection_bias": normal_values(keys[7], (2, FF), 0.5, 3.0, (), jnp.float32),
        "encoder_cotangent": normal_values(keys[8], (VISIBLE_SLOTS, IMAGE_TOTAL, MODEL_WIDTH), 1.0, 6.0, ((0, 4), (1, 8))),
        "cot_regressor": normal_values(keys[9], (MPAD, IMAGE_TOTAL, MODEL_WIDTH), 1.0, 6.0, ((0, 4), (1, 8))),
    }


@jax.custom_vjp
def low(v):
    return lax.optimization_barrier(v.astype(jnp.bfloat16)).astype(jnp.float32)

@jax.custom_vjp
def low_back(v):
    return v

def low_keep(v):
    return (low(v), None)

def low_pass(kept, grad):
    return (grad,)

def back_keep(v):
    return (v, None)

def back_low(kept, grad):
    return (low(grad),)
low.defvjp(low_keep, low_pass)
low_back.defvjp(back_keep, back_low)
EPS = 1e-06
HIGH = lax.Precision.HIGHEST

def both_ways(value):
    return low_back(low(value))

def norm_rows(in_rows, norm_gain, norm_shift):
    row_mean = lax.optimization_barrier(jnp.mean(in_rows, -1, keepdims=True))
    centred = in_rows - row_mean
    return centred * lax.rsqrt(lax.optimization_barrier(jnp.mean(centred * centred, -1, keepdims=True)) + EPS) * norm_gain + norm_shift

def project(in_rows, weight):
    return jnp.dot(in_rows, weight, precision=HIGH)

def split_heads(in_rows):
    return in_rows.reshape(in_rows.shape[0], in_rows.shape[1], HEADS, HEAD)

def attend(queries, key_rows, values, key_mask):
    scores = jnp.einsum('qghd,kghd->ghqk', split_heads(queries), split_heads(key_rows), precision=HIGH) * HEAD ** (-0.5)
    scores = low_back(scores)
    scores = jnp.where(jnp.transpose(key_mask)[:, None, None, :], scores, -1e+30)
    row_top = lax.optimization_barrier(jnp.max(scores, -1, keepdims=True))
    exp_scores = jnp.exp(scores - row_top)
    attn_probs = low(exp_scores / lax.optimization_barrier(jnp.sum(exp_scores, -1, keepdims=True)))
    mixed_heads = jnp.einsum('ghqk,kghd->qghd', attn_probs, split_heads(values), precision=HIGH)
    return mixed_heads.reshape(queries.shape)

def block_layer(in_rows, first_query, key_mask, attn_weight, up_weight, down_weight, vectors_b, up_shift):
    normed = low(norm_rows(in_rows, vectors_b[0], vectors_b[1]))
    queries = both_ways(project(normed[first_query:], attn_weight[0]) + vectors_b[2])
    key_rows = both_ways(project(normed, attn_weight[1]))
    values = both_ways(project(normed, attn_weight[2]) + vectors_b[3])
    mixed_heads = both_ways(attend(queries, key_rows, values, key_mask))
    branch = low_back(project(mixed_heads, attn_weight[3]) + vectors_b[4])
    residual = in_rows[first_query:] + vectors_b[5] * branch
    normed_two = low(norm_rows(residual, vectors_b[6], vectors_b[7]))
    hidden_pre = low_back(project(normed_two, up_weight) + up_shift)
    active = low(jax.nn.gelu(hidden_pre, approximate=False))
    out_branch = low_back(project(active, down_weight) + vectors_b[8])
    return residual + vectors_b[9] * out_branch

def layer(in_rows, query_rows, grouped_counts, attention_matrices, up_projection_weights, down_projection_weights, vectors, up_projection_bias):
    visible_alive = jnp.arange(VISIBLE_SLOTS, dtype=jnp.int32)[:, None] < grouped_counts[None, :]
    masked_alive = jnp.arange(MPAD, dtype=jnp.int32)[:, None] < (NPATCH - grouped_counts)[None, :]
    encoded = block_layer(in_rows, 0, visible_alive, attention_matrices[0], up_projection_weights[0], down_projection_weights[0], vectors[0], up_projection_bias[0])
    encoded = encoded * visible_alive.astype(jnp.float32)[..., None]
    key_source_input = jnp.concatenate([encoded, query_rows], 0)
    regressor_output = block_layer(key_source_input, VISIBLE_SLOTS, jnp.concatenate([visible_alive, masked_alive], 0), attention_matrices[1], up_projection_weights[1], down_projection_weights[1], vectors[1], up_projection_bias[1])
    regressor_output = regressor_output * masked_alive.astype(jnp.float32)[..., None]
    return (encoded, regressor_output)

def reference(visible, masked_queries, visible_counts, attention_matrices, up_projection_weights, down_projection_weights, vectors, up_projection_bias, encoder_cotangent, cot_regressor):
    groups = N_IMG

    def split_group(array):
        return jnp.moveaxis(array.reshape(array.shape[0], groups, IMG_DEV, array.shape[-1]), 1, 0)

    def join_group(array):
        return jnp.moveaxis(array, 0, 1).reshape(array.shape[1], groups * IMG_DEV, array.shape[-1])
    params = (attention_matrices.astype(jnp.float32), up_projection_weights.astype(jnp.float32), down_projection_weights.astype(jnp.float32), vectors, up_projection_bias)
    zero_grads = jax.tree.map(jnp.zeros_like, params)

    def step_group(totals, group):
        in_rows, query_rows, grouped_counts, cot_enc, cot_reg = group

        def forward(rows_arg, query_arg, params_arg):
            return layer(rows_arg, query_arg, grouped_counts, *params_arg)
        outputs, pullback = jax.vjp(forward, in_rows.astype(jnp.float32), query_rows.astype(jnp.float32), params)
        grad_in, grad_query, grad_params = pullback((cot_enc.astype(jnp.float32), cot_reg.astype(jnp.float32)))
        totals = jax.tree.map(jnp.add, totals, grad_params)
        return (totals, (outputs[0], outputs[1], grad_in, grad_query))
    inputs = (split_group(visible), split_group(masked_queries), visible_counts.reshape(groups, IMG_DEV), split_group(encoder_cotangent), split_group(cot_regressor))
    grad_totals, stacked = lax.scan(step_group, zero_grads, inputs)
    encoded, regressor_output, grad_in, grad_query = stacked
    return (join_group(encoded).astype(jnp.bfloat16), join_group(regressor_output).astype(jnp.bfloat16), join_group(grad_in), join_group(grad_query), grad_totals[0], grad_totals[1], grad_totals[2], grad_totals[3], grad_totals[4])
```

```python
import jax
import jax.numpy as jnp
from jax import lax
from jax.sharding import PartitionSpec as P

HEADS = 12
HEAD = 64
NPATCH = 576
EPS = 1e-06
BF = jnp.bfloat16
F32 = jnp.float32


def round_up(value, unit):
    return (value + unit - 1) // unit * unit


def dot(left, right):
    return jnp.dot(left, right, preferred_element_type=F32)


def dot_tb(left, right):
    return lax.dot_general(left, right, (((1,), (1,)), ((), ())), preferred_element_type=F32)


def dot_ta(left, right):
    return lax.dot_general(left, right, (((0,), (0,)), ((), ())), preferred_element_type=F32)


def norm(rows):
    centred = rows - jnp.mean(rows, -1, keepdims=True)
    inverse = lax.rsqrt(jnp.mean(centred * centred, -1, keepdims=True) + EPS)
    return centred * inverse, inverse


def norm_back(grad_out, gain, normed, inverse):
    scaled = grad_out * gain
    return inverse * (
        scaled
        - jnp.mean(scaled, -1, keepdims=True)
        - normed * jnp.mean(scaled * normed, -1, keepdims=True)
    )


def swap(block, axis, offset):
    size = lax.axis_size(axis)
    return lax.ppermute(block, axis, [(i, i ^ offset) for i in range(size)])


def gather(block):
    return [block] + [swap(block, "blk", j) for j in range(1, lax.axis_size("blk"))]


def exchange(blocks):
    return [blocks[0]] + [swap(blocks[j], "blk", j) for j in range(1, len(blocks))]


def reduce_img(parts):
    size = lax.axis_size("img")
    place = lax.axis_index("img")
    bit = 0
    while size > 1:
        mine = (place >> bit) & 1
        pairs = parts.reshape((size // 2, 2) + parts.shape[1:])
        keep = lax.dynamic_index_in_dim(pairs, mine, 1, False)
        sent = lax.dynamic_index_in_dim(pairs, 1 - mine, 1, False)
        got = swap(sent, "img", 1 << bit)
        parts = (keep.astype(F32) + got.astype(F32)).astype(parts.dtype)
        size //= 2
        bit += 1
    return parts[0]


def transpose_owners(part):
    images, cycle = lax.axis_size("img"), lax.axis_size("blk")
    m = images // cycle
    pairs = []
    for i in range(images):
        for b in range(cycle):
            pairs.append((i * cycle + b, (b * m + i % m) * cycle + i // m))
    return lax.ppermute(part, ("img", "blk"), pairs)


def attend(queries, keys, values, alive, heads):
    probs, low, mixed = [], [], []
    for h in range(heads):
        cols = slice(h * HEAD, (h + 1) * HEAD)
        scores = dot_tb(queries[:, cols], keys[:, cols]) * HEAD**-0.5
        scores = jnp.where(alive[None, :], scores, -1e30)
        exps = jnp.exp(scores - jnp.max(scores, -1, keepdims=True))
        p = exps / jnp.sum(exps, -1, keepdims=True)
        pb = p.astype(BF)
        probs.append(p)
        low.append(pb)
        mixed.append(dot(pb, values[:, cols]).astype(BF))
    return jnp.concatenate(mixed, -1), (probs, low)


def attend_back(grad_mixed, queries, keys, values, kept, heads):
    probs, low = kept
    dq, dk, dv = [], [], []
    for h in range(heads):
        cols = slice(h * HEAD, (h + 1) * HEAD)
        do = grad_mixed[:, cols]
        dp = dot_tb(do, values[:, cols])
        ds = probs[h] * (dp - jnp.sum(probs[h] * dp, -1, keepdims=True))
        ds = ds.astype(BF)
        dq.append((dot(ds, keys[:, cols]) * HEAD**-0.5).astype(BF))
        dk.append((dot_ta(ds, queries[:, cols]) * HEAD**-0.5).astype(BF))
        dv.append(dot_ta(low[h], do).astype(BF))
    return jnp.concatenate(dq, -1), jnp.concatenate(dk, -1), jnp.concatenate(dv, -1)


def feed_forward(rows, mixed, weights):
    wo, up, down, vec, up_bias = weights
    r = dot(mixed, wo) + vec[4]
    y = rows + vec[5] * r
    normed, inverse = norm(y)
    h2 = (normed * vec[6] + vec[7]).astype(BF)
    u = dot(h2, up) + up_bias
    a = jax.nn.gelu(u, approximate=False).astype(BF)
    z = dot(a, down) + vec[8]
    out = y + vec[9] * z
    return out, (r, normed, inverse, h2, u, a, z)


def feed_forward_back(grad, kept, weights):
    wo, up, down, vec, up_bias = weights
    r, normed, inverse, h2, u, a, z = kept
    scale2 = jnp.sum(grad * z, 0)
    dz = (grad * vec[9]).astype(BF)
    da = dot_tb(dz, down)
    du = jax.vjp(lambda t: jax.nn.gelu(t, approximate=False), u)[1](da)[0].astype(BF)
    dh2 = dot_tb(du, up)
    gain2 = jnp.sum(dh2 * normed, 0)
    bias2 = jnp.sum(dh2, 0)
    dy = grad + norm_back(dh2, vec[6], normed, inverse)
    scale1 = jnp.sum(dy * r, 0)
    dr = (dy * vec[5]).astype(BF)
    return dz, du, dy, dr, (scale2, gain2, bias2, scale1)


def cut(rows, me, cycle):
    width = rows.shape[1] // cycle
    return [lax.dynamic_slice_in_dim(rows, (me ^ j) * width, width, 1) for j in range(cycle)]


def body(
    visible,
    masked_queries,
    visible_counts,
    attention_matrices,
    up_projection_weights,
    down_projection_weights,
    vectors,
    up_projection_bias,
    encoder_cotangent,
    cot_regressor,
):
    vis, width = visible.shape[0], visible.shape[2]
    hid = masked_queries.shape[0]
    cycle = lax.axis_size("blk")
    images = lax.axis_size("img")
    me = lax.axis_index("blk")
    pv, pm = round_up(vis, 16), round_up(hid, 16)
    share = width // cycle
    heads = HEADS // cycle
    ff = up_projection_weights.shape[2]
    ffb = ff // cycle

    def pad(rows, to):
        return jnp.pad(rows[:, 0, :], ((0, to - rows.shape[0]), (0, 0)))

    x = pad(visible, pv)
    mq = pad(masked_queries, pm)
    count = visible_counts[0]

    def alive_of(rows, padded, limit):
        at = jnp.arange(padded)
        return [((at < rows) & ((me ^ j) * rows + at < limit)) for j in range(cycle)]

    vis_alive = alive_of(vis, pv, count)
    hid_alive = alive_of(hid, pm, NPATCH - count)
    enc_keys = jnp.concatenate(vis_alive)
    reg_keys = jnp.concatenate(vis_alive + hid_alive)
    own_vis = vis_alive[0].astype(F32)[:, None]
    own_hid = hid_alive[0].astype(F32)[:, None]

    def weights_of(block):
        return (
            attention_matrices[block, 3],
            up_projection_weights[block],
            down_projection_weights[block],
            vectors[block],
            up_projection_bias[block],
        )

    def qkv_of(block):
        mats = lax.dynamic_slice_in_dim(attention_matrices[block, :3], me * share, share, 2)
        return jnp.concatenate([mats[0], mats[1], mats[2]], 1)

    def bias_of(block):
        part = lax.dynamic_slice_in_dim(vectors[block], me * share, share, 1)
        return jnp.concatenate([part[2], jnp.zeros_like(part[2]), part[3]])

    enc_w, reg_w = weights_of(0), weights_of(1)
    enc_qkv, reg_qkv = qkv_of(0), qkv_of(1)
    enc_b, reg_b = bias_of(0), bias_of(1)
    s = share

    x_all = jnp.concatenate(gather(x), 0)
    mq_all = jnp.concatenate(gather(mq), 0)
    xn, xinv = norm(x_all.astype(F32))
    h_enc = (xn * vectors[0, 0] + vectors[0, 1]).astype(BF)
    qkv = (dot(h_enc, enc_qkv) + enc_b).astype(BF)
    q0, k0, v0 = qkv[:, :s], qkv[:, s : 2 * s], qkv[:, 2 * s :]
    o0, kept_a0 = attend(q0, k0, v0, enc_keys, heads)
    mixed0 = exchange([o0[j * pv : (j + 1) * pv] for j in range(cycle)])

    def head_order(blocks):
        stacked = jnp.stack(blocks, 1)
        order = me ^ jnp.arange(cycle)
        return jnp.take(stacked, order, axis=1).reshape(stacked.shape[0], -1)

    x_own = x.astype(F32)
    e_out, kept_f0 = feed_forward(x_own, head_order(mixed0), enc_w)
    e_out = e_out * own_vis

    mn, minv = norm(mq_all.astype(F32))
    h_mask = (mn * vectors[1, 0] + vectors[1, 1]).astype(BF)
    qkv_m = (dot(h_mask, reg_qkv) + reg_b).astype(BF)
    en, einv = norm(e_out)
    h_e = (en * vectors[1, 0] + vectors[1, 1]).astype(BF)
    h_vis = jnp.concatenate(gather(h_e), 0)
    kv_e = (dot(h_vis, reg_qkv[:, s:]) + reg_b[s:]).astype(BF)
    q1 = qkv_m[:, :s]
    k1 = jnp.concatenate([kv_e[:, :s], qkv_m[:, s : 2 * s]], 0)
    v1 = jnp.concatenate([kv_e[:, s:], qkv_m[:, 2 * s :]], 0)
    o1, kept_a1 = attend(q1, k1, v1, reg_keys, heads)
    mixed1 = exchange([o1[j * pm : (j + 1) * pm] for j in range(cycle)])
    m_own = mq.astype(F32)
    g_out, kept_f1 = feed_forward(m_own, head_order(mixed1), reg_w)
    g_out = g_out * own_hid

    grad_g = pad(cot_regressor, pm).astype(F32) * own_hid
    dz1, du1, dy1, dr1, small1 = feed_forward_back(grad_g, kept_f1, reg_w)
    dr1_all = jnp.concatenate(gather(dr1), 0)
    reg_wo = lax.dynamic_slice_in_dim(reg_w[0], me * share, share, 0)
    do1 = dot_tb(dr1_all, reg_wo).astype(BF)
    dq1, dk1, dv1 = attend_back(do1, q1, k1, v1, kept_a1, heads)
    nv = cycle * pv
    dkv_e = jnp.concatenate([dk1[:nv], dv1[:nv]], 1)
    dqkv_m = jnp.concatenate([dq1, dk1[nv:], dv1[nv:]], 1)
    part_e = dot_tb(dkv_e, reg_qkv[:, s:]).astype(BF)
    part_m = dot_tb(dqkv_m, reg_qkv).astype(BF)
    dh_e = sum(t.astype(F32) for t in exchange([part_e[j * pv : (j + 1) * pv] for j in range(cycle)]))
    dh_m = sum(t.astype(F32) for t in exchange([part_m[j * pm : (j + 1) * pm] for j in range(cycle)]))
    grad_e = norm_back(dh_e, vectors[1, 0], en, einv)
    mn_own, minv_own = mn[:pm], minv[:pm]
    grad_m = norm_back(dh_m, vectors[1, 0], mn_own, minv_own) + dy1
    gain1_r = jnp.sum(dh_e * en, 0) + jnp.sum(dh_m * mn_own, 0)
    bias1_r = jnp.sum(dh_e, 0) + jnp.sum(dh_m, 0)

    grad_b = (pad(encoder_cotangent, pv).astype(F32) + grad_e) * own_vis
    dz0, du0, dy0, dr0, small0 = feed_forward_back(grad_b, kept_f0, enc_w)
    dr0_all = jnp.concatenate(gather(dr0), 0)
    enc_wo = lax.dynamic_slice_in_dim(enc_w[0], me * share, share, 0)
    do0 = dot_tb(dr0_all, enc_wo).astype(BF)
    dq0, dk0, dv0 = attend_back(do0, q0, k0, v0, kept_a0, heads)
    dqkv0 = jnp.concatenate([dq0, dk0, dv0], 1)
    part_x = dot_tb(dqkv0, enc_qkv).astype(BF)
    dh_x = sum(t.astype(F32) for t in exchange([part_x[j * pv : (j + 1) * pv] for j in range(cycle)]))
    xn_own, xinv_own = xn[:pv], xinv[:pv]
    grad_x = norm_back(dh_x, vectors[0, 0], xn_own, xinv_own) + dy0
    gain1_e = jnp.sum(dh_x * xn_own, 0)
    bias1_e = jnp.sum(dh_x, 0)

    def block_grads(kept, dz, du, o_b, dr_all, h_rows, dqkv, extra):
        h2, a = kept[3], kept[5]
        h2_all = jnp.concatenate(gather(h2), 0)
        dz_all = jnp.concatenate(gather(dz), 0)
        du_b = jnp.concatenate(exchange(cut(du, me, cycle)), 0)
        a_b = jnp.concatenate(exchange(cut(a, me, cycle)), 0)
        d_up = dot_ta(h2_all, du_b).astype(BF)
        d_down = dot_ta(a_b, dz_all).astype(BF)
        d_o = dot_ta(o_b, dr_all).astype(BF)
        d_qkv = dot_ta(h_rows, dqkv)
        if extra is not None:
            d_kv = dot_ta(*extra)
            d_qkv = jnp.concatenate([d_qkv[:, :s], d_qkv[:, s:] + d_kv], 1)
        d_qkv = d_qkv.astype(BF)
        m = images // cycle

        def by_owner(mat):
            rows = mat.shape[0] // m
            return (
                mat.reshape(m, rows, cycle, share)
                .transpose(2, 0, 1, 3)
                .reshape(images, rows, share)
            )

        got_up = reduce_img(d_up.reshape(images, width // images, ffb))
        got_qkv = reduce_img(d_qkv.reshape(images, width // images, 3 * s))
        got_down = transpose_owners(reduce_img(by_owner(d_down)))
        got_o = transpose_owners(reduce_img(by_owner(d_o)))
        attn = jnp.stack([got_qkv[:, :s], got_qkv[:, s : 2 * s], got_qkv[:, 2 * s :], got_o])
        return attn.astype(F32), got_up.astype(F32), got_down.astype(F32), du_b

    attn1, up1, down1, du1_b = block_grads(
        kept_f1, dz1, du1, o1, dr1_all, h_mask, dqkv_m, (h_vis, dkv_e)
    )
    attn0, up0, down0, du0_b = block_grads(kept_f0, dz0, du0, o0, dr0_all, h_enc, dqkv0, None)

    def col_sum(rows):
        return jnp.sum(rows.astype(F32), 0)

    def place(vector, total):
        return lax.dynamic_update_slice_in_dim(
            jnp.zeros((total,), F32), vector, me * vector.shape[0], 0
        )

    def vec_rows(small, gain1, bias1, dqs, dvs, dr, dz):
        scale2, gain2, bias2, scale1 = small
        return jnp.stack(
            [
                gain1,
                bias1,
                place(dqs, width),
                place(dvs, width),
                col_sum(dr),
                scale1,
                gain2,
                bias2,
                col_sum(dz),
                scale2,
            ]
        )

    vec0 = vec_rows(small0, gain1_e, bias1_e, col_sum(dq0), col_sum(dv0), dr0, dz0)
    vec1 = vec_rows(
        small1, gain1_r, bias1_r, col_sum(dq1), col_sum(dv1), dr1, dz1
    )
    vecs = jnp.stack([vec0, vec1]).reshape(20, images, width // images)
    ups_i = jnp.stack([place(col_sum(du0_b), ff), place(col_sum(du1_b), ff)]).reshape(2, images, ff // images)
    flat = jnp.concatenate(
        [
            vecs.transpose(1, 0, 2).reshape(images, -1),
            ups_i.transpose(1, 0, 2).reshape(images, -1),
        ],
        1,
    )
    j = 1
    while j < cycle:
        flat = flat + swap(flat, "blk", j)
        j *= 2
    flat = reduce_img(flat)
    nvec = 20 * (width // images)
    vec_total = flat[:nvec].reshape(2, 10, width // images)
    up_bias_total = flat[nvec:].reshape(2, ff // images)

    def out(rows, count_rows):
        return rows[:count_rows, None, :]

    return (
        out(e_out, vis).astype(BF),
        out(g_out, hid).astype(BF),
        out(grad_x, vis),
        out(grad_m, hid),
        jnp.stack([attn0, attn1]),
        jnp.stack([up0, up1]),
        jnp.stack([down0, down1]),
        vec_total,
        up_bias_total,
    )


def solution(mesh):
    rows = P("blk", "img", None)
    in_specs = (rows, rows, P("img"), P(), P(), P(), P(), P(), rows, rows)
    out_specs = (
        rows,
        rows,
        rows,
        rows,
        P(None, None, "img", "blk"),
        P(None, "img", "blk"),
        P(None, "img", "blk"),
        P(None, None, "img"),
        P(None, "img"),
    )
    return jax.shard_map(body, mesh=mesh, in_specs=in_specs, out_specs=out_specs, check_vma=False)
```

```python
import functools

import jax
import jax.numpy as jnp
from jax import lax
from jax.experimental import pallas as pl
from jax.experimental.pallas import tpu as pltpu
from jax.sharding import PartitionSpec as P

HEADS = 12
HEAD = 64
NPATCH = 576
EPS = 1e-06
BF = jnp.bfloat16
F32 = jnp.float32
CYCLE = 4
MIB = 1024 * 1024


def round_up(value, unit):
    return (value + unit - 1) // unit * unit


def dot(left, right):
    return jnp.dot(left, right, preferred_element_type=F32)


def dot_nt(left, right):
    return lax.dot_general(left, right, (((1,), (1,)), ((), ())), preferred_element_type=F32)


def dot_tn(left, right):
    return lax.dot_general(left, right, (((0,), (0,)), ((), ())), preferred_element_type=F32)


def norm(rows):
    centred = rows - jnp.mean(rows, -1, keepdims=True)
    inverse = lax.rsqrt(jnp.mean(centred * centred, -1, keepdims=True) + EPS)
    return centred * inverse, inverse


def norm_back(grad_out, gain, normed, inverse):
    scaled = grad_out * gain
    return inverse * (
        scaled
        - jnp.mean(scaled, -1, keepdims=True)
        - normed * jnp.mean(scaled * normed, -1, keepdims=True)
    )


def gelu_parts(u):
    cdf = 0.5 * (1.0 + lax.erf(u * 0.7071067811865476))
    slope = cdf + u * (jnp.exp(u * u * -0.5) * 0.3989422804014327)
    return cdf, slope


def col_sum(rows):
    return jnp.sum(rows, 0, keepdims=True)


def swap(block, axis, offset):
    size = lax.axis_size(axis)
    return lax.ppermute(block, axis, [(i, i ^ offset) for i in range(size)])


def gather(block):
    across = swap(block, "blk", 2)
    beside = swap(block, "blk", 1)
    return [block, beside, across, swap(across, "blk", 1)]


def exchange(blocks):
    across, over = swap(blocks[2], "blk", 2), swap(blocks[3], "blk", 3)
    return [blocks[0], swap(blocks[1], "blk", 1), across, over]


def reduce_img(keep, sent, order):
    place = lax.axis_index("img")
    bits = sorted(order[1:], reverse=True)
    tail = keep.shape[1:]
    keep = keep.reshape((2,) * len(bits) + tail)
    sent = sent.reshape((2,) * len(bits) + tail)
    got = swap(sent, "img", 1 << order[0])
    for bit in order[1:]:
        total = (keep.astype(F32) + got.astype(F32)).astype(BF)
        axis = bits.index(bit)
        bits.remove(bit)
        mine = (place >> bit) & 1
        keep = lax.dynamic_index_in_dim(total, mine, axis, False)
        sent = lax.dynamic_index_in_dim(total, 1 - mine, axis, False)
        got = swap(sent, "img", 1 << bit)
    return keep.astype(F32) + got.astype(F32)


def reduce_whole(parts):
    images = parts.shape[0]
    place = lax.axis_index("img")
    pairs = parts.reshape((images // 2, 2) + parts.shape[1:])
    keep = lax.dynamic_index_in_dim(pairs, place & 1, 1, False)
    sent = lax.dynamic_index_in_dim(pairs, 1 - (place & 1), 1, False)
    return reduce_img(keep, sent, list(range(images.bit_length() - 1)))


def transpose_owners(part):
    images, cycle = lax.axis_size("img"), lax.axis_size("blk")
    m = images // cycle
    pairs = []
    for i in range(images):
        for b in range(cycle):
            pairs.append((i * cycle + b, (b * m + i % m) * cycle + i // m))
    return lax.ppermute(part, ("img", "blk"), pairs)


def call(name, kernel, ins, outs, scratch=(), limit=32, flops=0, moved=0):
    spaces = {"s": pltpu.SMEM, "v": pltpu.VMEM, "a": pltpu.HBM}
    return pl.pallas_call(
        kernel,
        name=name,
        out_shape=[jax.ShapeDtypeStruct(s, d) for s, d in outs],
        in_specs=[pl.BlockSpec(memory_space=spaces[k]) for _, k in ins],
        out_specs=[pl.BlockSpec(memory_space=pltpu.VMEM) for _ in outs],
        scratch_shapes=list(scratch),
        compiler_params=pltpu.CompilerParams(vmem_limit_bytes=limit * MIB),
        cost_estimate=pl.CostEstimate(flops=flops, bytes_accessed=moved, transcendentals=0),
    )(*[pltpu.with_memory_space_constraint(a, pltpu.HBM) if k == "a" else a for a, k in ins])


def prep_kernel(scal, attn, vec, w_out, b_out, win, sems):
    me = scal[0]
    share = w_out.shape[3]
    window = win.shape[3]
    odd = me & 1
    start = pl.multiple_of(me * share - odd * (share % 128), 128)
    copies = []
    for blk in range(2):
        for m in range(3):
            copy = pltpu.make_async_copy(
                attn.at[blk, m, :, pl.ds(start, window)], win.at[blk, m], sems.at[blk, m]
            )
            copy.start()
            copies.append((blk, m, copy))
    for blk, m, copy in copies:
        copy.wait()
        for parity in range(2):
            shift = parity * (share % 128)

            @pl.when(odd == parity)
            def _():
                w_out[blk, m] = win[blk, m, :, shift : shift + share]
                if m == 1:
                    b_out[blk, m] = jnp.zeros((1, share), F32)
                else:
                    row = vec[blk, 2 + m // 2 : 3 + m // 2, pl.ds(start, window)]
                    b_out[blk, m] = row[:, shift : shift + share]


def key_bias(me, rows, padded, limit):
    at = lax.broadcasted_iota(jnp.int32, (padded, 1), 0)
    parts = []
    for j in range(CYCLE):
        live = (at < rows) & (at + (me ^ j) * rows < limit)
        parts.append(jnp.where(live, 0.0, -1e30))
    return jnp.concatenate(parts, 0)


def own_live(me, rows, padded, limit):
    at = lax.broadcasted_iota(jnp.int32, (padded, 1), 0)
    return jnp.where((at < rows) & (at + me * rows < limit), 1.0, 0.0)


def probs_t(keys, queries, bias):
    scores = dot_nt(keys, queries) + bias
    exps = jnp.exp(scores - jnp.max(scores, 0, keepdims=True))
    return exps * (1.0 / jnp.sum(exps, 0, keepdims=True))


def attend_t(q, k, v, bias, out_ref):
    qs = (q.astype(F32) * HEAD**-0.5).astype(BF)
    vt = v.astype(F32).T.astype(BF)
    mixed = []
    for h in range(q.shape[1] // HEAD):
        c = slice(h * HEAD, (h + 1) * HEAD)
        p = probs_t(k[:, c], qs[:, c], bias).astype(BF)
        mixed.append(dot(vt[c], p))
    out_ref[...] = jnp.concatenate(mixed, 0).T.astype(BF)


def attend_back_t(q, k, v, do, bias):
    qs = (q.astype(F32) * HEAD**-0.5).astype(BF)
    kt = (k.astype(F32) * HEAD**-0.5).T.astype(BF)
    dq, dk, dv = [], [], []
    for h in range(q.shape[1] // HEAD):
        c = slice(h * HEAD, (h + 1) * HEAD)
        p = probs_t(k[:, c], qs[:, c], bias)
        dp = dot_nt(v[:, c], do[:, c])
        ds = (p * (dp - jnp.sum(p * dp, 0, keepdims=True))).astype(BF)
        dv.append(dot(p.astype(BF), do[:, c]))
        dk.append(dot(ds, qs[:, c]))
        dq.append(dot(kt[c], ds))
    return (
        jnp.concatenate(dq, 0).T.astype(BF),
        jnp.concatenate(dk, 1).astype(BF),
        jnp.concatenate(dv, 1).astype(BF),
    )


def enc_attend_kernel(vis, scal, x0, x1, x2, x3, w, b, vec, h_out, q_out, k_out, v_out, o_out):
    me, count = scal[0], scal[1]
    padded = x0.shape[0]
    for j, ref in enumerate((x0, x1, x2, x3)):
        n, _ = norm(ref[...].astype(F32))
        h_out[j * padded : (j + 1) * padded] = (n * vec[0, 0:1] + vec[0, 1:2]).astype(BF)
    h = h_out[...]
    q = (dot(h, w[0, 0]) + b[0, 0]).astype(BF)
    k = dot(h, w[0, 1]).astype(BF)
    v = (dot(h, w[0, 2]) + b[0, 2]).astype(BF)
    q_out[...], k_out[...], v_out[...] = q, k, v
    attend_t(q, k, v, key_bias(me, vis, padded, count), o_out)


def mask_project_kernel(x0, x1, x2, x3, w, b, vec, h_out, q_out, k_out, v_out):
    padded = x0.shape[0]
    for j, ref in enumerate((x0, x1, x2, x3)):
        n, _ = norm(ref[...].astype(F32))
        h_out[j * padded : (j + 1) * padded] = (n * vec[1, 0:1] + vec[1, 1:2]).astype(BF)
    h = h_out[...]
    q_out[...] = (dot(h, w[1, 0]) + b[1, 0]).astype(BF)
    k_out[...] = dot(h, w[1, 1]).astype(BF)
    v_out[...] = (dot(h, w[1, 2]) + b[1, 2]).astype(BF)


def reg_attend_kernel(
    vis, hid, scal, x0, x1, x2, x3, w, b, qm, km, vm, h_out, k_out, v_out, o_out
):
    me, count = scal[0], scal[1]
    padded = x0.shape[0]
    nv = CYCLE * padded
    for j, ref in enumerate((x0, x1, x2, x3)):
        h_out[j * padded : (j + 1) * padded] = ref[...]
    h = h_out[...]
    k_out[0:nv] = dot(h, w[1, 1]).astype(BF)
    v_out[0:nv] = (dot(h, w[1, 2]) + b[1, 2]).astype(BF)
    k_out[nv:] = km[...]
    v_out[nv:] = vm[...]
    bias = jnp.concatenate(
        [
            key_bias(me, vis, padded, count),
            key_bias(me, hid, qm.shape[0] // CYCLE, NPATCH - count),
        ],
        0,
    )
    attend_t(qm[...], k_out[...], v_out[...], bias, o_out)


def assemble(me, blocks, scratch, lane):
    share = blocks[0].shape[1] if lane is None else lane[1]
    for m in range(CYCLE):

        @pl.when(me == m)
        def _():
            for j, ref in enumerate(blocks):
                at = (m ^ j) * share
                value = ref[...] if lane is None else ref[:, lane[0] : lane[0] + share]
                scratch[:, at : at + share] = value


def ffn_copies(blk, attn, up, down, wo_s, up_s, down_s, sems):
    width = up_s.shape[2]
    copies = {}
    if wo_s is not None:
        copies["o"] = pltpu.make_async_copy(attn.at[blk, 3], wo_s, sems.at[0])
    for c in range(up_s.shape[0]):
        copies["u", c] = pltpu.make_async_copy(
            up.at[blk, :, pl.ds(c * width, width)], up_s.at[c], sems.at[1 + 2 * c]
        )
        copies["d", c] = pltpu.make_async_copy(
            down.at[blk, pl.ds(c * width, width), :], down_s.at[c], sems.at[2 + 2 * c]
        )
    for copy in copies.values():
        copy.start()
    return copies


def ffn_forward(blk, copies, rows, mixed, vec, upb, wo_s, up_s, down_s, gp, act):
    copies["o"].wait()
    r = dot(mixed, wo_s[...]) + vec[blk, 4:5]
    y = rows + vec[blk, 5:6] * r
    n, _ = norm(y)
    h2 = (n * vec[blk, 6:7] + vec[blk, 7:8]).astype(BF)
    width = up_s.shape[2]
    z = vec[blk, 8:9]
    for c in range(up_s.shape[0]):
        cols = slice(c * width, (c + 1) * width)
        copies["u", c].wait()
        u = dot(h2, up_s[c]) + upb[blk : blk + 1, cols]
        cdf, slope = gelu_parts(u)
        gp[:, cols] = slope
        a = (u * cdf).astype(BF)
        copies["d", c].wait()
        z = z + dot(a, down_s[c])
    return r, y, h2, z


def ffn_backward(blk, copies, grad, r, y, z, vec, up_s, down_s, gp):
    n, inverse = norm(y)
    scale2 = col_sum(grad * z)
    dz = (grad * vec[blk, 9:10]).astype(BF)
    width = up_s.shape[2]
    dh2 = 0.0
    for c in range(up_s.shape[0]):
        cols = slice(c * width, (c + 1) * width)
        if copies is not None:
            copies["d", c].wait()
        da = dot_nt(dz, down_s[c])
        du = (gp[:, cols] * da).astype(BF)
        if copies is not None:
            copies["u", c].wait()
        dh2 = dh2 + dot_nt(du, up_s[c])
    dy = grad + norm_back(dh2, vec[blk, 6:7], n, inverse)
    dr = (dy * vec[blk, 5:6]).astype(BF)
    small = [
        scale2,
        col_sum(dh2 * n),
        col_sum(dh2),
        col_sum(dy * r),
        col_sum(dz.astype(F32)),
        col_sum(dr.astype(F32)),
    ]
    return dz, dy, dr, small


def enc_ffn_kernel(
    vis, scal, o0, o1, o2, o3, x, vec, upb, attn, up, down,
    e_out, eb_out, he_out, h2_out, y_out, r_out, z_out, gp_out,
    mixed, wo_s, up_s, down_s, sems,
):
    me, count = scal[0], scal[1]
    copies = ffn_copies(0, attn, up, down, wo_s, up_s, down_s, sems)
    assemble(me, (o0, o1, o2, o3), mixed, None)
    r, y, h2, z = ffn_forward(
        0, copies, x[...].astype(F32), mixed[...], vec, upb, wo_s, up_s, down_s, gp_out, None
    )
    h2_out[...], y_out[...], r_out[...], z_out[...] = h2, y, r, z
    e = (y + vec[0, 9:10] * z) * own_live(me, vis, x.shape[0], count)
    e_out[...] = e
    eb_out[...] = e[0 : eb_out.shape[0]].astype(BF)
    n, _ = norm(e)
    he_out[...] = (n * vec[1, 0:1] + vec[1, 1:2]).astype(BF)


def reg_ffn_kernel(
    hid, scal, o0, o1, o2, o3, x, cot, vec, upb, attn, up, down,
    gb_out, pair_out, dr_out, dy_out, small_out,
    mixed, gp, wo_s, up_s, down_s, sems,
):
    me, count = scal[0], scal[1]
    copies = ffn_copies(1, attn, up, down, wo_s, up_s, down_s, sems)
    assemble(me, (o0, o1, o2, o3), mixed, None)
    r, y, h2, z = ffn_forward(
        1, copies, x[...].astype(F32), mixed[...], vec, upb, wo_s, up_s, down_s, gp, None
    )
    padded = x.shape[0]
    live = own_live(me, hid, padded, NPATCH - count)
    g = (y + vec[1, 9:10] * z) * live
    gb_out[...] = g[0 : gb_out.shape[0]].astype(BF)
    grad = cot[...].astype(F32) * live
    dz, dy, dr, small = ffn_backward(1, None, grad, r, y, z, vec, up_s, down_s, gp)
    pair_out[0:padded] = h2
    pair_out[padded:] = dz
    dr_out[...] = dr
    dy_out[...] = dy
    for i, row in enumerate(small):
        small_out[i : i + 1] = row
    small_out[6:8] = jnp.zeros((2, small_out.shape[1]), F32)


def enc_ffn_back_kernel(
    vis, scal, g0, g1, g2, g3, e, cot, y, r, z, gp, vec, attn, up, down,
    dz_out, dr_out, dy_out, small_out,
    dk, dv, wk, wv, up_s, down_s, ksems, sems,
):
    me, count = scal[0], scal[1]
    first = [
        pltpu.make_async_copy(attn.at[1, 1], wk, ksems.at[0]),
        pltpu.make_async_copy(attn.at[1, 2], wv, ksems.at[1]),
    ]
    for copy in first:
        copy.start()
    copies = ffn_copies(0, attn, up, down, None, up_s, down_s, sems)
    share = g0.shape[1] // 2
    assemble(me, (g0, g1, g2, g3), dk, (0, share))
    assemble(me, (g0, g1, g2, g3), dv, (share, share))
    n, inverse = norm(e[...])
    first[0].wait()
    first[1].wait()
    dh = dot_nt(dk[...], wk[...]) + dot_nt(dv[...], wv[...])
    grad_e = norm_back(dh, vec[1, 0:1], n, inverse)
    grad = (cot[...].astype(F32) + grad_e) * own_live(me, vis, cot.shape[0], count)
    dz, dy, dr, small = ffn_backward(
        0, copies, grad, r[...], y[...], z[...], vec, up_s, down_s, gp
    )
    dz_out[...], dy_out[...], dr_out[...] = dz, dy, dr
    for i, row in enumerate(small + [col_sum(dh * n), col_sum(dh)]):
        small_out[i : i + 1] = row


def spread(result, place_of, keep, sent, mine, bit, rows, cols):
    for i in range(8):
        t = (i >> (bit + 1) << bit) | (i & ((1 << bit) - 1))
        value = place_of(i)

        for side in range(2):
            target = keep if side == ((i >> bit) & 1) else sent

            @pl.when(mine == side)
            def _():
                target[t, rows, cols] = value


def qkv_grad(h, dqkv, keep, sent, mine, bit, nat):
    share = dqkv[0].shape[1]
    for m, grad in enumerate(dqkv):
        result = dot_tn(h, grad).astype(BF)
        cols = slice(m * share, (m + 1) * share)
        if nat is not None:
            nat[:, cols] = result
        else:
            step = result.shape[0] // 8
            spread(
                result, lambda i: result[i * step : (i + 1) * step], keep, sent, mine, bit,
                slice(0, step), cols,
            )


def reg_attend_back_kernel(
    vis, hid, scal, d0, d1, d2, d3, q, k, v, attn,
    e_out, m_out, qv_out,
    dr, wo, sems,
):
    me, count = scal[0], scal[1]
    share = q.shape[1]
    copy = pltpu.make_async_copy(attn.at[1, 3, pl.ds(me * share, share), :], wo, sems.at[0])
    copy.start()
    padded = d0.shape[0]
    for j, ref in enumerate((d0, d1, d2, d3)):
        dr[j * padded : (j + 1) * padded] = ref[...]
    copy.wait()
    do = dot_nt(dr[...], wo[...]).astype(BF)
    nm = CYCLE * padded
    nv = k.shape[0] - nm
    bias = jnp.concatenate(
        [
            key_bias(me, vis, nv // CYCLE, count),
            key_bias(me, hid, padded, NPATCH - count),
        ],
        0,
    )
    dq, dk, dv = attend_back_t(q[...], k[...], v[...], do, bias)
    e_out[:, 0:share] = dk[0:nv]
    e_out[:, share:] = dv[0:nv]
    m_out[:, 0:share] = dq
    m_out[:, share : 2 * share] = dk[nv:]
    m_out[:, 2 * share :] = dv[nv:]
    qv_out[0:1] = col_sum(dq.astype(F32))
    qv_out[1:2] = col_sum(dv.astype(F32))
    qv_out[2:8] = jnp.zeros((6, share), F32)


def reg_qkv_grad_kernel(bit, natural, scal, h_m, h_e, g_m, g_e, *refs):
    keep, sent, nat = (None, None, refs[0]) if natural else (refs[0], refs[1], None)
    mine = (scal[2] >> bit) & 1
    share = g_e.shape[1] // 2
    h = jnp.concatenate([h_e[...], h_m[...]], 0)
    none = jnp.zeros((h_e.shape[0], share), BF)
    grads = []
    for m in range(3):
        top = none if m == 0 else g_e[:, (m - 1) * share : m * share]
        grads.append(jnp.concatenate([top, g_m[:, m * share : (m + 1) * share]], 0))
    qkv_grad(h, grads, keep, sent, mine, bit, nat)


def enc_attend_back_kernel(
    vis, bit, natural, scal, d0, d1, d2, d3, h, q, k, v, attn, *refs
):
    if natural:
        g_out, qv_out, nat, dr, wo, sems = refs
        keep = sent = None
    else:
        g_out, qv_out, keep, sent, dr, wo, sems = refs
        nat = None
    me, count = scal[0], scal[1]
    share = q.shape[1]
    copy = pltpu.make_async_copy(attn.at[0, 3, pl.ds(me * share, share), :], wo, sems.at[0])
    copy.start()
    padded = d0.shape[0]
    for j, ref in enumerate((d0, d1, d2, d3)):
        dr[j * padded : (j + 1) * padded] = ref[...]
    copy.wait()
    do = dot_nt(dr[...], wo[...]).astype(BF)
    dq, dk, dv = attend_back_t(
        q[...], k[...], v[...], do, key_bias(me, vis, padded, count)
    )
    g_out[:, 0:share] = dq
    g_out[:, share : 2 * share] = dk
    g_out[:, 2 * share :] = dv
    qv_out[0:1] = col_sum(dq.astype(F32))
    qv_out[1:2] = col_sum(dv.astype(F32))
    qv_out[2:8] = jnp.zeros((6, share), F32)
    qkv_grad(h[...], (dq, dk, dv), keep, sent, (scal[2] >> bit) & 1, bit, nat)


def ffn_grad_kernel(blk, bits, natural, paired, scal, *refs):
    if paired:
        pairs, refs = refs[:4], refs[4:]
        padded = pairs[0].shape[0] // 2
    else:
        h2s, dzs, refs = refs[:4], refs[4:8], refs[8:]
        padded = h2s[0].shape[0]
    drs, (o, upb, up, down), refs = refs[:4], refs[4:8], refs[8:]
    if natural:
        nat_up, nat_down, nat_o, sum_out, h2, dz, dr, wu, wd, sems = refs
    else:
        keep_a, sent_a, keep_b, sent_b, sum_out, h2, dz, dr, wu, wd, sems = refs
    me, place = scal[0], scal[2]
    width = wu.shape[1]
    cols = pl.ds(pl.multiple_of(me * width, 128), width)
    copies = [
        pltpu.make_async_copy(up.at[blk, :, cols], wu, sems.at[0]),
        pltpu.make_async_copy(down.at[blk, cols, :], wd, sems.at[1]),
    ]
    for copy in copies:
        copy.start()
    for j in range(CYCLE):
        at = slice(j * padded, (j + 1) * padded)
        if paired:
            h2[at] = pairs[j][0:padded]
            dz[at] = pairs[j][padded:]
        else:
            h2[at] = h2s[j][...]
            dz[at] = dzs[j][...]
        dr[at] = drs[j][...]
    copies[0].wait()
    u = dot(h2[...], wu[...]) + upb[blk : blk + 1, cols]
    cdf, slope = gelu_parts(u)
    a = (u * cdf).astype(BF)
    d_down = dot_tn(a, dz[...])
    d_o = dot_tn(o[...], dr[...])
    copies[1].wait()
    du = (slope * dot_nt(dz[...], wd[...])).astype(BF)
    sum_out[0:1] = col_sum(du.astype(F32))
    sum_out[1:8] = jnp.zeros((7, width), F32)
    d_up = dot_tn(h2[...], du).astype(BF)
    if natural:
        nat_up[...] = d_up
        nat_down[...] = d_down.astype(BF)
        nat_o[...] = d_o.astype(BF)
        return
    step = width // 8
    share = o.shape[1]
    bit_a, bit_b = bits
    mine_a, mine_b = (place >> bit_a) & 1, (place >> bit_b) & 1
    spread(
        None, lambda i: d_up[i * step : (i + 1) * step], keep_b, sent_b, mine_b, bit_b,
        slice(0, step), slice(0, width),
    )

    def down_piece(i):
        quarter, half = i >> 1, i & 1
        rows = d_down.shape[0] // 2
        part = d_down[half * rows : (half + 1) * rows, quarter * share : (quarter + 1) * share]
        return jnp.concatenate([part[k * step : (k + 1) * step] for k in range(4)], 1).astype(BF)

    def o_piece(i):
        quarter, half = i >> 1, i & 1
        rows = d_o.shape[0] // 2
        part = d_o[half * rows : (half + 1) * rows, quarter * share : (quarter + 1) * share]
        third = rows // 3
        parts = [part[k * third : (k + 1) * third] for k in range(3)]
        return jnp.concatenate(parts + [jnp.zeros((third, share), F32)], 1).astype(BF)

    spread(
        None, down_piece, keep_a, sent_a, mine_a, bit_a, slice(0, step), slice(0, width)
    )
    spread(
        None, o_piece, keep_a, sent_a, mine_a, bit_a, slice(step, step + 32), slice(0, width)
    )


def input_grad_kernel(blk, masked, scal, g0, g1, g2, g3, x, dy, vec, attn, out, small_out,
                      dq, dk, dv, w, sems):
    me = scal[0]
    copies = [pltpu.make_async_copy(attn.at[blk, m], w.at[m], sems.at[m]) for m in range(3)]
    for copy in copies:
        copy.start()
    share = g0.shape[1] // 3
    grads = (dq, dk, dv)
    for m, ref in enumerate(grads):
        assemble(me, (g0, g1, g2, g3), ref, (m * share, share))
    n, inverse = norm(x[...].astype(F32))
    dh = 0.0
    for m, ref in enumerate(grads):
        copies[m].wait()
        dh = dh + dot_nt(ref[...], w[m])
    dx = norm_back(dh, vec[blk, 0:1], n, inverse) + dy[...]
    out[...] = dx[0 : out.shape[0]]
    small_out[0:1] = col_sum(dh * n)
    small_out[1:2] = col_sum(dh)
    small_out[2:8] = jnp.zeros((6, small_out.shape[1]), F32)


def vector_kernel(scal, small0, small1, small_m, small_x, sum0, sum1, qv0, qv1, out):
    me = scal[0]
    share = qv0.shape[1]
    out[...] = jnp.zeros(out.shape, F32)
    gains = (
        (small_x[0:1], small_x[1:2]),
        (small0[6:7] + small_m[0:1], small0[7:8] + small_m[1:2]),
    )
    for blk, (small, qv, sums) in enumerate(((small0, qv0, sum0), (small1, qv1, sum1))):
        at = 10 * blk
        scale2, gain2, bias2, scale1, dzs, drs = [small[i : i + 1] for i in range(6)]
        rows = {0: gains[blk][0], 1: gains[blk][1], 4: drs, 5: scale1, 6: gain2, 7: bias2,
                8: dzs, 9: scale2}
        for i, row in rows.items():
            out[at + i : at + i + 1] = row
        for m in range(CYCLE):

            @pl.when(me == m)
            def _():
                cols = slice(m * share, (m + 1) * share)
                out[at + 2 : at + 3, cols] = qv[0:1]
                out[at + 3 : at + 4, cols] = qv[1:2]
                out[20 + 4 * blk + m : 21 + 4 * blk + m] = sums[0:1]


def body(
    visible,
    masked_queries,
    visible_counts,
    attention_matrices,
    up_projection_weights,
    down_projection_weights,
    vectors,
    up_projection_bias,
    encoder_cotangent,
    cot_regressor,
):
    vis, width = visible.shape[0], visible.shape[2]
    hid = masked_queries.shape[0]
    images = lax.axis_size("img")
    me = lax.axis_index("blk")
    place = lax.axis_index("img")
    pv, pm = round_up(vis, 16), round_up(hid, 16)
    nv, nm = CYCLE * pv, CYCLE * pm
    s = width // CYCLE
    ff = up_projection_weights.shape[2]
    ffb = ff // CYCLE
    natural = images != 8
    attn, up, down = attention_matrices, up_projection_weights, down_projection_weights
    vec, upb = vectors, up_projection_bias
    dma = pltpu.SemaphoreType.DMA

    def pad(rows, to):
        return jnp.pad(rows[:, 0, :], ((0, to - rows.shape[0]), (0, 0)))

    def many(arrays, kind="v"):
        return [(a, kind) for a in arrays]

    x = pad(visible, pv)
    xs = gather(x)
    mq = pad(masked_queries, pm)
    mqs = gather(mq)
    cot_e, cot_g = pad(encoder_cotangent, pv), pad(cot_regressor, pm)
    scal = jnp.stack([me, visible_counts[0], place]).astype(jnp.int32)

    w_own, b_own = call(
        "prep",
        prep_kernel,
        [(scal, "s"), (attn, "a"), (vec, "v")],
        [((2, 3, width, s), BF), ((2, 3, 1, s), F32)],
        [pltpu.VMEM((2, 3, width, s + s % 128), BF), dma((2, 3))],
    )

    h0, q0, k0, v0, o0 = call(
        "enc_attend",
        functools.partial(enc_attend_kernel, vis),
        [(scal, "s")] + many(xs) + many([w_own, b_own, vec]),
        [((nv, width), BF)] + [((nv, s), BF)] * 4,
    )
    mixed0 = exchange([o0[j * pv : (j + 1) * pv] for j in range(CYCLE)])
    chunks = ff // width
    weights_scratch = [
        pltpu.VMEM((chunks, width, width), BF),
        pltpu.VMEM((chunks, width, width), BF),
        dma((1 + 2 * chunks,)),
    ]
    square = pltpu.VMEM((width, width), BF)
    e, e_b, he, h2_0, y0, r0, z0, gp0 = call(
        "enc_ffn",
        functools.partial(enc_ffn_kernel, vis),
        [(scal, "s")] + many(mixed0) + many([x, vec, upb]) + many([attn, up, down], "a"),
        [((pv, width), F32), ((vis, width), BF), ((pv, width), BF), ((pv, width), BF)]
        + [((pv, width), F32)] * 3
        + [((pv, ff), F32)],
        [pltpu.VMEM((pv, width), BF), square] + weights_scratch,
    )

    hm, qm, km, vm = call(
        "mask_project",
        mask_project_kernel,
        many(mqs) + many([w_own, b_own, vec]),
        [((nm, width), BF)] + [((nm, s), BF)] * 3,
    )
    hes = gather(he)
    h_vis, k1, v1, o1 = call(
        "reg_attend",
        functools.partial(reg_attend_kernel, vis, hid),
        [(scal, "s")] + many(hes) + many([w_own, b_own, qm, km, vm]),
        [((nv, width), BF), ((nv + nm, s), BF), ((nv + nm, s), BF), ((nm, s), BF)],
    )
    mixed1 = exchange([o1[j * pm : (j + 1) * pm] for j in range(CYCLE)])
    g_b, pair1, dr1, dy1, small1 = call(
        "reg_ffn",
        functools.partial(reg_ffn_kernel, hid),
        [(scal, "s")] + many(mixed1) + many([mq, cot_g, vec, upb]) + many([attn, up, down], "a"),
        [((hid, width), BF), ((2 * pm, width), BF), ((pm, width), BF), ((pm, width), F32)]
        + [((8, width), F32)],
        [pltpu.VMEM((pm, width), BF), pltpu.VMEM((pm, ff), F32), square] + weights_scratch,
    )

    dr1s = gather(dr1)
    pairs1 = gather(pair1)
    ge, gm, qv1 = call(
        "reg_attend_back",
        functools.partial(reg_attend_back_kernel, vis, hid),
        [(scal, "s")] + many(dr1s) + many([qm, k1, v1]) + [(attn, "a")],
        [((nv, 2 * s), BF), ((nm, 3 * s), BF), ((8, s), F32)],
        [pltpu.VMEM((nm, width), BF), pltpu.VMEM((s, width), BF), dma((1,))],
    )
    ges = exchange([ge[j * pv : (j + 1) * pv] for j in range(CYCLE)])
    dz0, dr0, dy0, small0 = call(
        "enc_ffn_back",
        functools.partial(enc_ffn_back_kernel, vis),
        [(scal, "s")]
        + many(ges)
        + many([e, cot_e, y0, r0, z0, gp0, vec])
        + many([attn, up, down], "a"),
        [((pv, width), BF), ((pv, width), BF), ((pv, width), F32), ((8, width), F32)],
        [pltpu.VMEM((pv, width), BF)] * 2 + [square] * 2 + [weights_scratch[0]] * 2
        + [dma((2,)), weights_scratch[2]],
    )

    h2_0s = gather(h2_0)
    dz0s = gather(dz0)
    dr0s = gather(dr0)
    bit_a, bit_b, bit_c = 0, 1, 0
    piece = width // images
    msg = [((images // 2, piece, 3 * s), BF)] * 2
    whole = [((width, 3 * s), BF)]
    out = call(
        "enc_attend_back",
        functools.partial(enc_attend_back_kernel, vis, bit_c, natural),
        [(scal, "s")] + many(dr0s) + many([h0, q0, k0, v0]) + [(attn, "a")],
        [((nv, 3 * s), BF), ((8, s), F32)] + (whole if natural else msg),
        [pltpu.VMEM((nv, width), BF), pltpu.VMEM((s, width), BF), dma((1,))],
    )
    gx, qv0, parts_c0 = out[0], out[1], out[2:]

    parts_c1 = call(
        "reg_qkv_grad",
        functools.partial(reg_qkv_grad_kernel, bit_c, natural),
        [(scal, "s")] + many([hm, h_vis, gm, ge]),
        whole if natural else msg,
    )

    def ffn_grads(blk, sources, drs, o, rows):
        if natural:
            outs = [((width, ffb), BF), ((ffb, width), BF), ((s, width), BF)]
        else:
            outs = [((images // 2, piece + 32, width), BF)] * 2
            outs = outs + [((images // 2, piece, width), BF)] * 2
        return call(
            "ffn_grad",
            functools.partial(ffn_grad_kernel, blk, (bit_a, bit_b), natural, blk == 1),
            [(scal, "s")] + many(sources) + many(drs) + many([o, upb]) + many([up, down], "a"),
            outs + [((8, ffb), F32)],
            [pltpu.VMEM((rows, width), BF)] * 3 + [square] * 2 + [dma((2,))],
        )

    grads1 = ffn_grads(1, pairs1, dr1s, o1, nm)
    grads0 = ffn_grads(0, h2_0s + dz0s, dr0s, o0, nv)
    sum0, sum1 = grads0[-1], grads1[-1]

    def input_grads(blk, g, padded, rows, x_own, dy):
        gs = exchange([g[j * padded : (j + 1) * padded] for j in range(CYCLE)])
        return call(
            "input_grad",
            functools.partial(input_grad_kernel, blk, blk == 1),
            [(scal, "s")] + many(gs) + many([x_own, dy, vec]) + [(attn, "a")],
            [((rows, width), F32), ((8, width), F32)],
            [pltpu.VMEM((padded, width), BF)] * 3
            + [pltpu.VMEM((3, width, width), BF), dma((3,))],
        )

    grad_m, small_m = input_grads(1, gm, pm, hid, mq, dy1)
    grad_x, small_x = input_grads(0, gx, pv, vis, x, dy0)

    def finish(grads, parts_c):
        if natural:
            m = images // CYCLE

            def by_owner(mat):
                rows = mat.shape[0] // m
                return (
                    mat.reshape(m, rows, CYCLE, s)
                    .transpose(2, 0, 1, 3)
                    .reshape(images, rows, s)
                )

            got_up = reduce_whole(grads[0].reshape(images, piece, ffb))
            got_c = reduce_whole(parts_c[0].reshape(images, piece, 3 * s))
            got_down = transpose_owners(reduce_whole(by_owner(grads[1])).astype(BF)).astype(F32)
            got_o = transpose_owners(reduce_whole(by_owner(grads[2])).astype(BF)).astype(F32)
        else:
            got_a = reduce_img(grads[0], grads[1], [0, 1, 2])
            got_a = transpose_owners(got_a.astype(BF)).astype(F32)
            got_up = reduce_img(grads[2], grads[3], [1, 0, 2])
            got_c = reduce_img(parts_c[0], parts_c[1], [0, 1, 2])
            got_down = jnp.concatenate(
                [got_a[:piece, k * s : (k + 1) * s] for k in range(4)], 0
            )
            got_o = jnp.concatenate(
                [got_a[piece:, k * s : (k + 1) * s] for k in range(3)], 0
            )
        got_attn = jnp.stack([got_c[:, :s], got_c[:, s : 2 * s], got_c[:, 2 * s :], got_o])
        return got_attn, got_up, got_down

    attn1, up1, down1 = finish(grads1, parts_c1)
    attn0, up0, down0 = finish(grads0, parts_c0)

    (rows,) = call(
        "vectors",
        vector_kernel,
        [(scal, "s")] + many([small0, small1, small_m, small_x, sum0, sum1, qv0, qv1]),
        [((32, width), F32)],
    )
    for axis in ("blk", "img"):
        j = 1
        while j < lax.axis_size(axis):
            rows = rows + swap(rows, axis, j)
            j *= 2
    vec_total = lax.dynamic_slice_in_dim(rows[:20], place * piece, piece, 1)
    bias_total = lax.dynamic_slice_in_dim(
        rows[20:28].reshape(2, ff), place * (ff // images), ff // images, 1
    )

    return (
        e_b[:, None, :],
        g_b[:, None, :],
        grad_x[:, None, :],
        grad_m[:, None, :],
        jnp.stack([attn0, attn1]),
        jnp.stack([up0, up1]),
        jnp.stack([down0, down1]),
        vec_total.reshape(2, 10, piece),
        bias_total,
    )


def solution(mesh):
    rows = P("blk", "img", None)
    in_specs = (rows, rows, P("img"), P(), P(), P(), P(), P(), rows, rows)
    out_specs = (
        rows,
        rows,
        rows,
        rows,
        P(None, None, "img", "blk"),
        P(None, "img", "blk"),
        P(None, "img", "blk"),
        P(None, None, "img"),
        P(None, "img"),
    )
    return jax.shard_map(body, mesh=mesh, in_specs=in_specs, out_specs=out_specs, check_vma=False)
```

```python
import functools

import jax
import jax.numpy as jnp
from jax import lax
from jax.experimental import pallas as pl
from jax.experimental.pallas import tpu as pltpu
from jax.sharding import PartitionSpec as P

HEADS = 12
HEAD = 64
NPATCH = 576
EPS = 1e-06
BF = jnp.bfloat16
F32 = jnp.float32
CYCLE = 4
MIB = 1024 * 1024


def round_up(value, unit):
    return (value + unit - 1) // unit * unit


def dot(left, right):
    return jnp.dot(left, right, preferred_element_type=F32)


def dot_nt(left, right):
    return lax.dot_general(left, right, (((1,), (1,)), ((), ())), preferred_element_type=F32)


def dot_tn(left, right):
    return lax.dot_general(left, right, (((0,), (0,)), ((), ())), preferred_element_type=F32)


def norm(rows):
    centred = rows - jnp.mean(rows, -1, keepdims=True)
    inverse = lax.rsqrt(jnp.mean(centred * centred, -1, keepdims=True) + EPS)
    return centred * inverse, inverse


def norm_back(grad_out, gain, normed, inverse):
    scaled = grad_out * gain
    return inverse * (
        scaled
        - jnp.mean(scaled, -1, keepdims=True)
        - normed * jnp.mean(scaled * normed, -1, keepdims=True)
    )


def gelu_parts(u):
    cdf = 0.5 * (1.0 + lax.erf(u * 0.7071067811865476))
    slope = cdf + u * (jnp.exp(u * u * -0.5) * 0.3989422804014327)
    return cdf, slope


def col_sum(rows):
    return jnp.sum(rows, 0, keepdims=True)


def swap(block, axis, offset):
    size = lax.axis_size(axis)
    return lax.ppermute(block, axis, [(i, i ^ offset) for i in range(size)])


def gather(block, first=None, second=None):
    across = swap(block if first is None else later(block, first), "blk", 2)
    if second is not None:
        over, beside = swap(later(across, second), "blk", 1), later(block, second)
    else:
        over, beside = swap(across, "blk", 1), block
    return [block, swap(beside, "blk", 1), across, over]


def later(value, *arrays):
    return lax.optimization_barrier((value, *arrays))[0]


def exchange(blocks):
    across, over = swap(blocks[2], "blk", 2), swap(blocks[3], "blk", 3)
    return [blocks[0], swap(blocks[1], "blk", 1), across, over]


class ImgSum:
    def __init__(self, keep, sent, order):
        self.order = list(order)
        self.keep, self.sent, self.got = keep, sent, None

    def step(self, *after):
        bit = self.order.pop(0)
        if self.got is not None:
            total = self.total().astype(BF)
            total = total.reshape((2, total.shape[0] // 2) + total.shape[1:])
            mine = (lax.axis_index("img") >> bit) & 1
            self.keep = lax.dynamic_index_in_dim(total, mine, 0, False)
            self.sent = lax.dynamic_index_in_dim(total, 1 - mine, 0, False)
        if after:
            self.sent = later(self.sent, *after)
        self.got = swap(self.sent, "img", 1 << bit)
        return self.sent

    def total(self):
        return self.keep.astype(F32) + self.got.astype(F32)

    def finish(self):
        while self.order:
            self.step()
        return self.total()[0]


def reduce_whole(parts):
    images = parts.shape[0]
    place = lax.axis_index("img")
    bits = images.bit_length() - 1
    pairs = parts.reshape((2, images // 2) + parts.shape[1:])
    mine = place >> (bits - 1)
    keep = lax.dynamic_index_in_dim(pairs, mine, 0, False)
    sent = lax.dynamic_index_in_dim(pairs, 1 - mine, 0, False)
    return ImgSum(keep, sent, range(bits - 1, -1, -1))


def transpose_owners(part):
    images, cycle = lax.axis_size("img"), lax.axis_size("blk")
    m = images // cycle
    pairs = []
    for i in range(images):
        for b in range(cycle):
            pairs.append((i * cycle + b, (b * m + i % m) * cycle + i // m))
    return lax.ppermute(part, ("img", "blk"), pairs)


def call(name, kernel, ins, outs, scratch=(), limit=24, after=(), cost=1):
    spaces = {"s": pltpu.SMEM, "v": pltpu.VMEM, "a": pltpu.HBM, "n": pl.ANY}
    count = len(ins)
    ins = ins + [(a, "n") for a in after]

    def run(*refs):
        kernel(*refs[:count], *refs[len(ins) :])

    return pl.pallas_call(
        run,
        name=name,
        out_shape=[jax.ShapeDtypeStruct(s, d) for s, d in outs],
        in_specs=[pl.BlockSpec(memory_space=spaces[k]) for _, k in ins],
        out_specs=[pl.BlockSpec(memory_space=pltpu.VMEM) for _ in outs],
        scratch_shapes=list(scratch),
        compiler_params=pltpu.CompilerParams(vmem_limit_bytes=limit * MIB),
        cost_estimate=pl.CostEstimate(flops=int(cost * 1.15e9), bytes_accessed=1, transcendentals=0),
    )(*[pltpu.with_memory_space_constraint(a, pltpu.HBM) if k == "a" else a for a, k in ins])


def step_kernel(bits, scal, *refs):
    count = len(bits)
    ins, outs = refs[: 2 * count], refs[2 * count :]
    for k, bit in enumerate(bits):
        keep, got = ins[2 * k : 2 * k + 2]
        half = keep.shape[0] // 2
        mine = (scal[2] >> bit) & 1
        for side, out in ((mine, outs[2 * k]), (1 - mine, outs[2 * k + 1])):
            at = pl.ds(side * half, half)
            out[...] = (keep[at].astype(F32) + got[at].astype(F32)).astype(BF)


def step_all(scal, sums, after=()):
    fresh = [one for one in sums if one.got is not None]
    if fresh:
        bits = [one.order[0] for one in fresh]
        ins, outs = [(scal, "s")], []
        for one in fresh:
            ins += [(one.keep, "v"), (one.got, "v")]
            half = (one.keep.shape[0] // 2,) + one.keep.shape[1:]
            outs += [(half, BF)] * 2
        parts = call(
            "img_step", functools.partial(step_kernel, bits), ins, outs, after=after, cost=0.001
        )
        for k, one in enumerate(fresh):
            one.keep, one.sent = parts[2 * k : 2 * k + 2]
            one.got = None
    for one in sums:
        one.got = swap(one.sent, "img", 1 << one.order.pop(0))


def prep_kernel(scal, attn, vec, w_out, b_out, win, sems):
    me = scal[0]
    share = w_out.shape[3]
    window = win.shape[3]
    odd = me & 1
    start = pl.multiple_of(me * share - odd * (share % 128), 128)
    copies = []
    for blk in range(2):
        for m in range(3):
            copy = pltpu.make_async_copy(
                attn.at[blk, m, :, pl.ds(start, window)], win.at[blk, m], sems.at[blk, m]
            )
            copy.start()
            copies.append((blk, m, copy))
    for blk, m, copy in copies:
        copy.wait()
        for parity in range(2):
            shift = parity * (share % 128)

            @pl.when(odd == parity)
            def _():
                w_out[blk, m] = win[blk, m, :, shift : shift + share]
                if m == 1:
                    b_out[blk, m] = jnp.zeros((1, share), F32)
                else:
                    row = vec[2 + m // 2, blk : blk + 1, pl.ds(start, window)]
                    b_out[blk, m] = row[:, shift : shift + share]


def key_bias(me, rows, padded, limit):
    at = lax.broadcasted_iota(jnp.int32, (padded, 1), 0)
    parts = []
    for j in range(CYCLE):
        live = (at < rows) & (at + (me ^ j) * rows < limit)
        parts.append(jnp.where(live, 0.0, -1e30))
    return jnp.concatenate(parts, 0)


def own_live(me, rows, padded, limit):
    at = lax.broadcasted_iota(jnp.int32, (padded, 1), 0)
    return jnp.where((at < rows) & (at + me * rows < limit), 1.0, 0.0)


def probs_t(keys, queries, bias):
    scores = dot_nt(keys, queries) + bias
    exps = jnp.exp(scores - jnp.max(scores, 0, keepdims=True))
    return exps * (1.0 / jnp.sum(exps, 0, keepdims=True))


def attend_t(q, k, v, bias, out_ref):
    qs = (q.astype(F32) * HEAD**-0.5).astype(BF)
    vt = v.astype(F32).T.astype(BF)
    mixed = []
    for h in range(q.shape[1] // HEAD):
        c = slice(h * HEAD, (h + 1) * HEAD)
        p = probs_t(k[:, c], qs[:, c], bias).astype(BF)
        mixed.append(dot(vt[c], p))
    out_ref[...] = jnp.concatenate(mixed, 0).T.astype(BF)


def attend_back_t(q, k, v, do, bias):
    qs = (q.astype(F32) * HEAD**-0.5).astype(BF)
    kt = (k.astype(F32) * HEAD**-0.5).T.astype(BF)
    dq, dk, dv = [], [], []
    for h in range(q.shape[1] // HEAD):
        c = slice(h * HEAD, (h + 1) * HEAD)
        p = probs_t(k[:, c], qs[:, c], bias)
        dp = dot_nt(v[:, c], do[:, c])
        ds = (p * (dp - jnp.sum(p * dp, 0, keepdims=True))).astype(BF)
        dv.append(dot(p.astype(BF), do[:, c]))
        dk.append(dot(ds, qs[:, c]))
        dq.append(dot(kt[c], ds))
    return (
        jnp.concatenate(dq, 0).T.astype(BF),
        jnp.concatenate(dk, 1).astype(BF),
        jnp.concatenate(dv, 1).astype(BF),
    )


def enc_attend_kernel(vis, scal, x0, x1, x2, x3, w, b, vec, h_out, q_out, k_out, v_out, o_out):
    me, count = scal[0], scal[1]
    padded = h_out.shape[0] // CYCLE
    for j, ref in enumerate((x0, x1, x2, x3)):
        n, _ = norm(ref[0:padded].astype(F32))
        h_out[j * padded : (j + 1) * padded] = (n * vec[0, 0:1] + vec[1, 0:1]).astype(BF)
    h = h_out[...]
    q = (dot(h, w[0, 0]) + b[0, 0]).astype(BF)
    k = dot(h, w[0, 1]).astype(BF)
    v = (dot(h, w[0, 2]) + b[0, 2]).astype(BF)
    q_out[...], k_out[...], v_out[...] = q, k, v
    attend_t(q, k, v, key_bias(me, vis, padded, count), o_out)


def mask_project_kernel(x0, x1, x2, x3, w, b, vec, h_out, q_out, k_out, v_out):
    padded = h_out.shape[0] // CYCLE
    for j, ref in enumerate((x0, x1, x2, x3)):
        n, _ = norm(ref[x0.shape[0] - padded :].astype(F32))
        h_out[j * padded : (j + 1) * padded] = (n * vec[0, 1:2] + vec[1, 1:2]).astype(BF)
    h = h_out[...]
    q_out[...] = (dot(h, w[1, 0]) + b[1, 0]).astype(BF)
    k_out[...] = dot(h, w[1, 1]).astype(BF)
    v_out[...] = (dot(h, w[1, 2]) + b[1, 2]).astype(BF)


def reg_attend_kernel(
    vis, hid, scal, x0, x1, x2, x3, w, b, qm, km, vm, h_out, k_out, v_out, o_out
):
    me, count = scal[0], scal[1]
    padded = x0.shape[0]
    nv = CYCLE * padded
    for j, ref in enumerate((x0, x1, x2, x3)):
        h_out[j * padded : (j + 1) * padded] = ref[...]
    h = h_out[...]
    k_out[0:nv] = dot(h, w[1, 1]).astype(BF)
    v_out[0:nv] = (dot(h, w[1, 2]) + b[1, 2]).astype(BF)
    k_out[nv:] = km[...]
    v_out[nv:] = vm[...]
    bias = jnp.concatenate(
        [
            key_bias(me, vis, padded, count),
            key_bias(me, hid, qm.shape[0] // CYCLE, NPATCH - count),
        ],
        0,
    )
    attend_t(qm[...], k_out[...], v_out[...], bias, o_out)


def assemble(me, blocks, scratch, lane):
    share = blocks[0].shape[1] if lane is None else lane[1]
    rows = scratch.shape[0]
    for m in range(CYCLE):

        @pl.when(me == m)
        def _():
            for j, ref in enumerate(blocks):
                at = (m ^ j) * share
                value = ref[...] if lane is None else ref[0:rows, lane[0] : lane[0] + share]
                scratch[:, at : at + share] = value


def ffn_copies(blk, attn, up, down, wo_s, up_s, down_s, sems):
    width = up_s.shape[2]
    copies = {}
    if wo_s is not None:
        copies["o"] = pltpu.make_async_copy(attn.at[blk, 3], wo_s, sems.at[0])
    for c in range(up_s.shape[0]):
        copies["u", c] = pltpu.make_async_copy(
            up.at[blk, :, pl.ds(c * width, width)], up_s.at[c], sems.at[1 + 2 * c]
        )
        copies["d", c] = pltpu.make_async_copy(
            down.at[blk, pl.ds(c * width, width), :], down_s.at[c], sems.at[2 + 2 * c]
        )
    for copy in copies.values():
        copy.start()
    return copies


def ffn_forward(blk, copies, rows, mixed, vec, upb, wo_s, up_s, down_s, gp, act):
    copies["o"].wait()
    r = dot(mixed, wo_s[...]) + vec[4, blk : blk + 1]
    y = rows + vec[5, blk : blk + 1] * r
    n, _ = norm(y)
    h2 = (n * vec[6, blk : blk + 1] + vec[7, blk : blk + 1]).astype(BF)
    width = up_s.shape[2]
    z = vec[8, blk : blk + 1]
    for c in range(up_s.shape[0]):
        cols = slice(c * width, (c + 1) * width)
        copies["u", c].wait()
        u = dot(h2, up_s[c]) + upb[blk : blk + 1, cols]
        cdf, slope = gelu_parts(u)
        gp[:, cols] = slope
        a = (u * cdf).astype(BF)
        copies["d", c].wait()
        z = z + dot(a, down_s[c])
    return r, y, h2, z


def ffn_backward(blk, copies, grad, r, y, z, vec, up_s, down_s, gp):
    n, inverse = norm(y)
    scale2 = col_sum(grad * z)
    dz = (grad * vec[9, blk : blk + 1]).astype(BF)
    width = up_s.shape[2]
    dh2 = 0.0
    for c in range(up_s.shape[0]):
        cols = slice(c * width, (c + 1) * width)
        if copies is not None:
            copies["d", c].wait()
        da = dot_nt(dz, down_s[c])
        du = (gp[:, cols] * da).astype(BF)
        if copies is not None:
            copies["u", c].wait()
        dh2 = dh2 + dot_nt(du, up_s[c])
    dy = grad + norm_back(dh2, vec[6, blk : blk + 1], n, inverse)
    dr = (dy * vec[5, blk : blk + 1]).astype(BF)
    small = [
        scale2,
        col_sum(dh2 * n),
        col_sum(dh2),
        col_sum(dy * r),
        col_sum(dz.astype(F32)),
        col_sum(dr.astype(F32)),
    ]
    return dz, dy, dr, small


def enc_ffn_kernel(
    vis, scal, o0, o1, o2, o3, x, vec, upb, attn, up, down,
    e_out, eb_out, he_out, h2_out, y_out, r_out, z_out, gp_out,
    mixed, wo_s, up_s, down_s, sems,
):
    me, count = scal[0], scal[1]
    copies = ffn_copies(0, attn, up, down, wo_s, up_s, down_s, sems)
    assemble(me, (o0, o1, o2, o3), mixed, None)
    r, y, h2, z = ffn_forward(
        0, copies, x[0 : he_out.shape[0]].astype(F32), mixed[...], vec, upb, wo_s, up_s, down_s, gp_out, None
    )
    h2_out[...], y_out[...], r_out[...], z_out[...] = h2, y, r, z
    e = (y + vec[9, 0:1] * z) * own_live(me, vis, he_out.shape[0], count)
    e_out[...] = e
    eb_out[...] = e[0 : eb_out.shape[0]].astype(BF)
    n, _ = norm(e)
    he_out[...] = (n * vec[0, 1:2] + vec[1, 1:2]).astype(BF)


def reg_ffn_kernel(
    hid, scal, o0, o1, o2, o3, x, cot, vec, upb, attn, up, down,
    gb_out, pair_out, dr_out, dy_out, small_out,
    mixed, gp, wo_s, up_s, down_s, sems,
):
    me, count = scal[0], scal[1]
    copies = ffn_copies(1, attn, up, down, wo_s, up_s, down_s, sems)
    assemble(me, (o0, o1, o2, o3), mixed, None)
    r, y, h2, z = ffn_forward(
        1, copies, x[x.shape[0] - dr_out.shape[0] :].astype(F32), mixed[...], vec, upb, wo_s, up_s, down_s, gp, None
    )
    padded = dr_out.shape[0]
    live = own_live(me, hid, padded, NPATCH - count)
    g = (y + vec[9, 1:2] * z) * live
    gb_out[...] = g[0 : gb_out.shape[0]].astype(BF)
    grad = cot[...].astype(F32) * live
    dz, dy, dr, small = ffn_backward(1, None, grad, r, y, z, vec, up_s, down_s, gp)
    pair_out[0:padded] = h2
    pair_out[padded:] = dz
    dr_out[...] = dr
    dy_out[...] = dy
    for i, row in enumerate(small):
        small_out[i : i + 1] = row
    small_out[6:8] = jnp.zeros((2, small_out.shape[1]), F32)


def enc_ffn_back_kernel(
    vis, scal, g0, g1, g2, g3, e, cot, y, r, z, gp, h2, vec, attn, up, down,
    pair_out, dr_out, dy_out, small_out,
    dk, dv, wk, wv, up_s, down_s, ksems, sems,
):
    me, count = scal[0], scal[1]
    first = [
        pltpu.make_async_copy(attn.at[1, 1], wk, ksems.at[0]),
        pltpu.make_async_copy(attn.at[1, 2], wv, ksems.at[1]),
    ]
    for copy in first:
        copy.start()
    copies = ffn_copies(0, attn, up, down, None, up_s, down_s, sems)
    share = g0.shape[1] // 2
    assemble(me, (g0, g1, g2, g3), dk, (0, share))
    assemble(me, (g0, g1, g2, g3), dv, (share, share))
    n, inverse = norm(e[...])
    first[0].wait()
    first[1].wait()
    dh = dot_nt(dk[...], wk[...]) + dot_nt(dv[...], wv[...])
    grad_e = norm_back(dh, vec[0, 1:2], n, inverse)
    grad = (cot[...].astype(F32) + grad_e) * own_live(me, vis, cot.shape[0], count)
    dz, dy, dr, small = ffn_backward(
        0, copies, grad, r[...], y[...], z[...], vec, up_s, down_s, gp
    )
    pair_out[0 : dz.shape[0]] = h2[...]
    pair_out[dz.shape[0] :] = dz
    dy_out[...], dr_out[...] = dy, dr
    for i, row in enumerate(small + [col_sum(dh * n), col_sum(dh)]):
        small_out[i : i + 1] = row


def spread(place_of, keep, sent, place, order, rows, cols):
    first, second, third = order
    for i in range(8):
        t = 2 * ((i >> second) & 1) + ((i >> third) & 1)
        value = place_of(i)

        for side in range(2):
            target = keep if side == ((i >> first) & 1) else sent

            @pl.when(((place >> first) & 1) == side)
            def _():
                target[t, rows, cols] = value


def owner_piece(mat, i, share, parts):
    quarter, half = i >> 1, i & 1
    rows = mat.shape[0] // 2
    part = mat[half * rows : (half + 1) * rows, quarter * share : (quarter + 1) * share]
    rows = rows // parts
    return jnp.concatenate([part[k * rows : (k + 1) * rows] for k in range(parts)], 1)


def attn_pieces(h, dqkv, o, dr):
    share = dqkv[0].shape[1]
    results = [dot_tn(h, grad).astype(BF) for grad in dqkv]
    d_o = dot_tn(o, dr).astype(BF)
    step = h.shape[1] // 8

    def piece(i):
        parts = [result[i * step : (i + 1) * step] for result in results]
        return jnp.concatenate(parts + [owner_piece(d_o, i, share, 1)], 1)

    return results, d_o, piece


def norm_sums(rows, dqkv, w):
    dh = 0.0
    for m, grad in enumerate(dqkv):
        dh = dh + dot_nt(grad, w[m])
    n, _ = norm(rows.astype(F32))
    return col_sum(dh * n), col_sum(dh)


def store_attn(results, d_o, nats):
    share = d_o.shape[0]
    for m, result in enumerate(results):
        nats[0][:, m * share : (m + 1) * share] = result
    nats[1][...] = d_o


def reg_attend_back_kernel(
    vis, hid, scal, d0, d1, d2, d3, q, k, v, attn,
    e_out, m_out, qv_out,
    dr, wo, sems,
):
    me, count = scal[0], scal[1]
    share = q.shape[1]
    copy = pltpu.make_async_copy(attn.at[1, 3, pl.ds(me * share, share), :], wo, sems.at[0])
    copy.start()
    padded = d0.shape[0]
    for j, ref in enumerate((d0, d1, d2, d3)):
        dr[j * padded : (j + 1) * padded] = ref[...]
    copy.wait()
    do = dot_nt(dr[...], wo[...]).astype(BF)
    nm = CYCLE * padded
    nv = k.shape[0] - nm
    bias = jnp.concatenate(
        [
            key_bias(me, vis, nv // CYCLE, count),
            key_bias(me, hid, padded, NPATCH - count),
        ],
        0,
    )
    dq, dk, dv = attend_back_t(q[...], k[...], v[...], do, bias)
    e_out[:, 0:share] = dk[0:nv]
    e_out[:, share:] = dv[0:nv]
    m_out[:, 0:share] = dq
    m_out[:, share : 2 * share] = dk[nv:]
    m_out[:, 2 * share :] = dv[nv:]
    qv_out[0:1] = col_sum(dq.astype(F32))
    qv_out[1:2] = col_sum(dv.astype(F32))
    qv_out[2:8] = jnp.zeros((6, share), F32)


def enc_attend_back_kernel(
    vis, order, natural, scal, d0, d1, d2, d3, h, q, k, v, o, gm, x0, x1, x2, x3, w, attn,
    g_out, qv_out, norm_out, first, second, dr, wo, sems,
):
    me, count = scal[0], scal[1]
    share = q.shape[1]
    copy = pltpu.make_async_copy(attn.at[0, 3, pl.ds(me * share, share), :], wo, sems.at[0])
    copy.start()
    padded = d0.shape[0]
    for j, ref in enumerate((d0, d1, d2, d3)):
        dr[j * padded : (j + 1) * padded] = ref[...]
    copy.wait()
    do = dot_nt(dr[...], wo[...]).astype(BF)
    dq, dk, dv = attend_back_t(
        q[...], k[...], v[...], do, key_bias(me, vis, padded, count)
    )
    for j in range(CYCLE):
        at = slice(j * padded, (j + 1) * padded)
        for m, grad in enumerate((dq, dk, dv)):
            g_out[me ^ j, 0:padded, m * share : (m + 1) * share] = grad[at]
        more = g_out.shape[1] - padded
        g_out[me ^ j, padded:] = gm[j * more : (j + 1) * more]
    qv_out[0:1] = col_sum(dq.astype(F32))
    qv_out[1:2] = col_sum(dv.astype(F32))
    qv_out[2:8] = jnp.zeros((6, share), F32)
    x = jnp.concatenate([ref[0:padded] for ref in (x0, x1, x2, x3)], 0)
    norm_out[0:1], norm_out[1:2] = norm_sums(x, (dq, dk, dv), (w[0, 0], w[0, 1], w[0, 2]))
    norm_out[2:8] = jnp.zeros((6, norm_out.shape[1]), F32)
    results, d_o, piece = attn_pieces(h[...], (dq, dk, dv), o[...], dr[...])
    if natural:
        store_attn(results, d_o, (first, second))
    else:
        rows = slice(0, h.shape[1] // 8)
        spread(piece, first, second, scal[2], order, rows, slice(0, 4 * share))


def ffn_pieces(blk, scal, pairs, upb, up, down, sum_out, h2, dz, wu, wd, sems):
    me = scal[0]
    width = wu.shape[1]
    cols = pl.ds(pl.multiple_of(me * width, 128), width)
    copies = [
        pltpu.make_async_copy(up.at[blk, :, cols], wu, sems.at[0]),
        pltpu.make_async_copy(down.at[blk, cols, :], wd, sems.at[1]),
    ]
    for copy in copies:
        copy.start()
    padded = pairs[0].shape[0] // 2
    for j, pair in enumerate(pairs):
        at = slice(j * padded, (j + 1) * padded)
        h2[at] = pair[0:padded]
        dz[at] = pair[padded:]
    copies[0].wait()
    u = dot(h2[...], wu[...]) + upb[blk : blk + 1, cols]
    cdf, slope = gelu_parts(u)
    a = (u * cdf).astype(BF)
    d_down = dot_tn(a, dz[...]).astype(BF)
    copies[1].wait()
    du = (slope * dot_nt(dz[...], wd[...])).astype(BF)
    sum_out[0:1] = col_sum(du.astype(F32))
    sum_out[1:8] = jnp.zeros((7, width), F32)
    d_up = dot_tn(h2[...], du).astype(BF)
    step = width // 8
    return (
        d_down,
        d_up,
        lambda i: owner_piece(d_down, i, width // 4, 4),
        lambda i: d_up[i * step : (i + 1) * step],
    )


def vector_rows(natural, me, smalls, norms, qvs, sums, out):
    share, width = qvs[0].shape[1], out.shape[1]
    step = width // 8
    out[...] = jnp.zeros(out.shape, F32)
    for blk, (small, qv, up_sum) in enumerate(zip(smalls, qvs, sums)):
        at = 10 * blk
        gain, bias = norms[blk][0:1], norms[blk][1:2]
        if blk == 1:
            gain, bias = gain + smalls[0][6:7], bias + smalls[0][7:8]
        scale2, gain2, bias2, scale1, dzs, drs = [small[i : i + 1] for i in range(6)]
        rows = {0: gain, 1: bias, 4: drs, 5: scale1, 6: gain2, 7: bias2, 8: dzs, 9: scale2}
        for i, row in rows.items():
            out[at + i : at + i + 1] = row
        first = 20 + 4 * blk
        for m in range(CYCLE):

            @pl.when(me == m)
            def _():
                cols = slice(m * share, (m + 1) * share)
                out[at + 2 : at + 3, cols] = qv[0:1]
                out[at + 3 : at + 4, cols] = qv[1:2]
                if natural:
                    out[first + m : first + m + 1] = up_sum[0:1]
                else:
                    for i in range(2):
                        for k in range(4):
                            start = (2 * m + i) * step
                            out[first + k : first + k + 1, start : start + step] = up_sum[
                                0:1, (4 * i + k) * step : (4 * i + k + 1) * step
                            ]


def enc_ffn_grad_kernel(
    orders, natural, scal, p0, p1, p2, p3, upb, small0, small1, norm0, norm1, qv0, qv1, sum1,
    up, down, *refs,
):
    outs, (rows, sum0, *scratch) = refs[:-7], refs[-7:]
    d_down, d_up, down_piece, up_piece = ffn_pieces(
        0, scal, (p0, p1, p2, p3), upb, up, down, sum0, *scratch
    )
    smalls, norms = (small0, small1), (norm0, norm1)
    vector_rows(natural, scal[0], smalls, norms, (qv0, qv1), (sum0, sum1), rows)
    if natural:
        outs[0][...], outs[1][...] = d_down, d_up
        return
    step = d_up.shape[0] // 8
    here, cols = slice(0, step), slice(0, d_up.shape[1])
    spread(down_piece, outs[0], outs[1], scal[2], orders[0], here, cols)
    spread(up_piece, outs[2], outs[3], scal[2], orders[1], here, cols)

    def vector_piece(i):
        mine = slice(i * step, (i + 1) * step)
        parts = [rows[0:16, mine], rows[16:32, mine]]
        parts.append(jnp.zeros((16, d_up.shape[1] - 2 * step), F32))
        return jnp.concatenate(parts, 1).astype(BF)

    spread(vector_piece, outs[2], outs[3], scal[2], orders[1], slice(step, step + 16), cols)


def reg_grad_kernel(
    orders, natural, scal, p0, p1, p2, p3, upb, h_m, h_e, g_m, g_e, o, d0, d1, d2, d3,
    x0, x1, x2, x3, w, up, down, *refs,
):
    outs, norm_out, scratch, dr = refs[:-8], refs[-8], refs[-7:-1], refs[-1]
    d_down, d_up, down_piece, up_piece = ffn_pieces(
        1, scal, (p0, p1, p2, p3), upb, up, down, *scratch
    )
    share = g_e.shape[1] // 2
    padded = d0.shape[0]
    for j, ref in enumerate((d0, d1, d2, d3)):
        dr[j * padded : (j + 1) * padded] = ref[...]
    x = jnp.concatenate([ref[ref.shape[0] - padded :] for ref in (x0, x1, x2, x3)], 0)
    dqkv_m = [g_m[:, m * share : (m + 1) * share] for m in range(3)]
    norm_out[0:1], norm_out[1:2] = norm_sums(x, dqkv_m, (w[1, 0], w[1, 1], w[1, 2]))
    norm_out[2:8] = jnp.zeros((6, norm_out.shape[1]), F32)
    h = jnp.concatenate([h_e[...], h_m[...]], 0)
    none = jnp.zeros((h_e.shape[0], share), BF)
    grads = []
    for m in range(3):
        top = none if m == 0 else g_e[:, (m - 1) * share : m * share]
        grads.append(jnp.concatenate([top, dqkv_m[m]], 0))
    results, d_o, attn_piece = attn_pieces(h, grads, o[...], dr[...])
    if natural:
        outs[0][...], outs[1][...] = d_down, d_up
        store_attn(results, d_o, outs[2:4])
        return
    step, cols = d_up.shape[0] // 8, slice(0, d_up.shape[1])
    half = step // 2
    for k, piece in enumerate((down_piece, up_piece)):
        keep, sent = outs[2 * k : 2 * k + 2]
        place, order = scal[2], orders[k]
        spread(piece, keep, sent, place, order, slice(0, step), cols)
        spread(
            lambda i: attn_piece(i)[k * half : (k + 1) * half], keep, sent, place, order,
            slice(step, step + half), cols,
        )


def input_grad_kernel(g, x, dy0, dy1, vec, attn, out0, out1, dq, dk, dv, w, sems):
    copies = [
        [pltpu.make_async_copy(attn.at[blk, m], w.at[blk, m], sems.at[blk, m]) for m in range(3)]
        for blk in range(2)
    ]
    for copy in copies[0] + copies[1]:
        copy.start()
    share = g.shape[2] // 3
    grads = (dq, dk, dv)
    for m, ref in enumerate(grads):
        for j in range(CYCLE):
            ref[:, j * share : (j + 1) * share] = g[j, :, m * share : (m + 1) * share]
    first = dy0.shape[0]
    rows = (slice(0, first), slice(first, x.shape[0]))
    for blk, (at, dy, out) in enumerate(((rows[0], dy0, out0), (rows[1], dy1, out1))):
        n, inverse = norm(x[at].astype(F32))
        dh = 0.0
        for m, ref in enumerate(grads):
            copies[blk][m].wait()
            dh = dh + dot_nt(ref[at], w[blk, m])
        dx = norm_back(dh, vec[0, blk : blk + 1], n, inverse) + dy[...]
        out[:, 0, :] = dx[0 : out.shape[0]]


def finish_kernel(scal, *refs):
    (up0, up0_got, attn0, attn0_got, fixed0) = refs[:5]
    (up1, up1_got, down1, down1_got, fixed1) = refs[5:10]
    rows, attn_out, up_out, down_out, vec_out, bias_out = refs[10:]
    place = scal[2]
    piece, share = attn_out.shape[2], attn_out.shape[3]
    half = piece // 2
    first, all_rows = slice(0, half), slice(0, piece)
    second, tail = slice(half, piece), slice(piece, piece + half)
    moves = (
        (0, all_rows, attn0, attn0_got, all_rows),
        (1, first, down1, down1_got, tail),
        (1, second, up1, up1_got, tail),
    )
    for blk, to, keep, got, at in moves:
        for m in range(3):
            cols = slice(m * share, (m + 1) * share)
            attn_out[blk, m, to] = keep[0, at, cols].astype(F32) + got[0, at, cols].astype(F32)
    for blk, keep, got, fixed in ((0, up0, up0_got, fixed0), (1, up1, up1_got, fixed1)):
        up_out[blk] = keep[0, 0:piece].astype(F32) + got[0, 0:piece].astype(F32)
        attn_out[blk, 3] = fixed[:, 4 * share :].astype(F32)
        for k in range(4):
            part = fixed[:, k * share : (k + 1) * share].astype(F32)
            down_out[blk, :, k * piece : (k + 1) * piece] = part.T
    for blk in range(2):
        for k in range(10):
            vec_out[k, blk : blk + 1] = rows[10 * blk + k : 10 * blk + k + 1]
        for k in range(4):
            bias_out[blk : blk + 1, k * piece : (k + 1) * piece] = rows[
                20 + 4 * blk + k : 21 + 4 * blk + k
            ]


def body(
    visible,
    masked_queries,
    visible_counts,
    attention_matrices,
    up_projection_weights,
    down_projection_weights,
    vectors,
    up_projection_bias,
    encoder_cotangent,
    cot_regressor,
):
    vis, width = visible.shape[0], visible.shape[2]
    hid = masked_queries.shape[0]
    images = lax.axis_size("img")
    me = lax.axis_index("blk")
    place = lax.axis_index("img")
    pv, pm = round_up(vis, 16), round_up(hid, 16)
    nv, nm = CYCLE * pv, CYCLE * pm
    s = width // CYCLE
    ff = up_projection_weights.shape[2]
    ffb = ff // CYCLE
    natural = images != 8
    attn, up, down = attention_matrices, up_projection_weights, down_projection_weights
    vec, upb = jnp.swapaxes(vectors, 0, 1), up_projection_bias
    dma = pltpu.SemaphoreType.DMA

    def pad(rows, to):
        return jnp.pad(rows[:, 0, :], ((0, to - rows.shape[0]), (0, 0)))

    def many(arrays, kind="v"):
        return [(a, kind) for a in arrays]

    scal = jnp.stack([me, visible_counts[0], place]).astype(jnp.int32)
    w_own, b_own = call(
        "prep",
        prep_kernel,
        [(scal, "s"), (attn, "a"), (vec, "v")],
        [((2, 3, width, s), BF), ((2, 3, 1, s), F32)],
        [pltpu.VMEM((2, 3, width, s + s % 128), BF), dma((2, 3))],
    )
    x = jnp.concatenate([pad(visible, pv), pad(masked_queries, pm)], 0)
    xs = gather(x, None, b_own)
    cot_e, cot_g = pad(encoder_cotangent, pv), pad(cot_regressor, pm)

    h0, q0, k0, v0, o0 = call(
        "enc_attend",
        functools.partial(enc_attend_kernel, vis),
        [(scal, "s")] + many(xs) + many([w_own, b_own, vec]),
        [((nv, width), BF)] + [((nv, s), BF)] * 4,
    )
    hm, qm, km, vm = call(
        "mask_project",
        mask_project_kernel,
        many(xs) + many([w_own, b_own, vec]),
        [((nm, width), BF)] + [((nm, s), BF)] * 3,
        after=[o0],
    )
    mixed0 = exchange([o0[j * pv : (j + 1) * pv] for j in range(CYCLE)])
    chunks = ff // width
    weights_scratch = [
        pltpu.VMEM((chunks, width, width), BF),
        pltpu.VMEM((chunks, width, width), BF),
        dma((1 + 2 * chunks,)),
    ]
    square = pltpu.VMEM((width, width), BF)
    e, e_b, he, h2_0, y0, r0, z0, gp0 = call(
        "enc_ffn",
        functools.partial(enc_ffn_kernel, vis),
        [(scal, "s")] + many(mixed0) + many([x, vec, upb]) + many([attn, up, down], "a"),
        [((pv, width), F32), ((vis, width), BF), ((pv, width), BF), ((pv, width), BF)]
        + [((pv, width), F32)] * 3
        + [((pv, ff), F32)],
        [pltpu.VMEM((pv, width), BF), square] + weights_scratch,
        after=[km],
    )

    hes = gather(he)
    h_vis, k1, v1, o1 = call(
        "reg_attend",
        functools.partial(reg_attend_kernel, vis, hid),
        [(scal, "s")] + many(hes) + many([w_own, b_own, qm, km, vm]),
        [((nv, width), BF), ((nv + nm, s), BF), ((nv + nm, s), BF), ((nm, s), BF)],
    )
    mixed1 = exchange([o1[j * pm : (j + 1) * pm] for j in range(CYCLE)])
    g_b, pair1, dr1, dy1, small1 = call(
        "reg_ffn",
        functools.partial(reg_ffn_kernel, hid),
        [(scal, "s")] + many(mixed1) + many([x, cot_g, vec, upb]) + many([attn, up, down], "a"),
        [((hid, width), BF), ((2 * pm, width), BF), ((pm, width), BF), ((pm, width), F32)]
        + [((8, width), F32)],
        [pltpu.VMEM((pm, width), BF), pltpu.VMEM((pm, ff), F32), square] + weights_scratch,
    )

    piece = width // images
    m = images // CYCLE
    first_x, first_z = [0, 1, 2], [1, 0, 2]
    split_z, last_z = [1, 2, 0], [0, 2, 1]

    def message(rows):
        return [((images // 2, rows, width), BF)] * 2

    def by_owner(mat):
        count = mat.shape[0] // m
        cut = mat.reshape(m, count, CYCLE, s).transpose(2, 0, 1, 3)
        return reduce_whole(cut.reshape(images, count, s))

    def by_rows(mat):
        return reduce_whole(mat.reshape(images, piece, mat.shape[1]))

    ffn_whole = [((ffb, width), BF), ((width, ffb), BF)]
    attn_whole = [((width, 3 * s), BF), ((s, width), BF)]

    def ffn_scratch(rows):
        return [pltpu.VMEM((rows, width), BF)] * 2 + [square] * 2 + [dma((2,))]

    dr1s = gather(dr1)
    ge, gm, qv1 = call(
        "reg_attend_back",
        functools.partial(reg_attend_back_kernel, vis, hid),
        [(scal, "s")] + many(dr1s) + many([qm, k1, v1]) + [(attn, "a")],
        [((nv, 2 * s), BF), ((nm, 3 * s), BF), ((8, s), F32)],
        [pltpu.VMEM((nm, width), BF), pltpu.VMEM((s, width), BF), dma((1,))],
        cost=6,
    )
    pairs1 = gather(pair1, dr1s[2], qv1)
    ges = exchange([ge[j * pv : (j + 1) * pv] for j in range(CYCLE)])
    out = call(
        "reg_grad",
        functools.partial(reg_grad_kernel, (first_x, split_z), natural),
        [(scal, "s")]
        + many(pairs1)
        + many([upb, hm, h_vis, gm, ge, o1])
        + many(dr1s + xs + [w_own])
        + many([up, down], "a"),
        (ffn_whole + attn_whole if natural else message(piece + piece // 2) * 2)
        + [((8, width), F32), ((8, ffb), F32)],
        ffn_scratch(nm) + [pltpu.VMEM((nm, width), BF)],
        after=[qv1],
        cost=9,
    )
    norm1, sum1 = out[-2:]
    if natural:
        sums1 = [by_owner(out[0]), by_rows(out[1]), by_rows(out[2]), by_owner(out[3])]
    else:
        sums1 = [ImgSum(out[0], out[1], first_x), ImgSum(out[2], out[3], split_z)]

    def steps(sums, *after):
        if natural:
            for one in sums:
                one.step()
        else:
            step_all(scal, sums, after)

    for one in sums1:
        one.sent = later(one.sent, *ges[1:])
    steps(sums1)
    pair0, dr0, dy0, small0 = call(
        "enc_ffn_back",
        functools.partial(enc_ffn_back_kernel, vis),
        [(scal, "s")]
        + many(ges)
        + many([e, cot_e, y0, r0, z0, gp0, h2_0, vec])
        + many([attn, up, down], "a"),
        [((2 * pv, width), BF), ((pv, width), BF), ((pv, width), F32), ((8, width), F32)],
        [pltpu.VMEM((pv, width), BF)] * 2 + [square] * 2 + [weights_scratch[0]] * 2
        + [dma((2,)), weights_scratch[2]],
        after=[sum1],
        cost=0.001,
    )

    dr0s = gather(dr0)
    steps(sums1)
    out = call(
        "enc_attend_back",
        functools.partial(enc_attend_back_kernel, vis, last_z, natural),
        [(scal, "s")]
        + many(dr0s)
        + many([h0, q0, k0, v0, o0, gm] + xs + [w_own])
        + [(attn, "a")],
        [((CYCLE, pv + pm, 3 * s), BF), ((8, s), F32), ((8, width), F32)]
        + (attn_whole if natural else message(piece)),
        [pltpu.VMEM((nv, width), BF), pltpu.VMEM((s, width), BF), dma((1,))],
        after=[small0, sums1[0].sent],
        cost=8,
    )
    g, qv0, norm0 = out[:3]
    pairs0 = gather(pair0, dr0s[2], qv0)
    if natural:
        attn0, o0_sum = by_rows(out[3]), by_owner(out[4])
    else:
        attn0 = ImgSum(out[3], out[4], last_z)
    steps([attn0])
    out = call(
        "enc_ffn_grad",
        functools.partial(enc_ffn_grad_kernel, (first_z, first_x), natural),
        [(scal, "s")]
        + many(pairs0)
        + many([upb, small0, small1, norm0, norm1, qv0, qv1, sum1])
        + many([up, down], "a"),
        (ffn_whole if natural else message(piece) + message(piece + 16)) + [((32, width), F32)],
        [pltpu.VMEM((8, ffb), F32)] + ffn_scratch(nv),
        cost=0.001,
    )
    rows = out[-1]
    if natural:
        ffn0 = [by_owner(out[0]), by_rows(out[1])]
    else:
        ffn0 = [ImgSum(out[0], out[1], first_z), ImgSum(out[2], out[3], first_x)]
    for one in ffn0:
        one.sent = later(one.sent, *[prior.got for prior in sums1])
    ffn0[1].sent = later(ffn0[1].sent, attn0.got)
    steps(ffn0)
    steps(sums1, rows)
    steps(ffn0 + [attn0], sums1[0].sent)
    g = lax.all_to_all(later(g, ffn0[0].sent), "blk", 0, 0, tiled=True)
    steps(ffn0 + [attn0], ffn0[0].sent)
    grad_x, grad_m = call(
        "input_grad",
        input_grad_kernel,
        many([g, x, dy0, dy1, vec]) + [(attn, "a")],
        [((vis, 1, width), F32), ((hid, 1, width), F32)],
        [pltpu.VMEM((pv + pm, width), BF)] * 3
        + [pltpu.VMEM((2, 3, width, width), BF), dma((2, 3))],
        after=[ffn0[0].sent],
        cost=6,
    )

    if natural:

        def owned(sums):
            return transpose_owners(sums.finish().astype(BF)).astype(F32)

        ups, downs, attns = [], [], []
        for down_sum, up_sum, qkv, o_sum in (ffn0 + [attn0, o0_sum], sums1):
            ups.append(up_sum.finish())
            downs.append(owned(down_sum))
            got = qkv.finish()
            attns.append(
                jnp.stack([got[:, :s], got[:, s : 2 * s], got[:, 2 * s :], owned(o_sum)])
            )
        grad_attn, grad_up, grad_down = jnp.stack(attns), jnp.stack(ups), jnp.stack(downs)
        for axis in ("blk", "img"):
            j = 1
            while j < lax.axis_size(axis):
                rows = rows + swap(rows, axis, j)
                j *= 2
        vec_total = lax.dynamic_slice_in_dim(rows[:20], place * piece, piece, 1)
        vec_total = vec_total.reshape(2, 10, piece)
        bias_total = lax.dynamic_slice_in_dim(
            rows[20:28].reshape(2, ff), place * (ff // images), ff // images, 1
        )
    else:
        for one in sums1:
            one.got = later(one.got, grad_x)

        def fix(down_total, o_total):
            both = jnp.concatenate([down_total[0, :piece], o_total], 1)
            return transpose_owners(both.astype(BF))

        totals = [sums.total() for sums in sums1]
        fixed1 = fix(
            totals[0], jnp.concatenate([total[0, piece:, 3 * s :] for total in totals], 0)
        )
        fixed0 = fix(ffn0[0].total(), attn0.total()[0, :, 3 * s :])
        both = ffn0[1].total()[0, piece:, : 2 * piece]
        rows = jnp.concatenate([both[:, :piece], both[:, piece:]], 0)
        rows = rows + swap(rows, "blk", 1)
        rows = rows + swap(rows, "blk", 2)
        last = [ffn0[1].keep, ffn0[1].got, attn0.keep, attn0.got, fixed0]
        last += [sums1[1].keep, sums1[1].got, sums1[0].keep, sums1[0].got, fixed1]
        grad_attn, grad_up, grad_down, vec_total, bias_total = call(
            "finish",
            finish_kernel,
            [(scal, "s")] + many(last + [rows]),
            [
                ((2, 4, piece, s), F32),
                ((2, piece, ffb), F32),
                ((2, s, ff // images), F32),
                ((10, 2, piece), F32),
                ((2, ff // images), F32),
            ],
        )
        grad_down, vec_total = jnp.swapaxes(grad_down, 1, 2), jnp.swapaxes(vec_total, 0, 1)

    return (
        e_b[:, None, :],
        g_b[:, None, :],
        grad_x,
        grad_m,
        grad_attn,
        grad_up,
        grad_down,
        vec_total,
        bias_total,
    )


def solution(mesh):
    rows = P("blk", "img", None)
    in_specs = (rows, rows, P("img"), P(), P(), P(), P(), P(), rows, rows)
    out_specs = (
        rows,
        rows,
        rows,
        rows,
        P(None, None, "img", "blk"),
        P(None, "img", "blk"),
        P(None, "img", "blk"),
        P(None, None, "img"),
        P(None, "img"),
    )
    return jax.shard_map(body, mesh=mesh, in_specs=in_specs, out_specs=out_specs, check_vma=False)
```

```python
import functools

import jax
import jax.numpy as jnp
from jax import lax
from jax.experimental import pallas as pl
from jax.experimental.pallas import tpu as pltpu
from jax.sharding import PartitionSpec as P

HEADS = 12
HEAD = 64
NPATCH = 576
EPS = 1e-06
BF = jnp.bfloat16
F32 = jnp.float32
CYCLE = 4
MIB = 1024 * 1024
COSTS = {'prep': 7.0, 'load': 3.0, 'enc_attend': 3.3, 'mask_project': 0.9, 'enc_ffn': 5.9, 'reg_attend': 3.4, 'reg_ffn': 8.2, 'reg_attend_back': 5.7, 'reg_grad': 8.7, 'enc_ffn_back': 10.4, 'enc_attend_back': 8.0, 'enc_ffn_grad': 5.9, 'img_step': 0.8, 'input_grad': 7.4, 'finish': 2.6}
COST_SCALE = 0.3


def round_up(value, unit):
    return (value + unit - 1) // unit * unit


def dot(left, right):
    return jnp.dot(left, right, preferred_element_type=F32)


def dot_nt(left, right):
    return lax.dot_general(left, right, (((1,), (1,)), ((), ())), preferred_element_type=F32)


def dot_tn(left, right):
    return lax.dot_general(left, right, (((0,), (0,)), ((), ())), preferred_element_type=F32)


def norm(rows):
    centred = rows - jnp.mean(rows, -1, keepdims=True)
    inverse = lax.rsqrt(jnp.mean(centred * centred, -1, keepdims=True) + EPS)
    return centred * inverse, inverse


def norm_back(grad_out, gain, normed, inverse):
    scaled = grad_out * gain
    return inverse * (
        scaled
        - jnp.mean(scaled, -1, keepdims=True)
        - normed * jnp.mean(scaled * normed, -1, keepdims=True)
    )


def gelu_parts(u):
    cdf = 0.5 * (1.0 + lax.erf(u * 0.7071067811865476))
    slope = cdf + u * (jnp.exp(u * u * -0.5) * 0.3989422804014327)
    return cdf, slope


def col_sum(rows):
    return jnp.sum(rows, 0, keepdims=True)


def swap(block, axis, offset):
    size = lax.axis_size(axis)
    return lax.ppermute(block, axis, [(i, i ^ offset) for i in range(size)])


def gather(block, first=None, second=None):
    across = swap(block if first is None else later(block, first), "blk", 2)
    if second is not None:
        over, beside = swap(later(across, second), "blk", 1), later(block, second)
    else:
        over, beside = swap(across, "blk", 1), block
    return [block, swap(beside, "blk", 1), across, over]


def later(value, *arrays):
    return lax.optimization_barrier((value, *arrays))[0]


def exchange(blocks, held=None):
    sent = blocks if held is None else held
    across, over = swap(sent[2], "blk", 2), swap(sent[3], "blk", 3)
    return [blocks[0], swap(sent[1], "blk", 1), across, over]


class ImgSum:
    def __init__(self, keep, sent, order):
        self.order = list(order)
        self.keep, self.sent, self.got = keep, sent, None
        self.at = slice(0, keep.shape[1])

    def step(self, *after):
        bit = self.order.pop(0)
        if self.got is not None:
            total = self.total().astype(BF)
            total = total.reshape((2, total.shape[0] // 2) + total.shape[1:])
            mine = (lax.axis_index("img") >> bit) & 1
            self.keep = lax.dynamic_index_in_dim(total, mine, 0, False)
            self.sent = lax.dynamic_index_in_dim(total, 1 - mine, 0, False)
        if after:
            self.sent = later(self.sent, *after)
        self.got = swap(self.sent, "img", 1 << bit)
        return self.sent

    def total(self):
        return self.keep.astype(F32) + self.got[:, self.at].astype(F32)

    def finish(self):
        while self.order:
            self.step()
        return self.total()[0]


def reduce_whole(parts):
    images = parts.shape[0]
    place = lax.axis_index("img")
    bits = images.bit_length() - 1
    pairs = parts.reshape((2, images // 2) + parts.shape[1:])
    mine = place >> (bits - 1)
    keep = lax.dynamic_index_in_dim(pairs, mine, 0, False)
    sent = lax.dynamic_index_in_dim(pairs, 1 - mine, 0, False)
    return ImgSum(keep, sent, range(bits - 1, -1, -1))


def transpose_owners(part):
    images, cycle = lax.axis_size("img"), lax.axis_size("blk")
    m = images // cycle
    pairs = []
    for i in range(images):
        for b in range(cycle):
            pairs.append((i * cycle + b, (b * m + i % m) * cycle + i // m))
    return lax.ppermute(part, ("img", "blk"), pairs)


def call(name, kernel, ins, outs, scratch=(), limit=8, after=(), keep=False, hold=()):
    spaces = {"s": pltpu.SMEM, "v": pltpu.VMEM, "w": pltpu.VMEM, "a": pltpu.HBM, "n": pl.ANY}
    places = {"w": pltpu.VMEM, "a": pltpu.HBM}
    count = len(ins)
    ins = ins + [(a, "n") for a in after] + [(a, "w") for a in hold]

    def run(*refs):
        kernel(*refs[:count], *refs[len(ins) :])

    return pl.pallas_call(
        run,
        name=name,
        out_shape=[
            pltpu.VMEM(s, d) if keep else jax.ShapeDtypeStruct(s, d) for s, d in outs
        ],
        in_specs=[pl.BlockSpec(memory_space=spaces[k]) for _, k in ins],
        out_specs=[pl.BlockSpec(memory_space=pltpu.VMEM) for _ in outs],
        scratch_shapes=list(scratch),
        compiler_params=pltpu.CompilerParams(vmem_limit_bytes=limit * MIB),
        cost_estimate=pl.CostEstimate(
            flops=int(COST_SCALE * COSTS[name] * 1.15e9), bytes_accessed=1, transcendentals=0
        ),
    )(*[pltpu.with_memory_space_constraint(a, places[k]) if k in places else a for a, k in ins])


def step_kernel(bits, starts, groups, scal, *refs):
    count = len(bits)
    ins, keeps, outs = refs[: 2 * count], refs[2 * count : 3 * count], refs[3 * count :]
    for out, group in zip(outs, groups):
        start = 0
        for k in group:
            keep, got = ins[2 * k : 2 * k + 2]
            half, rows = keep.shape[0] // 2, keep.shape[1]
            mine = (scal[2] >> bits[k]) & 1
            sides = []
            for side in (mine, 1 - mine):
                at = pl.ds(side * half, half)
                other = got[at, starts[k] : starts[k] + rows]
                sides.append((keep[at].astype(F32) + other.astype(F32)).astype(BF))
            keeps[k][...] = sides[0]
            out[:, start : start + rows] = sides[1]
            start += rows


def step_all(scal, groups, after=(), hold=()):
    sums = [one for group in groups for one in group]
    if sums[0].got is not None:
        bits = [one.order[0] for one in sums]
        places, ins, keeps, outs = [], [(scal, "s")], [], []
        for group in groups:
            places.append([sums.index(one) for one in group])
            half, rows = group[0].keep.shape[0] // 2, 0
            for one in group:
                ins += [(one.keep, "v"), (one.got, "v")]
                keeps.append(((half,) + one.keep.shape[1:], BF))
                rows += one.keep.shape[1]
            outs.append(((half, rows, one.keep.shape[2]), BF))
        parts = call(
            "img_step",
            functools.partial(step_kernel, bits, [one.at.start for one in sums], places),
            ins,
            keeps + outs,
            after=after,
            hold=hold,
        )
        for k, one in enumerate(sums):
            one.keep = parts[k]
        sent = parts[len(sums) :]
    else:
        sent = [group[0].sent for group in groups]
    for group, message in zip(groups, sent):
        got, start = swap(message, "img", 1 << group[0].order[0]), 0
        for one in group:
            rows = one.keep.shape[1]
            one.order.pop(0)
            one.sent, one.got = message, got
            one.at, start = slice(start, start + rows), start + rows


def load_kernel(blk, up, down, up_out, down_out, sems):
    copies = [
        pltpu.make_async_copy(up.at[blk], up_out, sems.at[0]),
        pltpu.make_async_copy(down.at[blk], down_out, sems.at[1]),
    ]
    for copy in copies:
        copy.start()
    for copy in copies:
        copy.wait()


def prep_kernel(scal, attn, up, down, vec, attn_out, up_out, down_out, w_out, b_out, sems):
    me = scal[0]
    share = w_out.shape[3]
    window = share + share % 128
    odd = me & 1
    start = pl.multiple_of(me * share - odd * (share % 128), 128)
    pairs = [(attn.at[0], attn_out.at[0]), (attn.at[1], attn_out.at[1])]
    pairs += [(up.at[0], up_out), (down.at[0], down_out)]
    copies = [
        pltpu.make_async_copy(source, target, sems.at[k])
        for k, (source, target) in enumerate(pairs)
    ]
    for copy in copies:
        copy.start()
    for blk in range(2):
        copies[blk].wait()
        for m in range(3):
            for parity in range(2):
                shift = parity * (share % 128)

                @pl.when(odd == parity)
                def _():
                    part = attn_out[blk, m, :, pl.ds(start, window)]
                    w_out[blk, m] = part[:, shift : shift + share]
                    if m == 1:
                        b_out[blk, m] = jnp.zeros((1, share), F32)
                    else:
                        row = vec[2 + m // 2, blk : blk + 1, pl.ds(start, window)]
                        b_out[blk, m] = row[:, shift : shift + share]
    for copy in copies[2:]:
        copy.wait()


def key_bias(me, rows, padded, limit):
    at = lax.broadcasted_iota(jnp.int32, (padded, 1), 0)
    parts = []
    for j in range(CYCLE):
        live = (at < rows) & (at + (me ^ j) * rows < limit)
        parts.append(jnp.where(live, 0.0, -1e30))
    return jnp.concatenate(parts, 0)


def own_live(me, rows, padded, limit):
    at = lax.broadcasted_iota(jnp.int32, (padded, 1), 0)
    return jnp.where((at < rows) & (at + me * rows < limit), 1.0, 0.0)


def probs_t(keys, queries, bias):
    scores = dot_nt(keys, queries) + bias
    exps = jnp.exp(scores - jnp.max(scores, 0, keepdims=True))
    return exps * (1.0 / jnp.sum(exps, 0, keepdims=True))


def attend_t(q, k, v, bias, out_ref):
    qs = (q.astype(F32) * HEAD**-0.5).astype(BF)
    vt = v.astype(F32).T.astype(BF)
    mixed = []
    for h in range(q.shape[1] // HEAD):
        c = slice(h * HEAD, (h + 1) * HEAD)
        p = probs_t(k[:, c], qs[:, c], bias).astype(BF)
        mixed.append(dot(vt[c], p))
    out_ref[...] = jnp.concatenate(mixed, 0).T.astype(BF)


def attend_back_t(q, k, v, do, bias):
    qs = (q.astype(F32) * HEAD**-0.5).astype(BF)
    kt = (k.astype(F32) * HEAD**-0.5).T.astype(BF)
    dq, dk, dv = [], [], []
    for h in range(q.shape[1] // HEAD):
        c = slice(h * HEAD, (h + 1) * HEAD)
        p = probs_t(k[:, c], qs[:, c], bias)
        dp = dot_nt(v[:, c], do[:, c])
        ds = (p * (dp - jnp.sum(p * dp, 0, keepdims=True))).astype(BF)
        dv.append(dot(p.astype(BF), do[:, c]))
        dk.append(dot(ds, qs[:, c]))
        dq.append(dot(kt[c], ds))
    return (
        jnp.concatenate(dq, 0).T.astype(BF),
        jnp.concatenate(dk, 1).astype(BF),
        jnp.concatenate(dv, 1).astype(BF),
    )


def enc_attend_kernel(vis, scal, x0, x1, x2, x3, w, b, vec, h_out, q_out, k_out, v_out, o_out):
    me, count = scal[0], scal[1]
    padded = h_out.shape[0] // CYCLE
    for j, ref in enumerate((x0, x1, x2, x3)):
        n, _ = norm(ref[0:padded].astype(F32))
        h_out[j * padded : (j + 1) * padded] = (n * vec[0, 0:1] + vec[1, 0:1]).astype(BF)
    h = h_out[...]
    q = (dot(h, w[0, 0]) + b[0, 0]).astype(BF)
    k = dot(h, w[0, 1]).astype(BF)
    v = (dot(h, w[0, 2]) + b[0, 2]).astype(BF)
    q_out[...], k_out[...], v_out[...] = q, k, v
    attend_t(q, k, v, key_bias(me, vis, padded, count), o_out)


def mask_project_kernel(x0, x1, x2, x3, w, b, vec, h_out, q_out, k_out, v_out):
    padded = h_out.shape[0] // CYCLE
    for j, ref in enumerate((x0, x1, x2, x3)):
        n, _ = norm(ref[x0.shape[0] - padded :].astype(F32))
        h_out[j * padded : (j + 1) * padded] = (n * vec[0, 1:2] + vec[1, 1:2]).astype(BF)
    h = h_out[...]
    q_out[...] = (dot(h, w[1, 0]) + b[1, 0]).astype(BF)
    k_out[...] = dot(h, w[1, 1]).astype(BF)
    v_out[...] = (dot(h, w[1, 2]) + b[1, 2]).astype(BF)


def reg_attend_kernel(
    vis, hid, scal, x0, x1, x2, x3, w, b, qm, km, vm, h_out, k_out, v_out, o_out
):
    me, count = scal[0], scal[1]
    padded = x0.shape[0]
    nv = CYCLE * padded
    for j, ref in enumerate((x0, x1, x2, x3)):
        h_out[j * padded : (j + 1) * padded] = ref[...]
    h = h_out[...]
    k_out[0:nv] = dot(h, w[1, 1]).astype(BF)
    v_out[0:nv] = (dot(h, w[1, 2]) + b[1, 2]).astype(BF)
    k_out[nv:] = km[...]
    v_out[nv:] = vm[...]
    bias = jnp.concatenate(
        [
            key_bias(me, vis, padded, count),
            key_bias(me, hid, qm.shape[0] // CYCLE, NPATCH - count),
        ],
        0,
    )
    attend_t(qm[...], k_out[...], v_out[...], bias, o_out)


def assemble(me, blocks, scratch, lane):
    share = blocks[0].shape[1] if lane is None else lane[1]
    rows = scratch.shape[0]
    for m in range(CYCLE):

        @pl.when(me == m)
        def _():
            for j, ref in enumerate(blocks):
                at = (m ^ j) * share
                value = ref[...] if lane is None else ref[0:rows, lane[0] : lane[0] + share]
                scratch[:, at : at + share] = value


def ffn_forward(blk, rows, mixed, vec, upb, attn, up, down, gp):
    r = dot(mixed, attn[blk, 3]) + vec[4, blk : blk + 1]
    y = rows + vec[5, blk : blk + 1] * r
    n, _ = norm(y)
    h2 = (n * vec[6, blk : blk + 1] + vec[7, blk : blk + 1]).astype(BF)
    width = up.shape[0]
    z = vec[8, blk : blk + 1]
    for c in range(up.shape[1] // width):
        cols = slice(c * width, (c + 1) * width)
        u = dot(h2, up[:, cols]) + upb[blk : blk + 1, cols]
        cdf, slope = gelu_parts(u)
        gp[:, cols] = slope
        a = (u * cdf).astype(BF)
        z = z + dot(a, down[cols, :])
    return r, y, h2, z


def ffn_backward(blk, grad, r, y, z, vec, up, down, gp, up_sum):
    n, inverse = norm(y)
    scale2 = col_sum(grad * z)
    dz = (grad * vec[9, blk : blk + 1]).astype(BF)
    width = up.shape[0]
    dh2 = 0.0
    for c in range(up.shape[1] // width):
        cols = slice(c * width, (c + 1) * width)
        da = dot_nt(dz, down[cols, :])
        du = (gp[:, cols] * da).astype(BF)
        up_sum[:, cols] = col_sum(du.astype(F32))
        dh2 = dh2 + dot_nt(du, up[:, cols])
    dy = grad + norm_back(dh2, vec[6, blk : blk + 1], n, inverse)
    dr = (dy * vec[5, blk : blk + 1]).astype(BF)
    small = [
        scale2,
        col_sum(dh2 * n),
        col_sum(dh2),
        col_sum(dy * r),
        col_sum(dz.astype(F32)),
        col_sum(dr.astype(F32)),
    ]
    return dz, dy, dr, small


def enc_ffn_kernel(
    vis, scal, o0, o1, o2, o3, x, vec, upb, attn, up, down,
    e_out, eb_out, he_out, h2_out, y_out, r_out, z_out, gp_out,
    mixed,
):
    me, count = scal[0], scal[1]
    assemble(me, (o0, o1, o2, o3), mixed, None)
    r, y, h2, z = ffn_forward(
        0, x[0 : he_out.shape[0]].astype(F32), mixed[...], vec, upb, attn, up, down, gp_out
    )
    h2_out[...], y_out[...], r_out[...], z_out[...] = h2, y, r, z
    e = (y + vec[9, 0:1] * z) * own_live(me, vis, he_out.shape[0], count)
    e_out[...] = e
    eb_out[...] = e[0 : eb_out.shape[0]].astype(BF)
    n, _ = norm(e)
    he_out[...] = (n * vec[0, 1:2] + vec[1, 1:2]).astype(BF)


def reg_ffn_kernel(
    hid, scal, o0, o1, o2, o3, x, cot, vec, upb, attn, up, down,
    gb_out, pair_out, dr_out, dy_out, small_out, up_sum,
    mixed, gp,
):
    me, count = scal[0], scal[1]
    assemble(me, (o0, o1, o2, o3), mixed, None)
    r, y, h2, z = ffn_forward(
        1, x[x.shape[0] - dr_out.shape[0] :].astype(F32), mixed[...], vec, upb, attn, up, down, gp
    )
    padded = dr_out.shape[0]
    live = own_live(me, hid, padded, NPATCH - count)
    g = (y + vec[9, 1:2] * z) * live
    gb_out[...] = g[0 : gb_out.shape[0]].astype(BF)
    grad = cot[...].astype(F32) * live
    dz, dy, dr, small = ffn_backward(1, grad, r, y, z, vec, up, down, gp, up_sum)
    pair_out[0:padded] = h2
    pair_out[padded:] = dz
    dr_out[...] = dr
    dy_out[...] = dy
    for i, row in enumerate(small):
        small_out[i : i + 1] = row
    small_out[6:8] = jnp.zeros((2, small_out.shape[1]), F32)


def enc_ffn_back_kernel(
    vis, scal, g0, g1, g2, g3, e, cot, y, r, z, gp, h2, vec, attn, up, down,
    pair_out, dr_out, dy_out, small_out, up_sum,
    dk, dv,
):
    me, count = scal[0], scal[1]
    share = g0.shape[1] // 2
    assemble(me, (g0, g1, g2, g3), dk, (0, share))
    assemble(me, (g0, g1, g2, g3), dv, (share, share))
    n, inverse = norm(e[...])
    dh = dot_nt(dk[...], attn[1, 1]) + dot_nt(dv[...], attn[1, 2])
    grad_e = norm_back(dh, vec[0, 1:2], n, inverse)
    grad = (cot[...].astype(F32) + grad_e) * own_live(me, vis, cot.shape[0], count)
    dz, dy, dr, small = ffn_backward(
        0, grad, r[...], y[...], z[...], vec, up, down, gp, up_sum
    )
    pair_out[0 : dz.shape[0]] = h2[...]
    pair_out[dz.shape[0] :] = dz
    dy_out[...], dr_out[...] = dy, dr
    for i, row in enumerate(small + [col_sum(dh * n), col_sum(dh)]):
        small_out[i : i + 1] = row


def spread(place_of, keep, sent, place, order, rows, cols):
    first, second, third = order
    for i in range(8):
        t = 2 * ((i >> second) & 1) + ((i >> third) & 1)
        value = place_of(i)

        for side in range(2):
            target = keep if side == ((i >> first) & 1) else sent

            @pl.when(((place >> first) & 1) == side)
            def _():
                target[t, rows, cols] = value


def owner_piece(mat, i, share, parts):
    quarter, half = i >> 1, i & 1
    rows = mat.shape[0] // 2
    part = mat[half * rows : (half + 1) * rows, quarter * share : (quarter + 1) * share]
    rows = rows // parts
    return jnp.concatenate([part[k * rows : (k + 1) * rows] for k in range(parts)], 1)


def attn_pieces(h, dqkv, o, dr):
    share = dqkv[0].shape[1]
    results = [dot_tn(h, grad).astype(BF) for grad in dqkv]
    d_o = dot_tn(o, dr).astype(BF)
    step = h.shape[1] // 8

    def piece(i):
        parts = [result[i * step : (i + 1) * step] for result in results]
        return jnp.concatenate(parts + [owner_piece(d_o, i, share, 1)], 1)

    return results, d_o, piece


def norm_sums(rows, dqkv, w):
    dh = 0.0
    for m, grad in enumerate(dqkv):
        dh = dh + dot_nt(grad, w[m])
    n, _ = norm(rows.astype(F32))
    return col_sum(dh * n), col_sum(dh)


def store_attn(results, d_o, nats):
    share = d_o.shape[0]
    for m, result in enumerate(results):
        nats[0][:, m * share : (m + 1) * share] = result
    nats[1][...] = d_o


def reg_attend_back_kernel(
    vis, hid, scal, d0, d1, d2, d3, q, k, v, attn,
    e_out, m_out, qv_out,
    dr,
):
    me, count = scal[0], scal[1]
    share = q.shape[1]
    padded = d0.shape[0]
    for j, ref in enumerate((d0, d1, d2, d3)):
        dr[j * padded : (j + 1) * padded] = ref[...]
    do = dot_nt(dr[...], attn[1, 3, pl.ds(pl.multiple_of(me * share, 16), share), :]).astype(BF)
    nm = CYCLE * padded
    nv = k.shape[0] - nm
    bias = jnp.concatenate(
        [
            key_bias(me, vis, nv // CYCLE, count),
            key_bias(me, hid, padded, NPATCH - count),
        ],
        0,
    )
    dq, dk, dv = attend_back_t(q[...], k[...], v[...], do, bias)
    e_out[:, 0:share] = dk[0:nv]
    e_out[:, share:] = dv[0:nv]
    m_out[:, 0:share] = dq
    m_out[:, share : 2 * share] = dk[nv:]
    m_out[:, 2 * share :] = dv[nv:]
    qv_out[0:1] = col_sum(dq.astype(F32))
    qv_out[1:2] = col_sum(dv.astype(F32))
    qv_out[2:8] = jnp.zeros((6, share), F32)


def enc_attend_back_kernel(
    vis, order, natural, scal, d0, d1, d2, d3, h, q, k, v, o, gm, x0, x1, x2, x3, w,
    small0, small1, norm1, qv1, ups0, ups1, attn,
    g_out, vec_out, first, second, dr, qv0, norm0,
):
    me, count = scal[0], scal[1]
    share = q.shape[1]
    padded = d0.shape[0]
    for j, ref in enumerate((d0, d1, d2, d3)):
        dr[j * padded : (j + 1) * padded] = ref[...]
    do = dot_nt(dr[...], attn[0, 3, pl.ds(pl.multiple_of(me * share, 16), share), :]).astype(BF)
    dq, dk, dv = attend_back_t(
        q[...], k[...], v[...], do, key_bias(me, vis, padded, count)
    )
    for j in range(CYCLE):
        at = slice(j * padded, (j + 1) * padded)
        for m, grad in enumerate((dq, dk, dv)):
            g_out[j, 0:padded, m * share : (m + 1) * share] = grad[at]
        more = g_out.shape[1] - padded
        g_out[j, padded:] = gm[j * more : (j + 1) * more]
    qv0[0:1] = col_sum(dq.astype(F32))
    qv0[1:2] = col_sum(dv.astype(F32))
    x = jnp.concatenate([ref[0:padded] for ref in (x0, x1, x2, x3)], 0)
    norm0[0:1], norm0[1:2] = norm_sums(x, (dq, dk, dv), (w[0, 0], w[0, 1], w[0, 2]))
    vector_rows(
        natural, me, (small0, small1), (norm0, norm1), (qv0, qv1), (ups0, ups1), vec_out
    )
    results, d_o, piece = attn_pieces(h[...], (dq, dk, dv), o[...], dr[...])
    if natural:
        store_attn(results, d_o, (first, second))
        return
    step, cols = h.shape[1] // 8, slice(0, 4 * share)

    def vector_piece(i):
        mine = slice(i * step, (i + 1) * step)
        parts = [vec_out[0:16, mine], vec_out[16:32, mine]]
        parts.append(jnp.zeros((16, 4 * share - 2 * step), F32))
        return jnp.concatenate(parts, 1).astype(BF)

    spread(piece, first, second, scal[2], order, slice(0, step), cols)
    spread(vector_piece, first, second, scal[2], order, slice(step, step + 16), cols)


def ffn_pieces(blk, scal, pairs, upb, up, down, h2, dz):
    me = scal[0]
    width = up.shape[0]
    cols = pl.ds(pl.multiple_of(me * width, 128), width)
    padded = pairs[0].shape[0] // 2
    for j, pair in enumerate(pairs):
        at = slice(j * padded, (j + 1) * padded)
        h2[at] = pair[0:padded]
        dz[at] = pair[padded:]
    u = dot(h2[...], up[:, cols]) + upb[blk : blk + 1, cols]
    cdf, slope = gelu_parts(u)
    a = (u * cdf).astype(BF)
    d_down = dot_tn(a, dz[...]).astype(BF)
    du = (slope * dot_nt(dz[...], down[cols, :])).astype(BF)
    d_up = dot_tn(h2[...], du).astype(BF)
    step = width // 8
    return (
        d_down,
        d_up,
        lambda i: owner_piece(d_down, i, width // 4, 4),
        lambda i: d_up[i * step : (i + 1) * step],
    )


def vector_rows(natural, me, smalls, norms, qvs, ups, out):
    share, width = qvs[0].shape[1], out.shape[1]
    step = width // 8
    out[...] = jnp.zeros(out.shape, F32)
    for blk, (small, qv, up_sum) in enumerate(zip(smalls, qvs, ups)):
        at = 10 * blk
        gain, bias = norms[blk][0:1], norms[blk][1:2]
        if blk == 1:
            gain, bias = gain + smalls[0][6:7], bias + smalls[0][7:8]
        scale2, gain2, bias2, scale1, dzs, drs = [small[i : i + 1] for i in range(6)]
        rows = {0: gain, 1: bias, 4: drs, 5: scale1, 6: gain2, 7: bias2, 8: dzs, 9: scale2}
        for i, row in rows.items():
            out[at + i : at + i + 1] = row
        first = 20 + 4 * blk
        for k in range(4):
            if natural:
                out[first + k : first + k + 1] = up_sum[0:1, k * width : (k + 1) * width]
            else:
                parts = [
                    up_sum[0:1, (4 * i + k) * step : (4 * i + k + 1) * step] for i in range(8)
                ]
                out[first + k : first + k + 1] = jnp.concatenate(parts, 1)
        for m in range(CYCLE):

            @pl.when(me == m)
            def _():
                cols = slice(m * share, (m + 1) * share)
                out[at + 2 : at + 3, cols] = qv[0:1]
                out[at + 3 : at + 4, cols] = qv[1:2]


def enc_ffn_grad_kernel(orders, natural, scal, p0, p1, p2, p3, upb, up, down, *refs):
    outs, scratch = refs[:-2], refs[-2:]
    d_down, d_up, down_piece, up_piece = ffn_pieces(
        0, scal, (p0, p1, p2, p3), upb, up, down, *scratch
    )
    if natural:
        outs[0][...], outs[1][...] = d_down, d_up
        return
    here, cols = slice(0, d_up.shape[0] // 8), slice(0, d_up.shape[1])
    spread(down_piece, outs[0], outs[1], scal[2], orders[0], here, cols)
    spread(up_piece, outs[2], outs[3], scal[2], orders[1], here, cols)


def reg_grad_kernel(
    orders, natural, scal, p0, p1, p2, p3, upb, h_m, h_e, g_m, g_e, o, d0, d1, d2, d3,
    x0, x1, x2, x3, w, up, down, *refs,
):
    outs, norm_out, scratch, dr = refs[:-4], refs[-4], refs[-3:-1], refs[-1]
    d_down, d_up, down_piece, up_piece = ffn_pieces(
        1, scal, (p0, p1, p2, p3), upb, up, down, *scratch
    )
    share = g_e.shape[1] // 2
    padded = d0.shape[0]
    for j, ref in enumerate((d0, d1, d2, d3)):
        dr[j * padded : (j + 1) * padded] = ref[...]
    x = jnp.concatenate([ref[ref.shape[0] - padded :] for ref in (x0, x1, x2, x3)], 0)
    dqkv_m = [g_m[:, m * share : (m + 1) * share] for m in range(3)]
    norm_out[0:1], norm_out[1:2] = norm_sums(x, dqkv_m, (w[1, 0], w[1, 1], w[1, 2]))
    norm_out[2:8] = jnp.zeros((6, norm_out.shape[1]), F32)
    h = jnp.concatenate([h_e[...], h_m[...]], 0)
    none = jnp.zeros((h_e.shape[0], share), BF)
    grads = []
    for m in range(3):
        top = none if m == 0 else g_e[:, (m - 1) * share : m * share]
        grads.append(jnp.concatenate([top, dqkv_m[m]], 0))
    results, d_o, attn_piece = attn_pieces(h, grads, o[...], dr[...])
    if natural:
        outs[0][...], outs[1][...] = d_down, d_up
        store_attn(results, d_o, outs[2:4])
        return
    step, cols = d_up.shape[0] // 8, slice(0, d_up.shape[1])
    half = step // 2
    for k, piece in enumerate((down_piece, up_piece)):
        keep, sent = outs[2 * k : 2 * k + 2]
        place, order = scal[2], orders[k]
        spread(piece, keep, sent, place, order, slice(0, step), cols)
        spread(
            lambda i: attn_piece(i)[k * half : (k + 1) * half], keep, sent, place, order,
            slice(step, step + half), cols,
        )


def input_grad_kernel(
    scal, g0, g1, g2, g3, x, dy0, dy1, vec, attn, out0, out1, dq, dk, dv
):
    share = g0.shape[1] // 3
    grads = (dq, dk, dv)
    for m, ref in enumerate(grads):
        assemble(scal[0], (g0, g1, g2, g3), ref, (m * share, share))
    first = dy0.shape[0]
    rows = (slice(0, first), slice(first, x.shape[0]))
    for blk, (at, dy, out) in enumerate(((rows[0], dy0, out0), (rows[1], dy1, out1))):
        n, inverse = norm(x[at].astype(F32))
        dh = 0.0
        for m, ref in enumerate(grads):
            dh = dh + dot_nt(ref[at], attn[blk, m])
        dx = norm_back(dh, vec[0, blk : blk + 1], n, inverse) + dy[...]
        out[:, 0, :] = dx[0 : out.shape[0]]


def finish_kernel(scal, *refs):
    (up0, attn0, got0, fixed0) = refs[:4]
    (up1, down1, got1, fixed1) = refs[4:8]
    rows, attn_out, up_out, down_out, vec_out, bias_out = refs[8:]
    piece, share = attn_out.shape[2], attn_out.shape[3]
    half = piece // 2
    moves = (
        (0, slice(0, piece), attn0, slice(0, piece), got0, slice(2 * piece, 3 * piece)),
        (1, slice(0, half), down1, slice(piece, piece + half), got1, slice(piece, piece + half)),
        (1, slice(half, piece), up1, slice(piece, piece + half),
         got1, slice(2 * piece + half, 2 * piece + 2 * half)),
    )
    for blk, to, keep, keep_at, got, got_at in moves:
        for m in range(3):
            cols = slice(m * share, (m + 1) * share)
            attn_out[blk, m, to] = keep[0, keep_at, cols].astype(F32) + got[
                0, got_at, cols
            ].astype(F32)
    starts = (piece, piece + half)
    for blk, keep, got, fixed in ((0, up0, got0, fixed0), (1, up1, got1, fixed1)):
        up_out[blk] = keep[0, 0:piece].astype(F32) + got[
            0, starts[blk] : starts[blk] + piece
        ].astype(F32)
        attn_out[blk, 3] = fixed[:, 4 * share :].astype(F32)
        for k in range(4):
            part = fixed[:, k * share : (k + 1) * share].astype(F32)
            down_out[blk, :, k * piece : (k + 1) * piece] = part.T
    for blk in range(2):
        for k in range(10):
            vec_out[k, blk : blk + 1] = rows[10 * blk + k : 10 * blk + k + 1]
        for k in range(4):
            bias_out[blk : blk + 1, k * piece : (k + 1) * piece] = rows[
                20 + 4 * blk + k : 21 + 4 * blk + k
            ]


def body(
    visible,
    masked_queries,
    visible_counts,
    attention_matrices,
    up_projection_weights,
    down_projection_weights,
    vectors,
    up_projection_bias,
    encoder_cotangent,
    cot_regressor,
):
    vis, width = visible.shape[0], visible.shape[2]
    hid = masked_queries.shape[0]
    images = lax.axis_size("img")
    me = lax.axis_index("blk")
    place = lax.axis_index("img")
    pv, pm = round_up(vis, 16), round_up(hid, 16)
    nv, nm = CYCLE * pv, CYCLE * pm
    s = width // CYCLE
    ff = up_projection_weights.shape[2]
    ffb = ff // CYCLE
    natural = images != 8
    vec, upb = jnp.swapaxes(vectors, 0, 1), up_projection_bias
    dma = pltpu.SemaphoreType.DMA

    def pad(rows, to):
        return jnp.pad(rows[:, 0, :], ((0, to - rows.shape[0]), (0, 0)))

    def many(arrays, kind="v"):
        return [(a, kind) for a in arrays]

    scal = jnp.stack([me, visible_counts[0], place]).astype(jnp.int32)
    half = [((width, ff), BF), ((ff, width), BF)]
    ups = many((up_projection_weights, down_projection_weights), "a")
    attn, up0, down0, w_own, b_own = call(
        "prep",
        prep_kernel,
        [(scal, "s"), (attention_matrices, "a")] + ups + [(vec, "v")],
        [(attention_matrices.shape, BF)] + half + [((2, 3, width, s), BF), ((2, 3, 1, s), F32)],
        [dma((4,))],
        keep=True,
    )
    x = jnp.concatenate([pad(visible, pv), pad(masked_queries, pm)], 0)
    xs = gather(x, None, b_own)
    cot_e, cot_g = pad(encoder_cotangent, pv), pad(cot_regressor, pm)

    h0, q0, k0, v0, o0 = call(
        "enc_attend",
        functools.partial(enc_attend_kernel, vis),
        [(scal, "s")] + many(xs) + many([w_own, b_own, vec]),
        [((nv, width), BF)] + [((nv, s), BF)] * 4,
        hold=[attn, up0, down0],
    )
    hm, qm, km, vm = call(
        "mask_project",
        mask_project_kernel,
        many(xs) + many([w_own, b_own, vec]),
        [((nm, width), BF)] + [((nm, s), BF)] * 3,
        after=[o0],
        hold=[attn, up0, down0],
    )
    mixed0 = exchange([o0[j * pv : (j + 1) * pv] for j in range(CYCLE)])
    e, e_b, he, h2_0, y0, r0, z0, gp0 = call(
        "enc_ffn",
        functools.partial(enc_ffn_kernel, vis),
        [(scal, "s")] + many(mixed0) + many([x, vec, upb]) + many([attn, up0, down0], "w"),
        [((pv, width), F32), ((vis, width), BF), ((pv, width), BF), ((pv, width), BF)]
        + [((pv, width), F32)] * 3
        + [((pv, ff), F32)],
        [pltpu.VMEM((pv, width), BF)],
        after=[km],
    )

    up1, down1 = call(
        "load",
        functools.partial(load_kernel, 1),
        ups,
        half,
        [dma((2,))],
        keep=True,
        after=[he],
        hold=[attn, up0, down0],
    )
    hes = gather(he, None, up1)
    h_vis, k1, v1, o1 = call(
        "reg_attend",
        functools.partial(reg_attend_kernel, vis, hid),
        [(scal, "s")] + many(hes) + many([w_own, b_own, qm, km, vm]),
        [((nv, width), BF), ((nv + nm, s), BF), ((nv + nm, s), BF), ((nm, s), BF)],
        hold=[attn, up0, down0, up1, down1],
    )
    mixed1 = exchange([o1[j * pm : (j + 1) * pm] for j in range(CYCLE)])
    g_b, pair1, dr1, dy1, small1, ups1 = call(
        "reg_ffn",
        functools.partial(reg_ffn_kernel, hid),
        [(scal, "s")] + many(mixed1) + many([x, cot_g, vec, upb]) + many([attn, up1, down1], "w"),
        [((hid, width), BF), ((2 * pm, width), BF), ((pm, width), BF), ((pm, width), F32)]
        + [((8, width), F32), ((1, ff), F32)],
        [pltpu.VMEM((pm, width), BF), pltpu.VMEM((pm, ff), F32)],
        hold=[up0, down0],
    )

    piece = width // images
    m = images // CYCLE
    first_x, first_z = [0, 1, 2], [1, 0, 2]

    def message(rows):
        return [((images // 2, rows, width), BF)] * 2

    def by_owner(mat):
        count = mat.shape[0] // m
        cut = mat.reshape(m, count, CYCLE, s).transpose(2, 0, 1, 3)
        return reduce_whole(cut.reshape(images, count, s))

    def by_rows(mat):
        return reduce_whole(mat.reshape(images, piece, mat.shape[1]))

    ffn_whole = [((ffb, width), BF), ((width, ffb), BF)]
    attn_whole = [((width, 3 * s), BF), ((s, width), BF)]

    def fix(down_total, o_total):
        both = jnp.concatenate([down_total[0, :piece], o_total], 1)
        return transpose_owners(both.astype(BF))

    def ffn_scratch(rows):
        return [pltpu.VMEM((rows, width), BF)] * 2

    dr1s = gather(dr1)
    ge, gm, qv1 = call(
        "reg_attend_back",
        functools.partial(reg_attend_back_kernel, vis, hid),
        [(scal, "s")] + many(dr1s) + many([qm, k1, v1]) + [(attn, "w")],
        [((nv, 2 * s), BF), ((nm, 3 * s), BF), ((8, s), F32)],
        [pltpu.VMEM((nm, width), BF)],
        limit=10,
        hold=[up0, down0, up1, down1],
    )
    pairs1 = gather(pair1, dr1s[2], qv1)
    ges = exchange([ge[j * pv : (j + 1) * pv] for j in range(CYCLE)])
    out = call(
        "reg_grad",
        functools.partial(reg_grad_kernel, (first_x, first_z), natural),
        [(scal, "s")]
        + many(pairs1)
        + many([upb, hm, h_vis, gm, ge, o1])
        + many(dr1s + xs + [w_own])
        + many([up1, down1], "w"),
        (ffn_whole + attn_whole if natural else message(piece + piece // 2) * 2)
        + [((8, width), F32)],
        ffn_scratch(nm) + [pltpu.VMEM((nm, width), BF)],
        after=[qv1],
        limit=12,
        hold=[attn, up0, down0],
    )
    norm1 = out[-1]
    if natural:
        sums1 = [by_owner(out[0]), by_rows(out[1]), by_rows(out[2]), by_owner(out[3])]
    else:
        sums1 = [ImgSum(out[0], out[1], first_x), ImgSum(out[2], out[3], first_z)]

    def steps(groups, *after, hold=(attn,)):
        if natural:
            for group in groups:
                for one in group:
                    one.step()
        else:
            step_all(scal, groups, after, hold)

    for one in sums1:
        one.sent = later(one.sent, *ges[1:])
    steps([[one] for one in sums1])
    pair0, dr0, dy0, small0, ups0 = call(
        "enc_ffn_back",
        functools.partial(enc_ffn_back_kernel, vis),
        [(scal, "s")]
        + many(ges)
        + many([e, cot_e, y0, r0, z0, gp0, h2_0, vec])
        + many([attn, up0, down0], "w"),
        [((2 * pv, width), BF), ((pv, width), BF), ((pv, width), F32), ((8, width), F32)]
        + [((1, ff), F32)],
        [pltpu.VMEM((pv, width), BF)] * 2,
        after=[norm1],
    )

    dr0s = gather(dr0)
    out = call(
        "enc_attend_back",
        functools.partial(enc_attend_back_kernel, vis, first_x, natural),
        [(scal, "s")]
        + many(dr0s)
        + many([h0, q0, k0, v0, o0, gm] + xs + [w_own])
        + many([small0, small1, norm1, qv1, ups0, ups1])
        + [(attn, "w")],
        [((CYCLE, pv + pm, 3 * s), BF), ((32, width), F32)]
        + (attn_whole if natural else message(piece + 16)),
        [pltpu.VMEM((nv, width), BF), pltpu.VMEM((8, s), F32), pltpu.VMEM((8, width), F32)],
        after=[sums1[0].sent],
        limit=10,
        hold=[up0, down0],
    )
    g, rows = out[:2]
    if natural:
        attn0, o0_sum = by_rows(out[2]), by_owner(out[3])
    else:
        attn0 = ImgSum(out[2], out[3], first_x)
    steps([[attn0]])
    steps([[one] for one in sums1], rows, hold=(attn, up0, down0))
    pairs0 = gather(pair0, dr0s[2], rows)
    out = call(
        "enc_ffn_grad",
        functools.partial(enc_ffn_grad_kernel, (first_z, first_x), natural),
        [(scal, "s")] + many(pairs0) + many([upb]) + many([up0, down0], "w"),
        ffn_whole if natural else message(piece) * 2,
        ffn_scratch(nv),
        after=[sums1[0].sent],
        hold=[attn],
    )
    if natural:
        ffn0 = [by_owner(out[0]), by_rows(out[1])]
    else:
        ffn0 = [ImgSum(out[0], out[1], first_z), ImgSum(out[2], out[3], first_x)]
    steps([[one] for one in ffn0])
    steps([sums1], out[0])
    steps([ffn0[:1], [ffn0[1], attn0]], sums1[0].got)
    g = later(g, ffn0[0].sent)
    gs = exchange([g[j] for j in range(CYCLE)])
    if not natural:
        for one in sums1:
            one.got = later(one.got, ffn0[0].sent)
        totals = [sums.total() for sums in sums1]
        fixed1 = fix(
            totals[0], jnp.concatenate([total[0, piece:, 3 * s :] for total in totals], 0)
        )
        steps([ffn0 + [attn0]])
    grad_x, grad_m = call(
        "input_grad",
        input_grad_kernel,
        [(scal, "s")] + many(gs) + many([x, dy0, dy1, vec]) + [(attn, "w")],
        [((vis, 1, width), F32), ((hid, 1, width), F32)],
        [pltpu.VMEM((pv + pm, width), BF)] * 3,
        after=[ffn0[0].sent],
    )

    if natural:

        def owned(sums):
            return transpose_owners(sums.finish().astype(BF)).astype(F32)

        ups, downs, attns = [], [], []
        for down_sum, up_sum, qkv, o_sum in (ffn0 + [attn0, o0_sum], sums1):
            ups.append(up_sum.finish())
            downs.append(owned(down_sum))
            got = qkv.finish()
            attns.append(
                jnp.stack([got[:, :s], got[:, s : 2 * s], got[:, 2 * s :], owned(o_sum)])
            )
        grad_attn, grad_up, grad_down = jnp.stack(attns), jnp.stack(ups), jnp.stack(downs)
        for axis in ("blk", "img"):
            j = 1
            while j < lax.axis_size(axis):
                rows = rows + swap(rows, axis, j)
                j *= 2
        vec_total = lax.dynamic_slice_in_dim(rows[:20], place * piece, piece, 1)
        vec_total = vec_total.reshape(2, 10, piece)
        bias_total = lax.dynamic_slice_in_dim(
            rows[20:28].reshape(2, ff), place * (ff // images), ff // images, 1
        )
    else:
        got0 = later(ffn0[0].got, grad_x)
        for one in ffn0 + [attn0]:
            one.got = got0
        both = attn0.total()[0, piece:, : 2 * piece]
        rows = jnp.concatenate([both[:, :piece], both[:, piece:]], 0)
        rows = rows + swap(rows, "blk", 1)
        rows = rows + swap(rows, "blk", 2)
        fixed0 = fix(ffn0[0].total(), attn0.total()[0, :piece, 3 * s :])
        last = [ffn0[1].keep, attn0.keep, got0, fixed0]
        last += [sums1[1].keep, sums1[0].keep, sums1[1].got, fixed1]
        grad_attn, grad_up, grad_down, vec_total, bias_total = call(
            "finish",
            finish_kernel,
            [(scal, "s")] + many(last + [rows]),
            [
                ((2, 4, piece, s), F32),
                ((2, piece, ffb), F32),
                ((2, s, ff // images), F32),
                ((10, 2, piece), F32),
                ((2, ff // images), F32),
            ],
        )
        grad_down, vec_total = jnp.swapaxes(grad_down, 1, 2), jnp.swapaxes(vec_total, 0, 1)

    return (
        e_b[:, None, :],
        g_b[:, None, :],
        grad_x,
        grad_m,
        grad_attn,
        grad_up,
        grad_down,
        vec_total,
        bias_total,
    )


def solution(mesh):
    rows = P("blk", "img", None)
    in_specs = (rows, rows, P("img"), P(), P(), P(), P(), P(), rows, rows)
    out_specs = (
        rows,
        rows,
        rows,
        rows,
        P(None, None, "img", "blk"),
        P(None, "img", "blk"),
        P(None, "img", "blk"),
        P(None, None, "img"),
        P(None, "img"),
    )
    return jax.shard_map(body, mesh=mesh, in_specs=in_specs, out_specs=out_specs, check_vma=False)
```

```python
import functools

import jax
import jax.numpy as jnp
from jax import lax
from jax.experimental import pallas as pl
from jax.experimental.pallas import tpu as pltpu
from jax.sharding import PartitionSpec as P

HEADS = 12
HEAD = 64
NPATCH = 576
EPS = 1e-06
BF = jnp.bfloat16
F32 = jnp.float32
CYCLE = 4
MIB = 1024 * 1024
COSTS = {'prep': 4.0, 'load': 5.0, 'tail': 1.0, 'vectors': 0.5, 'enc_attend': 3.3, 'mask_project': 0.9, 'enc_ffn': 5.9, 'reg_attend': 3.4, 'reg_ffn': 8.2, 'reg_attend_back': 5.7, 'reg_attn_grad': 2.7, 'reg_ffn_grad': 4.5, 'enc_ffn_back': 0.01, 'enc_attend_back': 8.0, 'enc_ffn_grad': 0.01, 'img_step': 0.01, 'input_grad': 7.4, 'finish': 2.6}
COST_SCALE = 0.3


def round_up(value, unit):
    return (value + unit - 1) // unit * unit


def dot(left, right):
    return jnp.dot(left, right, preferred_element_type=F32)


def dot_nt(left, right):
    return lax.dot_general(left, right, (((1,), (1,)), ((), ())), preferred_element_type=F32)


def dot_tn(left, right):
    return lax.dot_general(left, right, (((0,), (0,)), ((), ())), preferred_element_type=F32)


def norm(rows):
    centred = rows - jnp.mean(rows, -1, keepdims=True)
    inverse = lax.rsqrt(jnp.mean(centred * centred, -1, keepdims=True) + EPS)
    return centred * inverse, inverse


def norm_back(grad_out, gain, normed, inverse):
    scaled = grad_out * gain
    return inverse * (
        scaled
        - jnp.mean(scaled, -1, keepdims=True)
        - normed * jnp.mean(scaled * normed, -1, keepdims=True)
    )


def gelu_parts(u):
    cdf = 0.5 * (1.0 + lax.erf(u * 0.7071067811865476))
    slope = cdf + u * (jnp.exp(u * u * -0.5) * 0.3989422804014327)
    return cdf, slope


def col_sum(rows):
    return jnp.sum(rows, 0, keepdims=True)


def swap(block, axis, offset):
    size = lax.axis_size(axis)
    return lax.ppermute(block, axis, [(i, i ^ offset) for i in range(size)])


def gather(block, first=None, second=None):
    across = swap(block if first is None else later(block, first), "blk", 2)
    if second is not None:
        over, beside = swap(later(across, second), "blk", 1), later(block, second)
    else:
        over, beside = swap(across, "blk", 1), block
    return [block, swap(beside, "blk", 1), across, over]


def later(value, *arrays):
    return lax.optimization_barrier((value, *arrays))[0]


def exchange(blocks, held=None):
    sent = blocks if held is None else held
    across, over = swap(sent[2], "blk", 2), swap(sent[3], "blk", 3)
    return [blocks[0], swap(sent[1], "blk", 1), across, over]


class ImgSum:
    def __init__(self, keep, sent, order):
        self.order = list(order)
        self.keep, self.sent, self.got = keep, sent, None
        self.at = slice(0, keep.shape[1])

    def step(self, *after):
        bit = self.order.pop(0)
        if self.got is not None:
            total = self.total().astype(BF)
            total = total.reshape((2, total.shape[0] // 2) + total.shape[1:])
            mine = (lax.axis_index("img") >> bit) & 1
            self.keep = lax.dynamic_index_in_dim(total, mine, 0, False)
            self.sent = lax.dynamic_index_in_dim(total, 1 - mine, 0, False)
        if after:
            self.sent = later(self.sent, *after)
        self.got = swap(self.sent, "img", 1 << bit)
        return self.sent

    def total(self):
        return self.keep.astype(F32) + self.got[:, self.at].astype(F32)

    def finish(self):
        while self.order:
            self.step()
        return self.total()[0]


def reduce_whole(parts):
    images = parts.shape[0]
    place = lax.axis_index("img")
    bits = images.bit_length() - 1
    pairs = parts.reshape((2, images // 2) + parts.shape[1:])
    mine = place >> (bits - 1)
    keep = lax.dynamic_index_in_dim(pairs, mine, 0, False)
    sent = lax.dynamic_index_in_dim(pairs, 1 - mine, 0, False)
    return ImgSum(keep, sent, range(bits - 1, -1, -1))


def transpose_owners(part):
    images, cycle = lax.axis_size("img"), lax.axis_size("blk")
    m = images // cycle
    pairs = []
    for i in range(images):
        for b in range(cycle):
            pairs.append((i * cycle + b, (b * m + i % m) * cycle + i // m))
    return lax.ppermute(part, ("img", "blk"), pairs)


def call(name, kernel, ins, outs, scratch=(), limit=8, after=(), keep=False, hold=(), alias=()):
    spaces = {"s": pltpu.SMEM, "v": pltpu.VMEM, "w": pltpu.VMEM, "a": pltpu.HBM, "n": pl.ANY}
    places = {"w": pltpu.VMEM, "a": pltpu.HBM}
    count = len(ins)
    ins = ins + [(a, "n") for a in after] + [(a, "w") for a in hold]

    def run(*refs):
        kernel(*refs[:count], *refs[len(ins) :])

    return pl.pallas_call(
        run,
        name=name,
        out_shape=[
            pltpu.VMEM(s, d) if keep else jax.ShapeDtypeStruct(s, d) for s, d in outs
        ],
        in_specs=[pl.BlockSpec(memory_space=spaces[k]) for _, k in ins],
        out_specs=[pl.BlockSpec(memory_space=pltpu.VMEM) for _ in outs],
        scratch_shapes=list(scratch),
        input_output_aliases=dict(alias),
        compiler_params=pltpu.CompilerParams(vmem_limit_bytes=limit * MIB),
        cost_estimate=pl.CostEstimate(
            flops=int(COST_SCALE * COSTS[name] * 1.15e9), bytes_accessed=1, transcendentals=0
        ),
    )(*[pltpu.with_memory_space_constraint(a, places[k]) if k in places else a for a, k in ins])


def step_kernel(bits, starts, groups, scal, *refs):
    count = len(bits)
    ins, keeps, outs = refs[: 2 * count], refs[2 * count : 3 * count], refs[3 * count :]
    for out, group in zip(outs, groups):
        start = 0
        for k in group:
            keep, got = ins[2 * k : 2 * k + 2]
            half, rows = keep.shape[0] // 2, keep.shape[1]
            mine = (scal[2] >> bits[k]) & 1
            sides = []
            for side in (mine, 1 - mine):
                at = pl.ds(side * half, half)
                other = got[at, starts[k] : starts[k] + rows]
                sides.append((keep[at].astype(F32) + other.astype(F32)).astype(BF))
            keeps[k][...] = sides[0]
            out[:, start : start + rows] = sides[1]
            start += rows


def step_all(scal, groups, after=(), hold=()):
    sums = [one for group in groups for one in group]
    if sums[0].got is not None:
        bits = [one.order[0] for one in sums]
        places, ins, keeps, outs = [], [(scal, "s")], [], []
        for group in groups:
            places.append([sums.index(one) for one in group])
            half, rows = group[0].keep.shape[0] // 2, 0
            for one in group:
                ins += [(one.keep, "v"), (one.got, "v")]
                keeps.append(((half,) + one.keep.shape[1:], BF))
                rows += one.keep.shape[1]
            outs.append(((half, rows, one.keep.shape[2]), BF))
        parts = call(
            "img_step",
            functools.partial(step_kernel, bits, [one.at.start for one in sums], places),
            ins,
            keeps + outs,
            after=after,
            hold=hold,
        )
        for k, one in enumerate(sums):
            one.keep = parts[k]
        sent = parts[len(sums) :]
    else:
        sent = [group[0].sent for group in groups]
    for group, message in zip(groups, sent):
        got, start = swap(message, "img", 1 << group[0].order[0]), 0
        for one in group:
            rows = one.keep.shape[1]
            one.order.pop(0)
            one.sent, one.got = message, got
            one.at, start = slice(start, start + rows), start + rows


def load_kernel(blk, cut, scal, *refs):
    sems = refs[-1]
    count = (len(refs) - 1) // 2
    copies = []
    for k, (source, target) in enumerate(zip(refs[:count], refs[count:-1])):
        source = source.at[blk]
        if cut:
            width = target.shape[0]
            mine = pl.ds(pl.multiple_of(scal[0] * width, 128), width)
            source = source.at[:, mine] if k == 0 else source.at[mine]
        copies.append(pltpu.make_async_copy(source, target, sems.at[k]))
    for copy in copies:
        copy.start()
    for copy in copies:
        copy.wait()


def prep_kernel(scal, attn, up, vectors, attn_out, up_out, vec, w_out, b_out, sems):
    me = scal[0]
    share = w_out.shape[3]
    window = share + share % 128
    odd = me & 1
    start = pl.multiple_of(me * share - odd * (share % 128), 128)
    copies = [
        pltpu.make_async_copy(attn.at[blk], attn_out.at[blk], sems.at[blk]) for blk in range(2)
    ]
    copies.append(pltpu.make_async_copy(up.at[0], up_out, sems.at[2]))
    copies.append(pltpu.make_async_copy(vectors, vec, sems.at[3]))
    for copy in copies[::-1]:
        copy.start()
    copies[3].wait()
    for blk in range(2):
        copies[blk].wait()
        for m in range(3):
            for parity in range(2):
                shift = parity * (share % 128)

                @pl.when(odd == parity)
                def _():
                    part = attn_out[blk, m, :, pl.ds(start, window)]
                    w_out[blk, m] = part[:, shift : shift + share]
                    if m == 1:
                        b_out[blk, m] = jnp.zeros((1, share), F32)
                    else:
                        row = vec[2 + m // 2, blk : blk + 1, pl.ds(start, window)]
                        b_out[blk, m] = row[:, shift : shift + share]
    copies[2].wait()


def key_bias(me, rows, padded, limit):
    at = lax.broadcasted_iota(jnp.int32, (padded, 1), 0)
    parts = []
    for j in range(CYCLE):
        live = (at < rows) & (at + (me ^ j) * rows < limit)
        parts.append(jnp.where(live, 0.0, -1e30))
    return jnp.concatenate(parts, 0)


def own_live(me, rows, padded, limit):
    at = lax.broadcasted_iota(jnp.int32, (padded, 1), 0)
    return jnp.where((at < rows) & (at + me * rows < limit), 1.0, 0.0)


def probs_t(keys, queries, bias):
    scores = dot_nt(keys, queries) + bias
    exps = jnp.exp(scores - jnp.max(scores, 0, keepdims=True))
    return exps * (1.0 / jnp.sum(exps, 0, keepdims=True))


def attend_t(q, k, v, bias, out_ref):
    qs = (q.astype(F32) * HEAD**-0.5).astype(BF)
    vt = v.astype(F32).T.astype(BF)
    mixed = []
    for h in range(q.shape[1] // HEAD):
        c = slice(h * HEAD, (h + 1) * HEAD)
        p = probs_t(k[:, c], qs[:, c], bias).astype(BF)
        mixed.append(dot(vt[c], p))
    out_ref[...] = jnp.concatenate(mixed, 0).T.astype(BF)


def attend_back_t(q, k, v, do, bias):
    qs = (q.astype(F32) * HEAD**-0.5).astype(BF)
    kt = (k.astype(F32) * HEAD**-0.5).T.astype(BF)
    dq, dk, dv = [], [], []
    for h in range(q.shape[1] // HEAD):
        c = slice(h * HEAD, (h + 1) * HEAD)
        p = probs_t(k[:, c], qs[:, c], bias)
        dp = dot_nt(v[:, c], do[:, c])
        ds = (p * (dp - jnp.sum(p * dp, 0, keepdims=True))).astype(BF)
        dv.append(dot(p.astype(BF), do[:, c]))
        dk.append(dot(ds, qs[:, c]))
        dq.append(dot(kt[c], ds))
    return (
        jnp.concatenate(dq, 0).T.astype(BF),
        jnp.concatenate(dk, 1).astype(BF),
        jnp.concatenate(dv, 1).astype(BF),
    )


def enc_attend_kernel(vis, scal, x0, x1, x2, x3, w, b, vec, h_out, q_out, k_out, v_out, o_out):
    me, count = scal[0], scal[1]
    padded = h_out.shape[0] // CYCLE
    for j, ref in enumerate((x0, x1, x2, x3)):
        n, _ = norm(ref[0:padded].astype(F32))
        h_out[j * padded : (j + 1) * padded] = (n * vec[0, 0:1] + vec[1, 0:1]).astype(BF)
    h = h_out[...]
    q = (dot(h, w[0, 0]) + b[0, 0]).astype(BF)
    k = dot(h, w[0, 1]).astype(BF)
    v = (dot(h, w[0, 2]) + b[0, 2]).astype(BF)
    q_out[...], k_out[...], v_out[...] = q, k, v
    attend_t(q, k, v, key_bias(me, vis, padded, count), o_out)


def mask_project_kernel(x0, x1, x2, x3, w, b, vec, h_out, q_out, k_out, v_out):
    padded = h_out.shape[0] // CYCLE
    for j, ref in enumerate((x0, x1, x2, x3)):
        n, _ = norm(ref[x0.shape[0] - padded :].astype(F32))
        h_out[j * padded : (j + 1) * padded] = (n * vec[0, 1:2] + vec[1, 1:2]).astype(BF)
    h = h_out[...]
    q_out[...] = (dot(h, w[1, 0]) + b[1, 0]).astype(BF)
    k_out[...] = dot(h, w[1, 1]).astype(BF)
    v_out[...] = (dot(h, w[1, 2]) + b[1, 2]).astype(BF)


def reg_attend_kernel(
    vis, hid, scal, x0, x1, x2, x3, w, b, qm, km, vm, h_out, k_out, v_out, o_out
):
    me, count = scal[0], scal[1]
    padded = x0.shape[0]
    nv = CYCLE * padded
    for j, ref in enumerate((x0, x1, x2, x3)):
        h_out[j * padded : (j + 1) * padded] = ref[...]
    h = h_out[...]
    k_out[0:nv] = dot(h, w[1, 1]).astype(BF)
    v_out[0:nv] = (dot(h, w[1, 2]) + b[1, 2]).astype(BF)
    k_out[nv:] = km[...]
    v_out[nv:] = vm[...]
    bias = jnp.concatenate(
        [
            key_bias(me, vis, padded, count),
            key_bias(me, hid, qm.shape[0] // CYCLE, NPATCH - count),
        ],
        0,
    )
    attend_t(qm[...], k_out[...], v_out[...], bias, o_out)


def assemble(me, blocks, scratch, lane):
    share = blocks[0].shape[1] if lane is None else lane[1]
    rows = scratch.shape[0]
    for m in range(CYCLE):

        @pl.when(me == m)
        def _():
            for j, ref in enumerate(blocks):
                at = (m ^ j) * share
                value = ref[...] if lane is None else ref[0:rows, lane[0] : lane[0] + share]
                scratch[:, at : at + share] = value


def ffn_forward(blk, rows, mixed, vec, upb, attn, up, down, gp):
    r = dot(mixed, attn[blk, 3]) + vec[4, blk : blk + 1]
    y = rows + vec[5, blk : blk + 1] * r
    n, _ = norm(y)
    h2 = (n * vec[6, blk : blk + 1] + vec[7, blk : blk + 1]).astype(BF)
    width = up.shape[0]
    z = vec[8, blk : blk + 1]
    for c in range(up.shape[1] // width):
        cols = slice(c * width, (c + 1) * width)
        u = dot(h2, up[:, cols]) + upb[blk : blk + 1, cols]
        cdf, slope = gelu_parts(u)
        gp[:, cols] = slope
        a = (u * cdf).astype(BF)
        z = z + dot(a, down[cols, :])
    return r, y, h2, z


def ffn_backward(blk, grad, r, y, z, vec, up, down, gp, up_sum):
    n, inverse = norm(y)
    scale2 = col_sum(grad * z)
    dz = (grad * vec[9, blk : blk + 1]).astype(BF)
    width = up.shape[0]
    dh2 = 0.0
    for c in range(up.shape[1] // width):
        cols = slice(c * width, (c + 1) * width)
        da = dot_nt(dz, down[cols, :])
        du = (gp[:, cols] * da).astype(BF)
        up_sum[:, cols] = col_sum(du.astype(F32))
        dh2 = dh2 + dot_nt(du, up[:, cols])
    dy = grad + norm_back(dh2, vec[6, blk : blk + 1], n, inverse)
    dr = (dy * vec[5, blk : blk + 1]).astype(BF)
    small = [
        scale2,
        col_sum(dh2 * n),
        col_sum(dh2),
        col_sum(dy * r),
        col_sum(dz.astype(F32)),
        col_sum(dr.astype(F32)),
    ]
    return dz, dy, dr, small


def enc_ffn_kernel(
    vis, scal, o0, o1, o2, o3, x, vec, upb, attn, up, down,
    e_out, eb_out, he_out, h2_out, y_out, r_out, z_out, gp_out,
    mixed,
):
    me, count = scal[0], scal[1]
    assemble(me, (o0, o1, o2, o3), mixed, None)
    r, y, h2, z = ffn_forward(
        0, x[0 : he_out.shape[0]].astype(F32), mixed[...], vec, upb, attn, up, down, gp_out
    )
    h2_out[...], y_out[...], r_out[...], z_out[...] = h2, y, r, z
    e = (y + vec[9, 0:1] * z) * own_live(me, vis, he_out.shape[0], count)
    e_out[...] = e
    eb_out[...] = e[0 : eb_out.shape[0]].astype(BF)
    n, _ = norm(e)
    he_out[...] = (n * vec[0, 1:2] + vec[1, 1:2]).astype(BF)


def reg_ffn_kernel(
    hid, scal, o0, o1, o2, o3, x, cot, vec, upb, attn, up, down,
    gb_out, pair_out, dr_out, dy_out, small_out, up_sum,
    mixed, gp,
):
    me, count = scal[0], scal[1]
    assemble(me, (o0, o1, o2, o3), mixed, None)
    r, y, h2, z = ffn_forward(
        1, x[x.shape[0] - dr_out.shape[0] :].astype(F32), mixed[...], vec, upb, attn, up, down, gp
    )
    padded = dr_out.shape[0]
    live = own_live(me, hid, padded, NPATCH - count)
    g = (y + vec[9, 1:2] * z) * live
    gb_out[...] = g[0 : gb_out.shape[0]].astype(BF)
    grad = cot[...].astype(F32) * live
    dz, dy, dr, small = ffn_backward(1, grad, r, y, z, vec, up, down, gp, up_sum)
    pair_out[0:padded] = h2
    pair_out[padded:] = dz
    dr_out[...] = dr
    dy_out[...] = dy
    for i, row in enumerate(small):
        small_out[i : i + 1] = row
    small_out[6:8] = jnp.zeros((2, small_out.shape[1]), F32)


def enc_ffn_back_kernel(
    vis, scal, g0, g1, g2, g3, e, cot, y, r, z, gp, h2, vec, attn, up, down,
    pair_out, dr_out, dy_out, small_out, up_sum,
    dk, dv,
):
    me, count = scal[0], scal[1]
    share = g0.shape[1] // 2
    assemble(me, (g0, g1, g2, g3), dk, (0, share))
    assemble(me, (g0, g1, g2, g3), dv, (share, share))
    n, inverse = norm(e[...])
    dh = dot_nt(dk[...], attn[1, 1]) + dot_nt(dv[...], attn[1, 2])
    grad_e = norm_back(dh, vec[0, 1:2], n, inverse)
    grad = (cot[...].astype(F32) + grad_e) * own_live(me, vis, cot.shape[0], count)
    dz, dy, dr, small = ffn_backward(
        0, grad, r[...], y[...], z[...], vec, up, down, gp, up_sum
    )
    pair_out[0 : dz.shape[0]] = h2[...]
    pair_out[dz.shape[0] :] = dz
    dy_out[...], dr_out[...] = dy, dr
    for i, row in enumerate(small + [col_sum(dh * n), col_sum(dh)]):
        small_out[i : i + 1] = row


def spread(place_of, keep, sent, place, order, rows, cols):
    first, second, third = order
    for i in range(8):
        t = 2 * ((i >> second) & 1) + ((i >> third) & 1)
        value = place_of(i)

        for side in range(2):
            target = keep if side == ((i >> first) & 1) else sent

            @pl.when(((place >> first) & 1) == side)
            def _():
                target[t, rows, cols] = value


def owner_piece(mat, i, share, parts):
    quarter, half = i >> 1, i & 1
    rows = mat.shape[0] // 2
    part = mat[half * rows : (half + 1) * rows, quarter * share : (quarter + 1) * share]
    rows = rows // parts
    return jnp.concatenate([part[k * rows : (k + 1) * rows] for k in range(parts)], 1)


def attn_pieces(h, dqkv, o, dr):
    share = dqkv[0].shape[1]
    results = [dot_tn(h, grad).astype(BF) for grad in dqkv]
    d_o = dot_tn(o, dr).astype(BF)
    step = h.shape[1] // 8

    def piece(i):
        parts = [result[i * step : (i + 1) * step] for result in results]
        return jnp.concatenate(parts + [owner_piece(d_o, i, share, 1)], 1)

    return results, d_o, piece


def norm_sums(rows, dqkv, w):
    dh = 0.0
    for m, grad in enumerate(dqkv):
        dh = dh + dot_nt(grad, w[m])
    n, _ = norm(rows.astype(F32))
    return col_sum(dh * n), col_sum(dh)


def store_attn(results, d_o, nats):
    share = d_o.shape[0]
    for m, result in enumerate(results):
        nats[0][:, m * share : (m + 1) * share] = result
    nats[1][...] = d_o


def reg_attend_back_kernel(
    vis, hid, scal, d0, d1, d2, d3, q, k, v, attn,
    e_out, m_out, qv_out,
    dr,
):
    me, count = scal[0], scal[1]
    share = q.shape[1]
    padded = d0.shape[0]
    for j, ref in enumerate((d0, d1, d2, d3)):
        dr[j * padded : (j + 1) * padded] = ref[...]
    do = dot_nt(dr[...], attn[1, 3, pl.ds(pl.multiple_of(me * share, 16), share), :]).astype(BF)
    nm = CYCLE * padded
    nv = k.shape[0] - nm
    bias = jnp.concatenate(
        [
            key_bias(me, vis, nv // CYCLE, count),
            key_bias(me, hid, padded, NPATCH - count),
        ],
        0,
    )
    dq, dk, dv = attend_back_t(q[...], k[...], v[...], do, bias)
    e_out[:, 0:share] = dk[0:nv]
    e_out[:, share:] = dv[0:nv]
    m_out[:, 0:share] = dq
    m_out[:, share : 2 * share] = dk[nv:]
    m_out[:, 2 * share :] = dv[nv:]
    qv_out[0:1] = col_sum(dq.astype(F32))
    qv_out[1:2] = col_sum(dv.astype(F32))
    qv_out[2:8] = jnp.zeros((6, share), F32)


def enc_attend_back_kernel(
    vis, order, natural, scal, d0, d1, d2, d3, h, q, k, v, o, gm, x0, x1, x2, x3, w,
    small0, small1, norm1, qv1, ups0, ups1, attn,
    g_out, vec_out, first, second, dr, qv0, norm0,
):
    me, count = scal[0], scal[1]
    share = q.shape[1]
    padded = d0.shape[0]
    for j, ref in enumerate((d0, d1, d2, d3)):
        dr[j * padded : (j + 1) * padded] = ref[...]
    do = dot_nt(dr[...], attn[0, 3, pl.ds(pl.multiple_of(me * share, 16), share), :]).astype(BF)
    dq, dk, dv = attend_back_t(
        q[...], k[...], v[...], do, key_bias(me, vis, padded, count)
    )
    for j in range(CYCLE):
        at = slice(j * padded, (j + 1) * padded)
        for m, grad in enumerate((dq, dk, dv)):
            g_out[j, 0:padded, m * share : (m + 1) * share] = grad[at]
        more = g_out.shape[1] - padded
        g_out[j, padded:] = gm[j * more : (j + 1) * more]
    qv0[0:1] = col_sum(dq.astype(F32))
    qv0[1:2] = col_sum(dv.astype(F32))
    x = jnp.concatenate([ref[0:padded] for ref in (x0, x1, x2, x3)], 0)
    norm0[0:1], norm0[1:2] = norm_sums(x, (dq, dk, dv), (w[0, 0], w[0, 1], w[0, 2]))
    vector_rows(
        natural, me, (small0, small1), (norm0, norm1), (qv0, qv1), (ups0, ups1), vec_out
    )
    results, d_o, piece = attn_pieces(h[...], (dq, dk, dv), o[...], dr[...])
    if natural:
        store_attn(results, d_o, (first, second))
        return
    step, cols = h.shape[1] // 8, slice(0, 4 * share)

    def vector_piece(i):
        mine = slice(i * step, (i + 1) * step)
        parts = [vec_out[0:16, mine], vec_out[16:32, mine]]
        parts.append(jnp.zeros((16, 4 * share - 2 * step), F32))
        return jnp.concatenate(parts, 1).astype(BF)

    spread(piece, first, second, scal[2], order, slice(0, step), cols)
    spread(vector_piece, first, second, scal[2], order, slice(step, step + 16), cols)


def ffn_pieces(blk, scal, pairs, upb, up, down, h2, dz):
    me = scal[0]
    width = up.shape[0]
    cols = pl.ds(pl.multiple_of(me * width, 128), width)
    padded = pairs[0].shape[0] // 2
    for j, pair in enumerate(pairs):
        at = slice(j * padded, (j + 1) * padded)
        h2[at] = pair[0:padded]
        dz[at] = pair[padded:]
    whole = pl.ds(0, width) if up.shape[1] == width else cols
    u = dot(h2[...], up[:, whole]) + upb[blk : blk + 1, cols]
    cdf, slope = gelu_parts(u)
    du = (slope * dot_nt(dz[...], down[whole, :])).astype(BF)
    a = (u * cdf).astype(BF)
    d_down = dot_tn(a, dz[...]).astype(BF)
    d_up = dot_tn(h2[...], du).astype(BF)
    step = width // 8
    return (
        d_down,
        d_up,
        lambda i: owner_piece(d_down, i, width // 4, 4),
        lambda i: d_up[i * step : (i + 1) * step],
    )


def vector_rows(natural, me, smalls, norms, qvs, ups, out):
    share, width = qvs[0].shape[1], out.shape[1]
    step = width // 8
    out[...] = jnp.zeros(out.shape, F32)
    for blk, (small, qv, up_sum) in enumerate(zip(smalls, qvs, ups)):
        at = 10 * blk
        gain, bias = norms[blk][0:1], norms[blk][1:2]
        if blk == 1:
            gain, bias = gain + smalls[0][6:7], bias + smalls[0][7:8]
        scale2, gain2, bias2, scale1, dzs, drs = [small[i : i + 1] for i in range(6)]
        rows = {0: gain, 1: bias, 4: drs, 5: scale1, 6: gain2, 7: bias2, 8: dzs, 9: scale2}
        for i, row in rows.items():
            out[at + i : at + i + 1] = row
        first = 20 + 4 * blk
        for k in range(4):
            if natural:
                out[first + k : first + k + 1] = up_sum[0:1, k * width : (k + 1) * width]
            else:
                parts = [
                    up_sum[0:1, (4 * i + k) * step : (4 * i + k + 1) * step] for i in range(8)
                ]
                out[first + k : first + k + 1] = jnp.concatenate(parts, 1)
        for m in range(CYCLE):

            @pl.when(me == m)
            def _():
                cols = slice(m * share, (m + 1) * share)
                out[at + 2 : at + 3, cols] = qv[0:1]
                out[at + 3 : at + 4, cols] = qv[1:2]


def enc_ffn_grad_kernel(orders, natural, scal, p0, p1, p2, p3, upb, up, down, *refs):
    outs, scratch = refs[:-2], refs[-2:]
    d_down, d_up, down_piece, up_piece = ffn_pieces(
        0, scal, (p0, p1, p2, p3), upb, up, down, *scratch
    )
    if natural:
        outs[0][...], outs[1][...] = d_down, d_up
        return
    here, cols = slice(0, d_up.shape[0] // 8), slice(0, d_up.shape[1])
    spread(down_piece, outs[0], outs[1], scal[2], orders[0], here, cols)
    spread(up_piece, outs[2], outs[3], scal[2], orders[1], here, cols)


def reg_attn_grad_kernel(
    orders, natural, scal, h_m, h_e, g_m, g_e, o, d0, d1, d2, d3, x0, x1, x2, x3, w, *refs
):
    outs, norm_out, dr = refs[:-2], refs[-2], refs[-1]
    share = g_e.shape[1] // 2
    padded = d0.shape[0]
    for j, ref in enumerate((d0, d1, d2, d3)):
        dr[j * padded : (j + 1) * padded] = ref[...]
    x = jnp.concatenate([ref[ref.shape[0] - padded :] for ref in (x0, x1, x2, x3)], 0)
    dqkv_m = [g_m[:, m * share : (m + 1) * share] for m in range(3)]
    norm_out[0:1], norm_out[1:2] = norm_sums(x, dqkv_m, (w[1, 0], w[1, 1], w[1, 2]))
    norm_out[2:8] = jnp.zeros((6, norm_out.shape[1]), F32)
    h = jnp.concatenate([h_e[...], h_m[...]], 0)
    none = jnp.zeros((h_e.shape[0], share), BF)
    grads = []
    for m in range(3):
        top = none if m == 0 else g_e[:, (m - 1) * share : m * share]
        grads.append(jnp.concatenate([top, dqkv_m[m]], 0))
    results, d_o, attn_piece = attn_pieces(h, grads, o[...], dr[...])
    if natural:
        store_attn(results, d_o, outs)
        return
    step, cols = h.shape[1] // 8, slice(0, h.shape[1])
    half = step // 2
    for k in range(2):
        spread(
            lambda i: attn_piece(i)[k * half : (k + 1) * half], outs[2 * k], outs[2 * k + 1],
            scal[2], orders[k], slice(step, step + half), cols,
        )


def reg_ffn_grad_kernel(orders, natural, scal, p0, p1, p2, p3, upb, up, down, *refs):
    outs, scratch = refs[-6:-2] if not natural else refs[-4:-2], refs[-2:]
    d_down, d_up, down_piece, up_piece = ffn_pieces(
        1, scal, (p0, p1, p2, p3), upb, up, down, *scratch
    )
    if natural:
        outs[0][...], outs[1][...] = d_down, d_up
        return
    step, cols = d_up.shape[0] // 8, slice(0, d_up.shape[1])
    for k, piece in enumerate((down_piece, up_piece)):
        spread(piece, outs[2 * k], outs[2 * k + 1], scal[2], orders[k], slice(0, step), cols)


def input_grad_kernel(
    scal, g0, g1, g2, g3, x, mq, dy0, dy1, vec, attn, out0, out1, dq, dk, dv
):
    share = g0.shape[1] // 3
    grads = (dq, dk, dv)
    for m, ref in enumerate(grads):
        assemble(scal[0], (g0, g1, g2, g3), ref, (m * share, share))
    first = dy0.shape[0]
    rows = (slice(0, first), slice(first, g0.shape[0]))
    for blk, (at, own, dy, out) in enumerate(
        ((rows[0], x, dy0, out0), (rows[1], mq, dy1, out1))
    ):
        n, inverse = norm(own[...].astype(F32))
        dh = 0.0
        for m, ref in enumerate(grads):
            dh = dh + dot_nt(ref[at], attn[blk, m])
        dx = norm_back(dh, vec[0, blk : blk + 1], n, inverse) + dy[...]
        out[:, 0, :] = dx[0 : out.shape[0]]


def tail_kernel(parts, scal, *refs):
    ins, out = refs[:-1], refs[-1]

    def total(part, cols):
        keep, at, got, got_at = part
        return ins[keep][0, at, cols].astype(F32) + ins[got][0, got_at, cols].astype(F32)

    width = ins[0].shape[2]
    share = width // CYCLE
    out[:, 0:width] = total(parts[0], slice(0, width)).astype(BF)
    start = 0
    for part in parts[1:]:
        at = slice(start, start + part[1].stop - part[1].start)
        out[at, width:] = total(part, slice(3 * share, width)).astype(BF)
        start = at.stop


def vector_total_kernel(at, keep, got, out):
    step = out.shape[1]
    for k in range(2):
        cols = slice(k * step, (k + 1) * step)
        out[16 * k : 16 * k + 16] = keep[0, at, cols].astype(F32) + got[0, at, cols].astype(F32)


def finish_kernel(scal, *refs):
    (up0, got0, attn0, attn0_got, fixed0) = refs[:5]
    (up1, down1, got1, fixed1) = refs[5:9]
    rows, attn_out, up_out, down_out, vec_out, bias_out = refs[9:]
    piece, share = attn_out.shape[2], attn_out.shape[3]
    half = piece // 2
    tail = slice(piece, 3 * half)
    moves = (
        (0, slice(0, piece), attn0, slice(0, piece), attn0_got, slice(0, piece)),
        (1, slice(0, half), down1, tail, got1, tail),
        (1, slice(half, piece), up1, tail, got1, slice(5 * half, 6 * half)),
    )
    for blk, to, keep, keep_at, got, got_at in moves:
        for m in range(3):
            cols = slice(m * share, (m + 1) * share)
            attn_out[blk, m, to] = keep[0, keep_at, cols].astype(F32) + got[
                0, got_at, cols
            ].astype(F32)
    for blk, keep, got, start, fixed in (
        (0, up0, got0, piece, fixed0),
        (1, up1, got1, 3 * half, fixed1),
    ):
        up_out[blk] = keep[0, 0:piece].astype(F32) + got[0, start : start + piece].astype(F32)
        attn_out[blk, 3] = fixed[:, 4 * share :].astype(F32)
        for k in range(4):
            part = fixed[:, k * share : (k + 1) * share].astype(F32)
            down_out[blk, :, k * piece : (k + 1) * piece] = part.T
        for k in range(10):
            vec_out[k, blk : blk + 1] = rows[10 * blk + k : 10 * blk + k + 1]
        for k in range(4):
            bias_out[blk : blk + 1, k * piece : (k + 1) * piece] = rows[
                20 + 4 * blk + k : 21 + 4 * blk + k
            ]


def body(
    visible,
    masked_queries,
    visible_counts,
    attention_matrices,
    up_projection_weights,
    down_projection_weights,
    vectors,
    up_projection_bias,
    encoder_cotangent,
    cot_regressor,
):
    vis, width = visible.shape[0], visible.shape[2]
    hid = masked_queries.shape[0]
    images = lax.axis_size("img")
    me = lax.axis_index("blk")
    place = lax.axis_index("img")
    pv, pm = round_up(vis, 16), round_up(hid, 16)
    nv, nm = CYCLE * pv, CYCLE * pm
    s = width // CYCLE
    ff = up_projection_weights.shape[2]
    ffb = ff // CYCLE
    natural = images != 8
    vec, upb = jnp.swapaxes(vectors, 0, 1), up_projection_bias
    dma = pltpu.SemaphoreType.DMA

    def pad(rows, to):
        return jnp.pad(rows[:, 0, :], ((0, to - rows.shape[0]), (0, 0)))

    def many(arrays, kind="v"):
        return [(a, kind) for a in arrays]

    scal = jnp.stack([me, visible_counts[0], place]).astype(jnp.int32)
    attn, up0, vec, w_own, b_own = call(
        "prep",
        prep_kernel,
        [(scal, "s"), (attention_matrices, "a"), (up_projection_weights, "a"), (vec, "a")],
        [(attention_matrices.shape, BF), ((width, ff), BF), (vec.shape, F32)]
        + [((2, 3, width, s), BF), ((2, 3, 1, s), F32)],
        [dma((4,))],
        keep=True,
    )

    def load(blk, sources, shapes, after, hold, cut=False):
        return call(
            "load",
            functools.partial(load_kernel, blk, cut),
            [(scal, "s")] + many(sources, "a"),
            [(shape, BF) for shape in shapes],
            [dma((len(sources),))],
            keep=True,
            after=after,
            hold=hold,
        )

    both_projections = [up_projection_weights, down_projection_weights]
    x, mq = pad(visible, pv), pad(masked_queries, pm)
    xs = gather(x, None, b_own)
    cot_e, cot_g = pad(encoder_cotangent, pv), pad(cot_regressor, pm)

    h0, q0, k0, v0, o0 = call(
        "enc_attend",
        functools.partial(enc_attend_kernel, vis),
        [(scal, "s")] + many(xs) + many([w_own, b_own, vec]),
        [((nv, width), BF)] + [((nv, s), BF)] * 4,
        hold=[attn, up0],
    )
    (down0,) = load(0, [down_projection_weights], [(ff, width)], [o0], [attn, up0])
    mixed0 = exchange([o0[j * pv : (j + 1) * pv] for j in range(CYCLE)])
    e, e_b, he, h2_0, y0, r0, z0, gp0 = call(
        "enc_ffn",
        functools.partial(enc_ffn_kernel, vis),
        [(scal, "s")] + many(mixed0) + many([x, vec, upb]) + many([attn, up0, down0], "w"),
        [((pv, width), F32), ((vis, width), BF), ((pv, width), BF), ((pv, width), BF)]
        + [((pv, width), F32)] * 3
        + [((pv, ff), F32)],
        [pltpu.VMEM((pv, width), BF)],
    )

    up1, down1 = load(
        1, both_projections, [(width, ff), (ff, width)], [he], [attn, up0, down0]
    )
    mqs = gather(mq, xs[2], e)
    hm, qm, km, vm = call(
        "mask_project",
        mask_project_kernel,
        many(mqs) + many([w_own, b_own, vec]),
        [((nm, width), BF)] + [((nm, s), BF)] * 3,
        after=[up1],
        hold=[attn, up0, down0, up1, down1],
    )
    hes = gather(he, None, up1)
    h_vis, k1, v1, o1 = call(
        "reg_attend",
        functools.partial(reg_attend_kernel, vis, hid),
        [(scal, "s")] + many(hes) + many([w_own, b_own, qm, km, vm]),
        [((nv, width), BF), ((nv + nm, s), BF), ((nv + nm, s), BF), ((nm, s), BF)],
        hold=[attn, up0, down0, up1, down1],
    )
    mixed1 = exchange([o1[j * pm : (j + 1) * pm] for j in range(CYCLE)])
    g_b, pair1, dr1, dy1, small1, ups1 = call(
        "reg_ffn",
        functools.partial(reg_ffn_kernel, hid),
        [(scal, "s")] + many(mixed1) + many([mq, cot_g, vec, upb]) + many([attn, up1, down1], "w"),
        [((hid, width), BF), ((2 * pm, width), BF), ((pm, width), BF), ((pm, width), F32)]
        + [((8, width), F32), ((1, ff), F32)],
        [pltpu.VMEM((pm, width), BF), pltpu.VMEM((pm, ff), F32)],
        hold=[up0, down0],
    )

    piece = width // images
    m = images // CYCLE
    first_x, first_z = [0, 1, 2], [1, 0, 2]

    def message(rows):
        return [((images // 2, rows, width), BF)] * 2

    def by_owner(mat):
        count = mat.shape[0] // m
        cut = mat.reshape(m, count, CYCLE, s).transpose(2, 0, 1, 3)
        return reduce_whole(cut.reshape(images, count, s))

    def by_rows(mat):
        return reduce_whole(mat.reshape(images, piece, mat.shape[1]))

    ffn_whole = [((ffb, width), BF), ((width, ffb), BF)]
    attn_whole = [((width, 3 * s), BF), ((s, width), BF)]

    half = piece // 2

    def tails(ins, parts):
        (out,) = call(
            "tail",
            functools.partial(tail_kernel, parts),
            [(scal, "s")] + many(ins),
            [((piece, width + s), BF)],
        )
        return transpose_owners(out)

    def ffn_scratch(rows):
        return [pltpu.VMEM((rows, width), BF)] * 2

    up1_cut, down1_cut = load(
        1, both_projections, [(width, ffb), (ffb, width)], [dr1], [attn, up0, down0], True
    )
    dr1s = gather(dr1, None, up1_cut)
    ge, gm, qv1 = call(
        "reg_attend_back",
        functools.partial(reg_attend_back_kernel, vis, hid),
        [(scal, "s")] + many(dr1s) + many([qm, k1, v1]) + [(attn, "w")],
        [((nv, 2 * s), BF), ((nm, 3 * s), BF), ((8, s), F32)],
        [pltpu.VMEM((nm, width), BF)],
        limit=10,
        hold=[up0, down0, up1_cut, down1_cut],
    )
    ges = exchange([ge[j * pv : (j + 1) * pv] for j in range(CYCLE)])
    parts1 = call(
        "reg_attn_grad",
        functools.partial(reg_attn_grad_kernel, (first_x, first_z), natural),
        [(scal, "s")] + many([hm, h_vis, gm, ge, o1] + dr1s + mqs + [w_own]),
        (attn_whole if natural else message(piece + piece // 2) * 2) + [((8, width), F32)],
        [pltpu.VMEM((nm, width), BF)],
        after=[qv1],
        limit=10,
        hold=[attn, up0, down0, up1_cut, down1_cut],
    )
    norm1 = parts1[-1]
    pairs1 = gather(pair1, dr1s[2], norm1)
    buffers = [] if natural else list(parts1[:-1])
    first = 1 + CYCLE + 3
    out = call(
        "reg_ffn_grad",
        functools.partial(reg_ffn_grad_kernel, (first_x, first_z), natural),
        [(scal, "s")]
        + many(pairs1)
        + many([upb])
        + many([up1_cut, down1_cut], "w")
        + many(buffers),
        ffn_whole if natural else message(piece + piece // 2) * 2,
        ffn_scratch(nm),
        after=[norm1],
        limit=10,
        hold=[attn, up0, down0],
        alias=[(first + k, k) for k in range(len(buffers))],
    )
    if natural:
        sums1 = [by_owner(out[0]), by_rows(out[1]), by_rows(parts1[0]), by_owner(parts1[1])]
    else:
        sums1 = [ImgSum(out[0], out[1], first_x), ImgSum(out[2], out[3], first_z)]

    def steps(groups, *after, hold=(attn,)):
        if natural:
            for group in groups:
                for one in group:
                    one.step()
        else:
            step_all(scal, groups, after, hold)

    for one in sums1:
        one.sent = later(one.sent, *ges[1:])
    steps([[one] for one in sums1])
    pair0, dr0, dy0, small0, ups0 = call(
        "enc_ffn_back",
        functools.partial(enc_ffn_back_kernel, vis),
        [(scal, "s")]
        + many(ges)
        + many([e, cot_e, y0, r0, z0, gp0, h2_0, vec])
        + many([attn, up0, down0], "w"),
        [((2 * pv, width), BF), ((pv, width), BF), ((pv, width), F32), ((8, width), F32)]
        + [((1, ff), F32)],
        [pltpu.VMEM((pv, width), BF)] * 2,
        after=[norm1],
    )

    dr0s = gather(dr0)
    out = call(
        "enc_attend_back",
        functools.partial(enc_attend_back_kernel, vis, first_x, natural),
        [(scal, "s")]
        + many(dr0s)
        + many([h0, q0, k0, v0, o0, gm] + xs + [w_own])
        + many([small0, small1, norm1, qv1, ups0, ups1])
        + [(attn, "w")],
        [((CYCLE, pv + pm, 3 * s), BF), ((32, width), F32)]
        + (attn_whole if natural else message(piece + 16)),
        [pltpu.VMEM((nv, width), BF), pltpu.VMEM((8, s), F32), pltpu.VMEM((8, width), F32)],
        after=[small0],
        limit=10,
        hold=[up0, down0],
    )
    g, rows = out[:2]
    if natural:
        attn0, o0_sum = by_rows(out[2]), by_owner(out[3])
    else:
        attn0 = ImgSum(out[2], out[3], first_x)
    steps([[attn0]])
    steps([[one] for one in sums1], rows, hold=(attn, up0, down0))
    pairs0 = gather(pair0, dr0s[2], rows)
    out = call(
        "enc_ffn_grad",
        functools.partial(enc_ffn_grad_kernel, (first_z, first_x), natural),
        [(scal, "s")] + many(pairs0) + many([upb]) + many([up0, down0], "w"),
        ffn_whole if natural else message(piece) * 2,
        ffn_scratch(nv),
        after=[sums1[0].sent],
        hold=[attn],
    )
    if natural:
        ffn0 = [by_owner(out[0]), by_rows(out[1])]
    else:
        ffn0 = [ImgSum(out[0], out[1], first_z), ImgSum(out[2], out[3], first_x)]
    steps([[one] for one in ffn0])
    steps([sums1], out[0])
    steps([[attn0]], sums1[0].sent)
    steps([[one] for one in ffn0 + [attn0]], sums1[0].got)
    g = later(g, ffn0[0].sent)
    gs = exchange([g[j] for j in range(CYCLE)])
    if not natural:
        steps([ffn0], attn0.got)
        got1 = later(sums1[0].got, ffn0[0].sent)
        fixed1 = tails(
            [sums1[0].keep, sums1[1].keep, got1],
            [
                (0, slice(0, piece), 2, slice(0, piece)),
                (0, slice(piece, 3 * half), 2, slice(piece, 3 * half)),
                (1, slice(piece, 3 * half), 2, slice(5 * half, 6 * half)),
            ],
        )
    grad_x, grad_m = call(
        "input_grad",
        input_grad_kernel,
        [(scal, "s")] + many(gs) + many([x, mq, dy0, dy1, vec]) + [(attn, "w")],
        [((vis, 1, width), F32), ((hid, 1, width), F32)],
        [pltpu.VMEM((pv + pm, width), BF)] * 3,
        after=[ffn0[0].sent],
    )

    if natural:

        def owned(sums):
            return transpose_owners(sums.finish().astype(BF)).astype(F32)

        ups, downs, attns = [], [], []
        for down_sum, up_sum, qkv, o_sum in (ffn0 + [attn0, o0_sum], sums1):
            ups.append(up_sum.finish())
            downs.append(owned(down_sum))
            got = qkv.finish()
            attns.append(
                jnp.stack([got[:, :s], got[:, s : 2 * s], got[:, 2 * s :], owned(o_sum)])
            )
        grad_attn, grad_up, grad_down = jnp.stack(attns), jnp.stack(ups), jnp.stack(downs)
        for axis in ("blk", "img"):
            j = 1
            while j < lax.axis_size(axis):
                rows = rows + swap(rows, axis, j)
                j *= 2
        vec_total = lax.dynamic_slice_in_dim(rows[:20], place * piece, piece, 1)
        vec_total = vec_total.reshape(2, 10, piece)
        bias_total = lax.dynamic_slice_in_dim(
            rows[20:28].reshape(2, ff), place * (ff // images), ff // images, 1
        )
    else:
        (rows,) = call(
            "vectors",
            functools.partial(vector_total_kernel, slice(piece, piece + 16)),
            many([attn0.keep, attn0.got]),
            [((32, piece), F32)],
        )
        rows = rows + swap(rows, "blk", 1)
        rows = rows + swap(rows, "blk", 2)
        got0 = later(ffn0[0].got, grad_x)
        fixed0 = tails(
            [ffn0[0].keep, got0, attn0.keep, attn0.got],
            [
                (0, slice(0, piece), 1, slice(0, piece)),
                (2, slice(0, piece), 3, slice(0, piece)),
            ],
        )
        last = [ffn0[1].keep, got0, attn0.keep, attn0.got, fixed0]
        last += [sums1[1].keep, sums1[0].keep, got1, fixed1]
        grad_attn, grad_up, grad_down, vec_total, bias_total = call(
            "finish",
            finish_kernel,
            [(scal, "s")] + many(last + [rows]),
            [
                ((2, 4, piece, s), F32),
                ((2, piece, ffb), F32),
                ((2, s, ff // images), F32),
                ((10, 2, piece), F32),
                ((2, ff // images), F32),
            ],
        )
        grad_down, vec_total = jnp.swapaxes(grad_down, 1, 2), jnp.swapaxes(vec_total, 0, 1)

    return (
        e_b[:, None, :],
        g_b[:, None, :],
        grad_x,
        grad_m,
        grad_attn,
        grad_up,
        grad_down,
        vec_total,
        bias_total,
    )


def solution(mesh):
    rows = P("blk", "img", None)
    in_specs = (rows, rows, P("img"), P(), P(), P(), P(), P(), rows, rows)
    out_specs = (
        rows,
        rows,
        rows,
        rows,
        P(None, None, "img", "blk"),
        P(None, "img", "blk"),
        P(None, "img", "blk"),
        P(None, None, "img"),
        P(None, "img"),
    )
    return jax.shard_map(body, mesh=mesh, in_specs=in_specs, out_specs=out_specs, check_vma=False)
```

```python
import functools

import jax
import jax.numpy as jnp
from jax import lax
from jax.experimental import pallas as pl
from jax.experimental.pallas import tpu as pltpu
from jax.sharding import PartitionSpec as P

HEADS = 12
HEAD = 64
NPATCH = 576
EPS = 1e-06
BF = jnp.bfloat16
F32 = jnp.float32
CYCLE = 4
MIB = 1024 * 1024
COSTS = {'prep': 4.0, 'load': 5.0, 'tail': 1.0, 'pick': 1.3, 'cut': 2.5, 'vectors': 0.5, 'enc_attend': 3.3, 'mask_project': 0.9, 'enc_ffn': 5.9, 'reg_attend': 3.4, 'reg_ffn': 8.2, 'reg_attend_back': 5.7, 'reg_attn_grad': 2.7, 'reg_ffn_grad': 4.5, 'enc_ffn_back': 0.01, 'enc_attend_back': 8.0, 'enc_ffn_grad': 0.01, 'img_step': 0.01, 'input_grad': 7.4, 'finish': 2.6}
COST_SCALE = 0.3


def round_up(value, unit):
    return (value + unit - 1) // unit * unit


def dot(left, right):
    return jnp.dot(left, right, preferred_element_type=F32)


def dot_nt(left, right):
    return lax.dot_general(left, right, (((1,), (1,)), ((), ())), preferred_element_type=F32)


def dot_tn(left, right):
    return lax.dot_general(left, right, (((0,), (0,)), ((), ())), preferred_element_type=F32)


def norm(rows):
    centred = rows - jnp.mean(rows, -1, keepdims=True)
    inverse = lax.rsqrt(jnp.mean(centred * centred, -1, keepdims=True) + EPS)
    return centred * inverse, inverse


def norm_back(grad_out, gain, normed, inverse):
    scaled = grad_out * gain
    return inverse * (
        scaled
        - jnp.mean(scaled, -1, keepdims=True)
        - normed * jnp.mean(scaled * normed, -1, keepdims=True)
    )


def gelu_cdf(u):
    return 0.5 * (1.0 + lax.erf(u * 0.7071067811865476))


def gelu_parts(u):
    cdf = gelu_cdf(u)
    slope = cdf + u * (jnp.exp(u * u * -0.5) * 0.3989422804014327)
    return cdf, slope


def col_sum(rows):
    return jnp.sum(rows, 0, keepdims=True)


def swap(block, axis, offset):
    size = lax.axis_size(axis)
    return lax.ppermute(block, axis, [(i, i ^ offset) for i in range(size)])


def gather(block, first=None, second=None):
    across = swap(block if first is None else later(block, first), "blk", 2)
    if second is not None:
        over, beside = swap(later(across, second), "blk", 1), later(block, second)
    else:
        over, beside = swap(across, "blk", 1), block
    return [block, swap(beside, "blk", 1), across, over]


def later(value, *arrays):
    return lax.optimization_barrier((value, *arrays))[0]


def exchange(blocks, held=None):
    sent = blocks if held is None else held
    across, over = swap(sent[2], "blk", 2), swap(sent[3], "blk", 3)
    return [blocks[0], swap(sent[1], "blk", 1), across, over]


class ImgSum:
    def __init__(self, keep, sent, order):
        self.order = list(order)
        self.keep, self.sent, self.got = keep, sent, None
        self.at = slice(0, keep.shape[1])

    def step(self, *after):
        bit = self.order.pop(0)
        if self.got is not None:
            total = self.total().astype(BF)
            total = total.reshape((2, total.shape[0] // 2) + total.shape[1:])
            mine = (lax.axis_index("img") >> bit) & 1
            self.keep = lax.dynamic_index_in_dim(total, mine, 0, False)
            self.sent = lax.dynamic_index_in_dim(total, 1 - mine, 0, False)
        if after:
            self.sent = later(self.sent, *after)
        self.got = swap(self.sent, "img", 1 << bit)
        return self.sent

    def total(self):
        return self.keep.astype(F32) + self.got[:, self.at].astype(F32)

    def finish(self):
        while self.order:
            self.step()
        return self.total()[0]


def reduce_whole(parts):
    images = parts.shape[0]
    place = lax.axis_index("img")
    bits = images.bit_length() - 1
    pairs = parts.reshape((2, images // 2) + parts.shape[1:])
    mine = place >> (bits - 1)
    keep = lax.dynamic_index_in_dim(pairs, mine, 0, False)
    sent = lax.dynamic_index_in_dim(pairs, 1 - mine, 0, False)
    return ImgSum(keep, sent, range(bits - 1, -1, -1))


def transpose_owners(part):
    images, cycle = lax.axis_size("img"), lax.axis_size("blk")
    m = images // cycle
    pairs = []
    for i in range(images):
        for b in range(cycle):
            pairs.append((i * cycle + b, (b * m + i % m) * cycle + i // m))
    return lax.ppermute(part, ("img", "blk"), pairs)


def call(name, kernel, ins, outs, scratch=(), limit=8, after=(), keep=False, hold=(), alias=()):
    spaces = {"s": pltpu.SMEM, "v": pltpu.VMEM, "w": pltpu.VMEM, "a": pltpu.HBM, "n": pl.ANY}
    places = {"w": pltpu.VMEM, "a": pltpu.HBM}
    count = len(ins)
    ins = ins + [(a, "n") for a in after] + [(a, "w") for a in hold]

    def run(*refs):
        kernel(*refs[:count], *refs[len(ins) :])

    return pl.pallas_call(
        run,
        name=name,
        out_shape=[
            pltpu.VMEM(s, d) if keep else jax.ShapeDtypeStruct(s, d) for s, d in outs
        ],
        in_specs=[pl.BlockSpec(memory_space=spaces[k]) for _, k in ins],
        out_specs=[pl.BlockSpec(memory_space=pltpu.VMEM) for _ in outs],
        scratch_shapes=list(scratch),
        input_output_aliases=dict(alias),
        compiler_params=pltpu.CompilerParams(vmem_limit_bytes=limit * MIB),
        cost_estimate=pl.CostEstimate(
            flops=int(COST_SCALE * COSTS[name] * 1.15e9), bytes_accessed=1, transcendentals=0
        ),
    )(*[pltpu.with_memory_space_constraint(a, places[k]) if k in places else a for a, k in ins])


def step_kernel(bits, starts, groups, scal, *refs):
    count = len(bits)
    ins, keeps, outs = refs[: 2 * count], refs[2 * count : 3 * count], refs[3 * count :]
    for out, group in zip(outs, groups):
        start = 0
        for k in group:
            keep, got = ins[2 * k : 2 * k + 2]
            half, rows = keep.shape[0] // 2, keep.shape[1]
            mine = (scal[2] >> bits[k]) & 1
            sides = []
            for side in (mine, 1 - mine):
                at = pl.ds(side * half, half)
                other = got[at, starts[k] : starts[k] + rows]
                sides.append((keep[at].astype(F32) + other.astype(F32)).astype(BF))
            keeps[k][...] = sides[0]
            out[:, start : start + rows] = sides[1]
            start += rows


def step_all(scal, groups, after=(), hold=()):
    sums = [one for group in groups for one in group]
    if sums[0].got is not None:
        bits = [one.order[0] for one in sums]
        places, ins, keeps, outs = [], [(scal, "s")], [], []
        for group in groups:
            places.append([sums.index(one) for one in group])
            half, rows = group[0].keep.shape[0] // 2, 0
            for one in group:
                ins += [(one.keep, "v"), (one.got, "v")]
                keeps.append(((half,) + one.keep.shape[1:], BF))
                rows += one.keep.shape[1]
            outs.append(((half, rows, one.keep.shape[2]), BF))
        parts = call(
            "img_step",
            functools.partial(step_kernel, bits, [one.at.start for one in sums], places),
            ins,
            keeps + outs,
            after=after,
            hold=hold,
        )
        for k, one in enumerate(sums):
            one.keep = parts[k]
        sent = parts[len(sums) :]
    else:
        sent = [group[0].sent for group in groups]
    for group, message in zip(groups, sent):
        got, start = swap(message, "img", 1 << group[0].order[0]), 0
        for one in group:
            rows = one.keep.shape[1]
            one.order.pop(0)
            one.sent, one.got = message, got
            one.at, start = slice(start, start + rows), start + rows


def load_kernel(blk, scal, *refs):
    sems = refs[-1]
    count = (len(refs) - 1) // 2
    copies = []
    for k, (source, target) in enumerate(zip(refs[:count], refs[count:-1])):
        copies.append(pltpu.make_async_copy(source.at[blk], target, sems.at[k]))
    for copy in copies:
        copy.start()
    for copy in copies:
        copy.wait()


def pick_kernel(blk, scal, upb, up_all, own_out, bias_out):
    step = own_out.shape[1] // 8
    for m in range(CYCLE):

        @pl.when(scal[0] == m)
        def _():
            for i in range(8):
                at = (CYCLE * i + m) * step
                own_out[:, i * step : (i + 1) * step] = up_all[:, at : at + step]
                bias_out[:, i * step : (i + 1) * step] = upb[blk : blk + 1, at : at + step]


def cut_kernel(blk, scal, upb, up_all, up, down, up_out, down_out, own_out, bias_out, sems):
    width = up_out.shape[1]
    mine = pl.ds(pl.multiple_of(scal[0] * width, 128), width)
    copies = [
        pltpu.make_async_copy(up.at[blk, :, mine], up_out, sems.at[0]),
        pltpu.make_async_copy(down.at[blk, mine], down_out, sems.at[1]),
    ]
    for copy in copies:
        copy.start()
    pick_kernel(blk, scal, upb, up_all, own_out, bias_out)
    for copy in copies:
        copy.wait()


def prep_kernel(scal, attn, up, vectors, attn_out, up_out, vec, w_out, b_out, sems):
    me = scal[0]
    share = w_out.shape[3]
    window = share + share % 128
    odd = me & 1
    start = pl.multiple_of(me * share - odd * (share % 128), 128)
    copies = [
        pltpu.make_async_copy(attn.at[blk], attn_out.at[blk], sems.at[blk]) for blk in range(2)
    ]
    copies.append(pltpu.make_async_copy(up.at[0], up_out, sems.at[2]))
    copies.append(pltpu.make_async_copy(vectors, vec, sems.at[3]))
    for copy in copies[::-1]:
        copy.start()
    copies[3].wait()
    for blk in range(2):
        copies[blk].wait()
        for m in range(3):
            for parity in range(2):
                shift = parity * (share % 128)

                @pl.when(odd == parity)
                def _():
                    part = attn_out[blk, m, :, pl.ds(start, window)]
                    w_out[blk, m] = part[:, shift : shift + share]
                    if m == 1:
                        b_out[blk, m] = jnp.zeros((1, share), F32)
                    else:
                        row = vec[2 + m // 2, blk : blk + 1, pl.ds(start, window)]
                        b_out[blk, m] = row[:, shift : shift + share]
    copies[2].wait()


def key_bias(me, rows, padded, limit):
    at = lax.broadcasted_iota(jnp.int32, (padded, 1), 0)
    parts = []
    for j in range(CYCLE):
        live = (at < rows) & (at + (me ^ j) * rows < limit)
        parts.append(jnp.where(live, 0.0, -1e30))
    return jnp.concatenate(parts, 0)


def own_live(me, rows, padded, limit):
    at = lax.broadcasted_iota(jnp.int32, (padded, 1), 0)
    return jnp.where((at < rows) & (at + me * rows < limit), 1.0, 0.0)


def probs_t(keys, queries, bias):
    scores = dot_nt(keys, queries) + bias
    exps = jnp.exp(scores - jnp.max(scores, 0, keepdims=True))
    return exps * (1.0 / jnp.sum(exps, 0, keepdims=True))


def attend_t(q, k, v, bias, out_ref):
    qs = (q.astype(F32) * HEAD**-0.5).astype(BF)
    vt = v.astype(F32).T.astype(BF)
    mixed = []
    for h in range(q.shape[1] // HEAD):
        c = slice(h * HEAD, (h + 1) * HEAD)
        p = probs_t(k[:, c], qs[:, c], bias).astype(BF)
        mixed.append(dot(vt[c], p))
    out_ref[...] = jnp.concatenate(mixed, 0).T.astype(BF)


def attend_back_t(q, k, v, do, bias):
    qs = (q.astype(F32) * HEAD**-0.5).astype(BF)
    kt = (k.astype(F32) * HEAD**-0.5).T.astype(BF)
    dq, dk, dv = [], [], []
    for h in range(q.shape[1] // HEAD):
        c = slice(h * HEAD, (h + 1) * HEAD)
        p = probs_t(k[:, c], qs[:, c], bias)
        dp = dot_nt(v[:, c], do[:, c])
        ds = (p * (dp - jnp.sum(p * dp, 0, keepdims=True))).astype(BF)
        dv.append(dot(p.astype(BF), do[:, c]))
        dk.append(dot(ds, qs[:, c]))
        dq.append(dot(kt[c], ds))
    return (
        jnp.concatenate(dq, 0).T.astype(BF),
        jnp.concatenate(dk, 1).astype(BF),
        jnp.concatenate(dv, 1).astype(BF),
    )


def enc_attend_kernel(vis, scal, x0, x1, x2, x3, w, b, vec, h_out, q_out, k_out, v_out, o_out):
    me, count = scal[0], scal[1]
    padded = h_out.shape[0] // CYCLE
    for j, ref in enumerate((x0, x1, x2, x3)):
        n, _ = norm(ref[0:padded].astype(F32))
        h_out[j * padded : (j + 1) * padded] = (n * vec[0, 0:1] + vec[1, 0:1]).astype(BF)
    h = h_out[...]
    q = (dot(h, w[0, 0]) + b[0, 0]).astype(BF)
    k = dot(h, w[0, 1]).astype(BF)
    v = (dot(h, w[0, 2]) + b[0, 2]).astype(BF)
    q_out[...], k_out[...], v_out[...] = q, k, v
    attend_t(q, k, v, key_bias(me, vis, padded, count), o_out)


def mask_project_kernel(x0, x1, x2, x3, w, b, vec, h_out, q_out, k_out, v_out):
    padded = h_out.shape[0] // CYCLE
    for j, ref in enumerate((x0, x1, x2, x3)):
        n, _ = norm(ref[x0.shape[0] - padded :].astype(F32))
        h_out[j * padded : (j + 1) * padded] = (n * vec[0, 1:2] + vec[1, 1:2]).astype(BF)
    h = h_out[...]
    q_out[...] = (dot(h, w[1, 0]) + b[1, 0]).astype(BF)
    k_out[...] = dot(h, w[1, 1]).astype(BF)
    v_out[...] = (dot(h, w[1, 2]) + b[1, 2]).astype(BF)


def reg_attend_kernel(
    vis, hid, scal, x0, x1, x2, x3, w, b, qm, km, vm, h_out, k_out, v_out, o_out
):
    me, count = scal[0], scal[1]
    padded = x0.shape[0]
    nv = CYCLE * padded
    for j, ref in enumerate((x0, x1, x2, x3)):
        h_out[j * padded : (j + 1) * padded] = ref[...]
    h = h_out[...]
    k_out[0:nv] = dot(h, w[1, 1]).astype(BF)
    v_out[0:nv] = (dot(h, w[1, 2]) + b[1, 2]).astype(BF)
    k_out[nv:] = km[...]
    v_out[nv:] = vm[...]
    bias = jnp.concatenate(
        [
            key_bias(me, vis, padded, count),
            key_bias(me, hid, qm.shape[0] // CYCLE, NPATCH - count),
        ],
        0,
    )
    attend_t(qm[...], k_out[...], v_out[...], bias, o_out)


def assemble(me, blocks, scratch, lane):
    share = blocks[0].shape[1] if lane is None else lane[1]
    rows = scratch.shape[0]
    for m in range(CYCLE):

        @pl.when(me == m)
        def _():
            for j, ref in enumerate(blocks):
                at = (m ^ j) * share
                value = ref[...] if lane is None else ref[0:rows, lane[0] : lane[0] + share]
                scratch[:, at : at + share] = value


def ffn_forward(blk, rows, mixed, vec, upb, attn, up, down, gp):
    r = dot(mixed, attn[blk, 3]) + vec[4, blk : blk + 1]
    y = rows + vec[5, blk : blk + 1] * r
    n, _ = norm(y)
    h2 = (n * vec[6, blk : blk + 1] + vec[7, blk : blk + 1]).astype(BF)
    width = up.shape[0]
    z = vec[8, blk : blk + 1]
    for c in range(up.shape[1] // width):
        cols = slice(c * width, (c + 1) * width)
        u = dot(h2, up[:, cols]) + upb[blk : blk + 1, cols]
        cdf, slope = gelu_parts(u)
        gp[:, cols] = slope
        a = (u * cdf).astype(BF)
        z = z + dot(a, down[cols, :])
    return r, y, h2, z


def ffn_backward(blk, grad, r, y, z, vec, up, down, gp, up_sum):
    n, inverse = norm(y)
    scale2 = col_sum(grad * z)
    dz = (grad * vec[9, blk : blk + 1]).astype(BF)
    width = up.shape[0]
    dh2 = 0.0
    for c in range(up.shape[1] // width):
        cols = slice(c * width, (c + 1) * width)
        da = dot_nt(dz, down[cols, :])
        du = (gp[:, cols] * da).astype(BF)
        up_sum[:, cols] = col_sum(du.astype(F32))
        dh2 = dh2 + dot_nt(du, up[:, cols])
    dy = grad + norm_back(dh2, vec[6, blk : blk + 1], n, inverse)
    dr = (dy * vec[5, blk : blk + 1]).astype(BF)
    small = [
        scale2,
        col_sum(dh2 * n),
        col_sum(dh2),
        col_sum(dy * r),
        col_sum(dz.astype(F32)),
        col_sum(dr.astype(F32)),
    ]
    return dz, dy, dr, small


def enc_ffn_kernel(
    vis, scal, o0, o1, o2, o3, x, vec, upb, attn, up, down,
    e_out, eb_out, he_out, h2_out, y_out, r_out, z_out, gp_out,
    mixed,
):
    me, count = scal[0], scal[1]
    assemble(me, (o0, o1, o2, o3), mixed, None)
    r, y, h2, z = ffn_forward(
        0, x[0 : he_out.shape[0]].astype(F32), mixed[...], vec, upb, attn, up, down, gp_out
    )
    h2_out[...], y_out[...], r_out[...], z_out[...] = h2, y, r, z
    e = (y + vec[9, 0:1] * z) * own_live(me, vis, he_out.shape[0], count)
    e_out[...] = e
    eb_out[...] = e[0 : eb_out.shape[0]].astype(BF)
    n, _ = norm(e)
    he_out[...] = (n * vec[0, 1:2] + vec[1, 1:2]).astype(BF)


def reg_ffn_kernel(
    hid, scal, o0, o1, o2, o3, x, cot, vec, upb, attn, up, down,
    gb_out, pair_out, dr_out, dy_out, small_out, up_sum,
    mixed, gp,
):
    me, count = scal[0], scal[1]
    assemble(me, (o0, o1, o2, o3), mixed, None)
    r, y, h2, z = ffn_forward(
        1, x[x.shape[0] - dr_out.shape[0] :].astype(F32), mixed[...], vec, upb, attn, up, down, gp
    )
    padded = dr_out.shape[0]
    live = own_live(me, hid, padded, NPATCH - count)
    g = (y + vec[9, 1:2] * z) * live
    gb_out[...] = g[0 : gb_out.shape[0]].astype(BF)
    grad = cot[...].astype(F32) * live
    dz, dy, dr, small = ffn_backward(1, grad, r, y, z, vec, up, down, gp, up_sum)
    pair_out[0:padded] = h2
    pair_out[padded:] = dz
    dr_out[...] = dr
    dy_out[...] = dy
    for i, row in enumerate(small):
        small_out[i : i + 1] = row
    small_out[6:8] = jnp.zeros((2, small_out.shape[1]), F32)


def enc_ffn_back_kernel(
    vis, scal, g0, g1, g2, g3, e, cot, y, r, z, gp, h2, vec, attn, up, down,
    pair_out, dr_out, dy_out, small_out, up_sum,
    dk, dv,
):
    me, count = scal[0], scal[1]
    share = g0.shape[1] // 2
    assemble(me, (g0, g1, g2, g3), dk, (0, share))
    assemble(me, (g0, g1, g2, g3), dv, (share, share))
    n, inverse = norm(e[...])
    dh = dot_nt(dk[...], attn[1, 1]) + dot_nt(dv[...], attn[1, 2])
    grad_e = norm_back(dh, vec[0, 1:2], n, inverse)
    grad = (cot[...].astype(F32) + grad_e) * own_live(me, vis, cot.shape[0], count)
    dz, dy, dr, small = ffn_backward(
        0, grad, r[...], y[...], z[...], vec, up, down, gp, up_sum
    )
    pair_out[0 : dz.shape[0]] = h2[...]
    pair_out[dz.shape[0] :] = dz
    dy_out[...], dr_out[...] = dy, dr
    for i, row in enumerate(small + [col_sum(dh * n), col_sum(dh)]):
        small_out[i : i + 1] = row


def spread(place_of, keep, sent, place, order, rows, cols):
    first, second, third = order
    for i in range(8):
        t = 2 * ((i >> second) & 1) + ((i >> third) & 1)
        value = place_of(i)

        for side in range(2):
            target = keep if side == ((i >> first) & 1) else sent

            @pl.when(((place >> first) & 1) == side)
            def _():
                target[t, rows, cols] = value


def owner_piece(mat, i, share, parts):
    quarter, half = i >> 1, i & 1
    rows = mat.shape[0] // 2
    part = mat[half * rows : (half + 1) * rows, quarter * share : (quarter + 1) * share]
    rows = rows // parts
    return jnp.concatenate([part[k * rows : (k + 1) * rows] for k in range(parts)], 1)


def attn_pieces(h, dqkv, o, dr):
    share = dqkv[0].shape[1]
    results = [dot_tn(h, grad).astype(BF) for grad in dqkv]
    d_o = dot_tn(o, dr).astype(BF)
    step = h.shape[1] // 8

    def piece(i):
        parts = [result[i * step : (i + 1) * step] for result in results]
        return jnp.concatenate(parts + [owner_piece(d_o, i, share, 1)], 1)

    return results, d_o, piece


def norm_sums(rows, dqkv, w):
    dh = 0.0
    for m, grad in enumerate(dqkv):
        dh = dh + dot_nt(grad, w[m])
    n, _ = norm(rows.astype(F32))
    return col_sum(dh * n), col_sum(dh)


def store_attn(results, d_o, nats):
    share = d_o.shape[0]
    for m, result in enumerate(results):
        nats[0][:, m * share : (m + 1) * share] = result
    nats[1][...] = d_o


def reg_attend_back_kernel(
    vis, hid, scal, d0, d1, d2, d3, q, k, v, attn,
    e_out, m_out, qv_out,
    dr,
):
    me, count = scal[0], scal[1]
    share = q.shape[1]
    padded = d0.shape[0]
    for j, ref in enumerate((d0, d1, d2, d3)):
        dr[j * padded : (j + 1) * padded] = ref[...]
    do = dot_nt(dr[...], attn[1, 3, pl.ds(pl.multiple_of(me * share, 16), share), :]).astype(BF)
    nm = CYCLE * padded
    nv = k.shape[0] - nm
    bias = jnp.concatenate(
        [
            key_bias(me, vis, nv // CYCLE, count),
            key_bias(me, hid, padded, NPATCH - count),
        ],
        0,
    )
    dq, dk, dv = attend_back_t(q[...], k[...], v[...], do, bias)
    e_out[:, 0:share] = dk[0:nv]
    e_out[:, share:] = dv[0:nv]
    m_out[:, 0:share] = dq
    m_out[:, share : 2 * share] = dk[nv:]
    m_out[:, 2 * share :] = dv[nv:]
    qv_out[0:1] = col_sum(dq.astype(F32))
    qv_out[1:2] = col_sum(dv.astype(F32))
    qv_out[2:8] = jnp.zeros((6, share), F32)


def enc_attend_back_kernel(
    vis, order, natural, scal, d0, d1, d2, d3, h, q, k, v, o, gm, x0, x1, x2, x3, w,
    small0, small1, norm1, qv1, ups0, ups1, attn,
    g_out, vec_out, first, second, dr, qv0, norm0,
):
    me, count = scal[0], scal[1]
    share = q.shape[1]
    padded = d0.shape[0]
    for j, ref in enumerate((d0, d1, d2, d3)):
        dr[j * padded : (j + 1) * padded] = ref[...]
    do = dot_nt(dr[...], attn[0, 3, pl.ds(pl.multiple_of(me * share, 16), share), :]).astype(BF)
    dq, dk, dv = attend_back_t(
        q[...], k[...], v[...], do, key_bias(me, vis, padded, count)
    )
    for j in range(CYCLE):
        at = slice(j * padded, (j + 1) * padded)
        for m, grad in enumerate((dq, dk, dv)):
            g_out[j, 0:padded, m * share : (m + 1) * share] = grad[at]
        more = g_out.shape[1] - padded
        g_out[j, padded:] = gm[j * more : (j + 1) * more]
    qv0[0:1] = col_sum(dq.astype(F32))
    qv0[1:2] = col_sum(dv.astype(F32))
    x = jnp.concatenate([ref[0:padded] for ref in (x0, x1, x2, x3)], 0)
    norm0[0:1], norm0[1:2] = norm_sums(x, (dq, dk, dv), (w[0, 0], w[0, 1], w[0, 2]))
    vector_rows(
        natural, me, (small0, small1), (norm0, norm1), (qv0, qv1), (ups0, ups1), vec_out
    )
    results, d_o, piece = attn_pieces(h[...], (dq, dk, dv), o[...], dr[...])
    if natural:
        store_attn(results, d_o, (first, second))
        return
    step, cols = h.shape[1] // 8, slice(0, 4 * share)

    def vector_piece(i):
        mine = slice(i * step, (i + 1) * step)
        parts = [vec_out[0:16, mine], vec_out[16:32, mine]]
        parts.append(jnp.zeros((16, 4 * share - 2 * step), F32))
        return jnp.concatenate(parts, 1).astype(BF)

    spread(piece, first, second, scal[2], order, slice(0, step), cols)
    spread(vector_piece, first, second, scal[2], order, slice(step, step + 16), cols)


def ffn_pieces(blk, scal, pairs, upb, up, down, h2, dz, own=None, bias=None):
    me = scal[0]
    width = up.shape[0]
    cols = pl.ds(pl.multiple_of(me * width, 128), width)
    padded = pairs[0].shape[0] // 2
    for j, pair in enumerate(pairs):
        at = slice(j * padded, (j + 1) * padded)
        h2[at] = pair[0:padded]
        dz[at] = pair[padded:]
    whole = pl.ds(0, width) if up.shape[1] == width else cols
    u = dot(h2[...], up[:, whole]) + upb[blk : blk + 1, cols]
    cdf, slope = gelu_parts(u)
    du = (slope * dot_nt(dz[...], down[whole, :])).astype(BF)
    if own is not None:
        u = dot(h2[...], own[...]) + bias[...]
        cdf = gelu_cdf(u)
    a = (u * cdf).astype(BF)
    d_down = dot_tn(a, dz[...]).astype(BF)
    d_up = dot_tn(h2[...], du).astype(BF)
    step = width // 8
    return (
        d_down,
        d_up,
        lambda i: (
            d_down[i * step : (i + 1) * step]
            if own is not None
            else owner_piece(d_down, i, width // 4, 4)
        ),
        lambda i: d_up[i * step : (i + 1) * step],
    )


def vector_rows(natural, me, smalls, norms, qvs, ups, out):
    share, width = qvs[0].shape[1], out.shape[1]
    step = width // 8
    out[...] = jnp.zeros(out.shape, F32)
    for blk, (small, qv, up_sum) in enumerate(zip(smalls, qvs, ups)):
        at = 10 * blk
        gain, bias = norms[blk][0:1], norms[blk][1:2]
        if blk == 1:
            gain, bias = gain + smalls[0][6:7], bias + smalls[0][7:8]
        scale2, gain2, bias2, scale1, dzs, drs = [small[i : i + 1] for i in range(6)]
        rows = {0: gain, 1: bias, 4: drs, 5: scale1, 6: gain2, 7: bias2, 8: dzs, 9: scale2}
        for i, row in rows.items():
            out[at + i : at + i + 1] = row
        first = 20 + 4 * blk
        for k in range(4):
            if natural:
                out[first + k : first + k + 1] = up_sum[0:1, k * width : (k + 1) * width]
            else:
                parts = [
                    up_sum[0:1, (4 * i + k) * step : (4 * i + k + 1) * step] for i in range(8)
                ]
                out[first + k : first + k + 1] = jnp.concatenate(parts, 1)
        for m in range(CYCLE):

            @pl.when(me == m)
            def _():
                cols = slice(m * share, (m + 1) * share)
                out[at + 2 : at + 3, cols] = qv[0:1]
                out[at + 3 : at + 4, cols] = qv[1:2]


def enc_ffn_grad_kernel(
    orders, natural, scal, p0, p1, p2, p3, upb, own, bias, up, down, *refs
):
    outs, scratch = refs[:-2], refs[-2:]
    d_down, d_up, down_piece, up_piece = ffn_pieces(
        0, scal, (p0, p1, p2, p3), upb, up, down, *scratch, *(() if natural else (own, bias))
    )
    if natural:
        outs[0][...], outs[1][...] = d_down, d_up
        return
    here, cols = slice(0, d_up.shape[0] // 8), slice(0, d_up.shape[1])
    spread(down_piece, outs[0], outs[1], scal[2], orders[0], here, cols)
    spread(up_piece, outs[2], outs[3], scal[2], orders[1], here, cols)


def reg_attn_grad_kernel(
    orders, natural, scal, h_m, h_e, g_m, g_e, o, d0, d1, d2, d3, x0, x1, x2, x3, w, *refs
):
    outs, norm_out, dr = refs[:-2], refs[-2], refs[-1]
    share = g_e.shape[1] // 2
    padded = d0.shape[0]
    for j, ref in enumerate((d0, d1, d2, d3)):
        dr[j * padded : (j + 1) * padded] = ref[...]
    x = jnp.concatenate([ref[ref.shape[0] - padded :] for ref in (x0, x1, x2, x3)], 0)
    dqkv_m = [g_m[:, m * share : (m + 1) * share] for m in range(3)]
    norm_out[0:1], norm_out[1:2] = norm_sums(x, dqkv_m, (w[1, 0], w[1, 1], w[1, 2]))
    norm_out[2:8] = jnp.zeros((6, norm_out.shape[1]), F32)
    h = jnp.concatenate([h_e[...], h_m[...]], 0)
    none = jnp.zeros((h_e.shape[0], share), BF)
    grads = []
    for m in range(3):
        top = none if m == 0 else g_e[:, (m - 1) * share : m * share]
        grads.append(jnp.concatenate([top, dqkv_m[m]], 0))
    results, d_o, attn_piece = attn_pieces(h, grads, o[...], dr[...])
    if natural:
        store_attn(results, d_o, outs)
        return
    step, cols = h.shape[1] // 8, slice(0, h.shape[1])
    half = step // 2
    for k in range(2):
        spread(
            lambda i: attn_piece(i)[k * half : (k + 1) * half], outs[2 * k], outs[2 * k + 1],
            scal[2], orders[k], slice(step, step + half), cols,
        )


def reg_ffn_grad_kernel(
    orders, natural, scal, p0, p1, p2, p3, upb, own, bias, up, down, *refs
):
    outs, scratch = refs[-6:-2] if not natural else refs[-4:-2], refs[-2:]
    d_down, d_up, down_piece, up_piece = ffn_pieces(
        1, scal, (p0, p1, p2, p3), upb, up, down, *scratch, *(() if natural else (own, bias))
    )
    if natural:
        outs[0][...], outs[1][...] = d_down, d_up
        return
    step, cols = d_up.shape[0] // 8, slice(0, d_up.shape[1])
    for k, piece in enumerate((down_piece, up_piece)):
        spread(piece, outs[2 * k], outs[2 * k + 1], scal[2], orders[k], slice(0, step), cols)


def input_grad_kernel(
    scal, g0, g1, g2, g3, x, mq, dy0, dy1, vec, attn, out0, out1, dq, dk, dv
):
    share = g0.shape[1] // 3
    grads = (dq, dk, dv)
    for m, ref in enumerate(grads):
        assemble(scal[0], (g0, g1, g2, g3), ref, (m * share, share))
    first = dy0.shape[0]
    rows = (slice(0, first), slice(first, g0.shape[0]))
    for blk, (at, own, dy, out) in enumerate(
        ((rows[0], x, dy0, out0), (rows[1], mq, dy1, out1))
    ):
        n, inverse = norm(own[...].astype(F32))
        dh = 0.0
        for m, ref in enumerate(grads):
            dh = dh + dot_nt(ref[at], attn[blk, m])
        dx = norm_back(dh, vec[0, blk : blk + 1], n, inverse) + dy[...]
        out[:, 0, :] = dx[0 : out.shape[0]]


def tail_kernel(parts, scal, *refs):
    count = max(part[2] for part in parts) + 1
    ins, downs, o_out = refs[:count], refs[count : count + CYCLE], refs[count + CYCLE :]

    def total(part, cols):
        keep, at, got, got_at = part
        return ins[keep][0, at, cols].astype(F32) + ins[got][0, got_at, cols].astype(F32)

    share = downs[0].shape[1]
    for m in range(CYCLE):

        @pl.when(scal[0] == m)
        def _():
            for j, ref in enumerate(downs):
                at = (m ^ j) * share
                ref[...] = total(parts[0], slice(at, at + share)).astype(BF)

    start = 0
    for part in parts[1:]:
        at = slice(start, start + part[1].stop - part[1].start)
        o_out[0][at] = total(part, slice(3 * share, 4 * share)).astype(BF)
        start = at.stop


def vector_total_kernel(at, keep, got, out, o_out):
    step = out.shape[1]
    for k in range(2):
        cols = slice(k * step, (k + 1) * step)
        out[16 * k : 16 * k + 16] = keep[0, at, cols].astype(F32) + got[0, at, cols].astype(F32)
    rows, cols = slice(0, o_out.shape[0]), slice(3 * o_out.shape[1], 4 * o_out.shape[1])
    o_out[...] = (keep[0, rows, cols].astype(F32) + got[0, rows, cols].astype(F32)).astype(BF)


def finish_kernel(scal, *refs):
    (up0, attn0, attn0_got, got0, o0), downs0 = refs[:5], refs[5 : 5 + CYCLE]
    refs = refs[5 + CYCLE :]
    (up1, down1, got1, o1), downs1 = refs[:4], refs[4 : 4 + CYCLE]
    rows, attn_out, up_out, down_out, vec_out, bias_out = refs[4 + CYCLE :]
    piece, share = attn_out.shape[2], attn_out.shape[3]
    half = piece // 2
    tail = slice(piece, 3 * half)
    moves = (
        (0, slice(0, piece), attn0, slice(0, piece), attn0_got, slice(0, piece)),
        (1, slice(0, half), down1, tail, got1, tail),
        (1, slice(half, piece), up1, tail, got1, slice(5 * half, 6 * half)),
    )
    for blk, to, keep, keep_at, got, got_at in moves:
        for m in range(3):
            cols = slice(m * share, (m + 1) * share)
            attn_out[blk, m, to] = keep[0, keep_at, cols].astype(F32) + got[
                0, got_at, cols
            ].astype(F32)
    for blk, o, downs in ((0, o0, downs0), (1, o1, downs1)):
        attn_out[blk, 3] = o[...].astype(F32)
        for m in range(CYCLE):

            @pl.when(scal[0] == m)
            def _():
                for j, ref in enumerate(downs):
                    at = (m ^ j) * piece
                    down_out[blk, :, at : at + piece] = ref[...].astype(F32).T

    for blk, keep, got, start in ((0, up0, got0, piece), (1, up1, got1, 3 * half)):
        up_out[blk] = keep[0, 0:piece].astype(F32) + got[0, start : start + piece].astype(F32)
        for k in range(10):
            vec_out[k, blk : blk + 1] = rows[10 * blk + k : 10 * blk + k + 1]
        for k in range(4):
            bias_out[blk : blk + 1, k * piece : (k + 1) * piece] = rows[
                20 + 4 * blk + k : 21 + 4 * blk + k
            ]


def body(
    visible,
    masked_queries,
    visible_counts,
    attention_matrices,
    up_projection_weights,
    down_projection_weights,
    vectors,
    up_projection_bias,
    encoder_cotangent,
    cot_regressor,
):
    vis, width = visible.shape[0], visible.shape[2]
    hid = masked_queries.shape[0]
    images = lax.axis_size("img")
    me = lax.axis_index("blk")
    place = lax.axis_index("img")
    pv, pm = round_up(vis, 16), round_up(hid, 16)
    nv, nm = CYCLE * pv, CYCLE * pm
    s = width // CYCLE
    ff = up_projection_weights.shape[2]
    ffb = ff // CYCLE
    natural = images != 8
    vec, upb = jnp.swapaxes(vectors, 0, 1), up_projection_bias
    dma = pltpu.SemaphoreType.DMA

    def pad(rows, to):
        return jnp.pad(rows[:, 0, :], ((0, to - rows.shape[0]), (0, 0)))

    def many(arrays, kind="v"):
        return [(a, kind) for a in arrays]

    scal = jnp.stack([me, visible_counts[0], place]).astype(jnp.int32)
    attn, up0, vec, w_own, b_own = call(
        "prep",
        prep_kernel,
        [(scal, "s"), (attention_matrices, "a"), (up_projection_weights, "a"), (vec, "a")],
        [(attention_matrices.shape, BF), ((width, ff), BF), (vec.shape, F32)]
        + [((2, 3, width, s), BF), ((2, 3, 1, s), F32)],
        [dma((4,))],
        keep=True,
    )

    def load(blk, sources, shapes, after, hold):
        return call(
            "load",
            functools.partial(load_kernel, blk),
            [(scal, "s")] + many(sources, "a"),
            [(shape, BF) for shape in shapes],
            [dma((len(sources),))],
            keep=True,
            after=after,
            hold=hold,
        )

    both_projections = [up_projection_weights, down_projection_weights]
    x, mq = pad(visible, pv), pad(masked_queries, pm)
    xs = gather(x, None, b_own)
    cot_e, cot_g = pad(encoder_cotangent, pv), pad(cot_regressor, pm)

    h0, q0, k0, v0, o0 = call(
        "enc_attend",
        functools.partial(enc_attend_kernel, vis),
        [(scal, "s")] + many(xs) + many([w_own, b_own, vec]),
        [((nv, width), BF)] + [((nv, s), BF)] * 4,
        hold=[attn, up0],
    )
    (down0,) = load(0, [down_projection_weights], [(ff, width)], [o0], [attn, up0])
    mixed0 = exchange([o0[j * pv : (j + 1) * pv] for j in range(CYCLE)])
    e, e_b, he, h2_0, y0, r0, z0, gp0 = call(
        "enc_ffn",
        functools.partial(enc_ffn_kernel, vis),
        [(scal, "s")] + many(mixed0) + many([x, vec, upb]) + many([attn, up0, down0], "w"),
        [((pv, width), F32), ((vis, width), BF), ((pv, width), BF), ((pv, width), BF)]
        + [((pv, width), F32)] * 3
        + [((pv, ff), F32)],
        [pltpu.VMEM((pv, width), BF)],
    )

    up1, down1 = load(
        1, both_projections, [(width, ff), (ff, width)], [he], [attn, up0, down0]
    )
    mqs = gather(mq, xs[2], e)
    hm, qm, km, vm = call(
        "mask_project",
        mask_project_kernel,
        many(mqs) + many([w_own, b_own, vec]),
        [((nm, width), BF)] + [((nm, s), BF)] * 3,
        after=[up1],
        hold=[attn, up0, down0, up1, down1],
    )
    hes = gather(he, None, up1)
    h_vis, k1, v1, o1 = call(
        "reg_attend",
        functools.partial(reg_attend_kernel, vis, hid),
        [(scal, "s")] + many(hes) + many([w_own, b_own, qm, km, vm]),
        [((nv, width), BF), ((nv + nm, s), BF), ((nv + nm, s), BF), ((nm, s), BF)],
        hold=[attn, up0, down0, up1, down1],
    )
    mixed1 = exchange([o1[j * pm : (j + 1) * pm] for j in range(CYCLE)])
    g_b, pair1, dr1, dy1, small1, ups1 = call(
        "reg_ffn",
        functools.partial(reg_ffn_kernel, hid),
        [(scal, "s")] + many(mixed1) + many([mq, cot_g, vec, upb]) + many([attn, up1, down1], "w"),
        [((hid, width), BF), ((2 * pm, width), BF), ((pm, width), BF), ((pm, width), F32)]
        + [((8, width), F32), ((1, ff), F32)],
        [pltpu.VMEM((pm, width), BF), pltpu.VMEM((pm, ff), F32)],
        hold=[up0, down0],
    )

    piece = width // images
    m = images // CYCLE
    first_x, first_z = [0, 1, 2], [1, 0, 2]

    def message(rows):
        return [((images // 2, rows, width), BF)] * 2

    def by_owner(mat):
        count = mat.shape[0] // m
        cut = mat.reshape(m, count, CYCLE, s).transpose(2, 0, 1, 3)
        return reduce_whole(cut.reshape(images, count, s))

    def by_rows(mat):
        return reduce_whole(mat.reshape(images, piece, mat.shape[1]))

    ffn_whole = [((ffb, width), BF), ((width, ffb), BF)]
    attn_whole = [((width, 3 * s), BF), ((s, width), BF)]

    half = piece // 2

    def ffn_scratch(rows):
        return [pltpu.VMEM((rows, width), BF)] * 2

    up1_cut, down1_cut, own1, bias1 = call(
        "cut",
        functools.partial(cut_kernel, 1),
        [(scal, "s"), (upb, "v"), (up1, "w")] + many(both_projections, "a"),
        [((width, ffb), BF), ((ffb, width), BF), ((width, ffb), BF), ((1, ffb), F32)],
        [dma((2,))],
        keep=True,
        after=[dr1],
        hold=[attn, up0, down0],
    )
    dr1s = gather(dr1, None, up1_cut)
    ge, gm, qv1 = call(
        "reg_attend_back",
        functools.partial(reg_attend_back_kernel, vis, hid),
        [(scal, "s")] + many(dr1s) + many([qm, k1, v1]) + [(attn, "w")],
        [((nv, 2 * s), BF), ((nm, 3 * s), BF), ((8, s), F32)],
        [pltpu.VMEM((nm, width), BF)],
        limit=10,
        hold=[up0, down0, up1_cut, down1_cut],
    )
    ges = exchange([ge[j * pv : (j + 1) * pv] for j in range(CYCLE)])
    parts1 = call(
        "reg_attn_grad",
        functools.partial(reg_attn_grad_kernel, (first_x, first_z), natural),
        [(scal, "s")] + many([hm, h_vis, gm, ge, o1] + dr1s + mqs + [w_own]),
        (attn_whole if natural else message(piece + piece // 2) * 2) + [((8, width), F32)],
        [pltpu.VMEM((nm, width), BF)],
        after=[qv1],
        limit=10,
        hold=[attn, up0, down0, up1_cut, down1_cut],
    )
    norm1 = parts1[-1]
    pairs1 = gather(pair1, dr1s[2], norm1)
    buffers = [] if natural else list(parts1[:-1])
    first = 1 + CYCLE + 5
    out = call(
        "reg_ffn_grad",
        functools.partial(reg_ffn_grad_kernel, (first_x, first_z), natural),
        [(scal, "s")]
        + many(pairs1)
        + many([upb, own1, bias1])
        + many([up1_cut, down1_cut], "w")
        + many(buffers),
        ffn_whole if natural else message(piece + piece // 2) * 2,
        ffn_scratch(nm),
        after=[norm1],
        limit=10,
        hold=[attn, up0, down0],
        alias=[(first + k, k) for k in range(len(buffers))],
    )
    if natural:
        sums1 = [by_owner(out[0]), by_rows(out[1]), by_rows(parts1[0]), by_owner(parts1[1])]
    else:
        sums1 = [ImgSum(out[0], out[1], first_x), ImgSum(out[2], out[3], first_z)]

    def steps(groups, *after, hold=(attn,)):
        if natural:
            for group in groups:
                for one in group:
                    one.step()
        else:
            step_all(scal, groups, after, hold)

    for one in sums1:
        one.sent = later(one.sent, *ges[1:])
    steps([[one] for one in sums1])
    pair0, dr0, dy0, small0, ups0 = call(
        "enc_ffn_back",
        functools.partial(enc_ffn_back_kernel, vis),
        [(scal, "s")]
        + many(ges)
        + many([e, cot_e, y0, r0, z0, gp0, h2_0, vec])
        + many([attn, up0, down0], "w"),
        [((2 * pv, width), BF), ((pv, width), BF), ((pv, width), F32), ((8, width), F32)]
        + [((1, ff), F32)],
        [pltpu.VMEM((pv, width), BF)] * 2,
        after=[norm1],
    )

    own0, bias0 = call(
        "pick",
        functools.partial(pick_kernel, 0),
        [(scal, "s"), (upb, "v"), (up0, "w")],
        [((width, ffb), BF), ((1, ffb), F32)],
        after=[dr0],
        hold=[attn, down0],
    )
    dr0s = gather(dr0, None, own0)
    out = call(
        "enc_attend_back",
        functools.partial(enc_attend_back_kernel, vis, first_x, natural),
        [(scal, "s")]
        + many(dr0s)
        + many([h0, q0, k0, v0, o0, gm] + xs + [w_own])
        + many([small0, small1, norm1, qv1, ups0, ups1])
        + [(attn, "w")],
        [((CYCLE, pv + pm, 3 * s), BF), ((32, width), F32)]
        + (attn_whole if natural else message(piece + 16)),
        [pltpu.VMEM((nv, width), BF), pltpu.VMEM((8, s), F32), pltpu.VMEM((8, width), F32)],
        after=[small0],
        limit=10,
        hold=[up0, down0],
    )
    g, rows = out[:2]
    if natural:
        attn0, o0_sum = by_rows(out[2]), by_owner(out[3])
    else:
        attn0 = ImgSum(out[2], out[3], first_x)
    steps([[attn0]])
    steps([[one] for one in sums1], rows, hold=(attn, up0, down0))
    pairs0 = gather(pair0, dr0s[2], rows)
    out = call(
        "enc_ffn_grad",
        functools.partial(enc_ffn_grad_kernel, (first_z, first_x), natural),
        [(scal, "s")] + many(pairs0) + many([upb, own0, bias0]) + many([up0, down0], "w"),
        ffn_whole if natural else message(piece) * 2,
        ffn_scratch(nv),
        after=[sums1[0].sent],
        hold=[attn],
    )
    if natural:
        ffn0 = [by_owner(out[0]), by_rows(out[1])]
    else:
        ffn0 = [ImgSum(out[0], out[1], first_z), ImgSum(out[2], out[3], first_x)]
    steps([[one] for one in ffn0])
    steps([sums1], out[0])
    steps([[attn0]], sums1[0].sent)
    steps([[one] for one in ffn0 + [attn0]], sums1[0].got)
    g = later(g, ffn0[0].sent)
    gs = exchange([g[j] for j in range(CYCLE)])
    if not natural:
        steps([ffn0], attn0.got)
        got1 = later(sums1[0].got, ffn0[0].sent)
        parts1 = [
            (0, slice(0, piece), 2, slice(0, piece)),
            (0, slice(piece, 3 * half), 2, slice(piece, 3 * half)),
            (1, slice(piece, 3 * half), 2, slice(5 * half, 6 * half)),
        ]
        *downs1, o1_own = call(
            "tail",
            functools.partial(tail_kernel, parts1),
            [(scal, "s")] + many([sums1[0].keep, sums1[1].keep, got1]),
            [((piece, s), BF)] * (CYCLE + 1),
        )
        downs1, o1_own = exchange(downs1), transpose_owners(o1_own)

    grad_x, grad_m = call(
        "input_grad",
        input_grad_kernel,
        [(scal, "s")] + many(gs) + many([x, mq, dy0, dy1, vec]) + [(attn, "w")],
        [((vis, 1, width), F32), ((hid, 1, width), F32)],
        [pltpu.VMEM((pv + pm, width), BF)] * 3,
        after=[ffn0[0].sent],
    )

    if natural:

        def owned(sums):
            return transpose_owners(sums.finish().astype(BF)).astype(F32)

        ups, downs, attns = [], [], []
        for down_sum, up_sum, qkv, o_sum in (ffn0 + [attn0, o0_sum], sums1):
            ups.append(up_sum.finish())
            downs.append(owned(down_sum))
            got = qkv.finish()
            attns.append(
                jnp.stack([got[:, :s], got[:, s : 2 * s], got[:, 2 * s :], owned(o_sum)])
            )
        grad_attn, grad_up, grad_down = jnp.stack(attns), jnp.stack(ups), jnp.stack(downs)
        for axis in ("blk", "img"):
            j = 1
            while j < lax.axis_size(axis):
                rows = rows + swap(rows, axis, j)
                j *= 2
        vec_total = lax.dynamic_slice_in_dim(rows[:20], place * piece, piece, 1)
        vec_total = vec_total.reshape(2, 10, piece)
        bias_total = lax.dynamic_slice_in_dim(
            rows[20:28].reshape(2, ff), place * (ff // images), ff // images, 1
        )
    else:
        rows, o0_own = call(
            "vectors",
            functools.partial(vector_total_kernel, slice(piece, piece + 16)),
            many([attn0.keep, attn0.got]),
            [((32, piece), F32), ((piece, s), BF)],
        )
        o0_own = transpose_owners(o0_own)
        rows = rows + swap(rows, "blk", 1)
        rows = rows + swap(rows, "blk", 2)
        got0 = later(ffn0[0].got, grad_x, *downs1)
        downs0 = call(
            "tail",
            functools.partial(tail_kernel, [(0, slice(0, piece), 1, slice(0, piece))]),
            [(scal, "s")] + many([ffn0[0].keep, got0]),
            [((piece, s), BF)] * CYCLE,
        )
        downs0 = exchange(list(downs0))
        last = [ffn0[1].keep, attn0.keep, attn0.got, got0, o0_own] + downs0
        last += [sums1[1].keep, sums1[0].keep, got1, o1_own] + downs1
        grad_attn, grad_up, grad_down, vec_total, bias_total = call(
            "finish",
            finish_kernel,
            [(scal, "s")] + many(last + [rows]),
            [
                ((2, 4, piece, s), F32),
                ((2, piece, ffb), F32),
                ((2, s, ff // images), F32),
                ((10, 2, piece), F32),
                ((2, ff // images), F32),
            ],
        )
        grad_down, vec_total = jnp.swapaxes(grad_down, 1, 2), jnp.swapaxes(vec_total, 0, 1)

    return (
        e_b[:, None, :],
        g_b[:, None, :],
        grad_x,
        grad_m,
        grad_attn,
        grad_up,
        grad_down,
        vec_total,
        bias_total,
    )


def solution(mesh):
    rows = P("blk", "img", None)
    in_specs = (rows, rows, P("img"), P(), P(), P(), P(), P(), rows, rows)
    out_specs = (
        rows,
        rows,
        rows,
        rows,
        P(None, None, "img", "blk"),
        P(None, "img", "blk"),
        P(None, "img", "blk"),
        P(None, None, "img"),
        P(None, "img"),
    )
    return jax.shard_map(body, mesh=mesh, in_specs=in_specs, out_specs=out_specs, check_vma=False)
```

```python
import functools

import jax
import jax.numpy as jnp
from jax import lax
from jax.experimental import pallas as pl
from jax.experimental.pallas import tpu as pltpu
from jax.sharding import PartitionSpec as P

HEADS = 12
HEAD = 64
NPATCH = 576
EPS = 1e-06
BF = jnp.bfloat16
F32 = jnp.float32
CYCLE = 4
MIB = 1024 * 1024
COSTS = {'prep': 4.0, 'load': 5.0, 'tail': 0.01, 'pick': 1.3, 'cut': 2.5, 'vectors': 0.5, 'enc_attend': 3.3, 'mask_project': 0.9, 'enc_ffn': 5.9, 'reg_attend': 3.4, 'reg_ffn': 8.2, 'reg_attend_back': 5.7, 'reg_attn_grad': 2.7, 'reg_ffn_grad': 4.5, 'enc_ffn_back': 0.01, 'enc_attend_back': 8.0, 'enc_ffn_grad': 0.01, 'img_step': 0.01, 'input_grad': 7.4, 'finish': 2.6}
COST_SCALE = 0.3


def round_up(value, unit):
    return (value + unit - 1) // unit * unit


def dot(left, right):
    return jnp.dot(left, right, preferred_element_type=F32)


def dot_nt(left, right):
    return lax.dot_general(left, right, (((1,), (1,)), ((), ())), preferred_element_type=F32)


def dot_tn(left, right):
    return lax.dot_general(left, right, (((0,), (0,)), ((), ())), preferred_element_type=F32)


def norm(rows):
    centred = rows - jnp.mean(rows, -1, keepdims=True)
    inverse = lax.rsqrt(jnp.mean(centred * centred, -1, keepdims=True) + EPS)
    return centred * inverse, inverse


def norm_back(grad_out, gain, normed, inverse):
    scaled = grad_out * gain
    return inverse * (
        scaled
        - jnp.mean(scaled, -1, keepdims=True)
        - normed * jnp.mean(scaled * normed, -1, keepdims=True)
    )


def padded_rows(ref, padded):
    rows = ref[...].astype(F32)
    if rows.shape[0] == padded:
        return rows
    return jnp.concatenate([rows, jnp.zeros((padded - rows.shape[0], rows.shape[1]), F32)], 0)


def gelu_cdf(u):
    return 0.5 * (1.0 + lax.erf(u * 0.7071067811865476))


def gelu_parts(u):
    cdf = gelu_cdf(u)
    slope = cdf + u * (jnp.exp(u * u * -0.5) * 0.3989422804014327)
    return cdf, slope


def col_sum(rows):
    return jnp.sum(rows, 0, keepdims=True)


def swap(block, axis, offset):
    size = lax.axis_size(axis)
    return lax.ppermute(block, axis, [(i, i ^ offset) for i in range(size)])


def gather(block, first=None, second=None):
    across = swap(block if first is None else later(block, first), "blk", 2)
    if second is not None:
        over, beside = swap(later(across, second), "blk", 1), later(block, second)
    else:
        over, beside = swap(across, "blk", 1), block
    return [block, swap(beside, "blk", 1), across, over]


def later(value, *arrays):
    return lax.optimization_barrier((value, *arrays))[0]


def exchange(blocks, held=None):
    sent = blocks if held is None else held
    across, over = swap(sent[2], "blk", 2), swap(sent[3], "blk", 3)
    return [blocks[0], swap(sent[1], "blk", 1), across, over]


class ImgSum:
    def __init__(self, keep, sent, order):
        self.order = list(order)
        self.keep, self.sent, self.got = keep, sent, None
        self.at = slice(0, keep.shape[1])

    def step(self, *after):
        bit = self.order.pop(0)
        if self.got is not None:
            total = self.total().astype(BF)
            total = total.reshape((2, total.shape[0] // 2) + total.shape[1:])
            mine = (lax.axis_index("img") >> bit) & 1
            self.keep = lax.dynamic_index_in_dim(total, mine, 0, False)
            self.sent = lax.dynamic_index_in_dim(total, 1 - mine, 0, False)
        if after:
            self.sent = later(self.sent, *after)
        self.got = swap(self.sent, "img", 1 << bit)
        return self.sent

    def total(self):
        return self.keep.astype(F32) + self.got[:, self.at].astype(F32)

    def finish(self):
        while self.order:
            self.step()
        return self.total()[0]


def reduce_whole(parts):
    images = parts.shape[0]
    place = lax.axis_index("img")
    bits = images.bit_length() - 1
    pairs = parts.reshape((2, images // 2) + parts.shape[1:])
    mine = place >> (bits - 1)
    keep = lax.dynamic_index_in_dim(pairs, mine, 0, False)
    sent = lax.dynamic_index_in_dim(pairs, 1 - mine, 0, False)
    return ImgSum(keep, sent, range(bits - 1, -1, -1))


def transpose_owners(part):
    images, cycle = lax.axis_size("img"), lax.axis_size("blk")
    m = images // cycle
    pairs = []
    for i in range(images):
        for b in range(cycle):
            pairs.append((i * cycle + b, (b * m + i % m) * cycle + i // m))
    return lax.ppermute(part, ("img", "blk"), pairs)


def call(name, kernel, ins, outs, scratch=(), limit=8, after=(), keep=False, hold=(), alias=()):
    spaces = {"s": pltpu.SMEM, "v": pltpu.VMEM, "w": pltpu.VMEM, "a": pltpu.HBM, "n": pl.ANY}
    places = {"w": pltpu.VMEM, "a": pltpu.HBM}
    count = len(ins)
    ins = ins + [(a, "n") for a in after] + [(a, "w") for a in hold]

    def run(*refs):
        kernel(*refs[:count], *refs[len(ins) :])

    return pl.pallas_call(
        run,
        name=name,
        out_shape=[
            pltpu.VMEM(s, d) if keep else jax.ShapeDtypeStruct(s, d) for s, d in outs
        ],
        in_specs=[pl.BlockSpec(memory_space=spaces[k]) for _, k in ins],
        out_specs=[pl.BlockSpec(memory_space=pltpu.VMEM) for _ in outs],
        scratch_shapes=list(scratch),
        input_output_aliases=dict(alias),
        compiler_params=pltpu.CompilerParams(vmem_limit_bytes=limit * MIB),
        cost_estimate=pl.CostEstimate(
            flops=int(COST_SCALE * COSTS[name] * 1.15e9), bytes_accessed=1, transcendentals=0
        ),
    )(*[pltpu.with_memory_space_constraint(a, places[k]) if k in places else a for a, k in ins])


def step_kernel(bits, starts, groups, scal, *refs):
    count = len(bits)
    ins, keeps, outs = refs[: 2 * count], refs[2 * count : 3 * count], refs[3 * count :]
    for out, group in zip(outs, groups):
        start = 0
        for k in group:
            keep, got = ins[2 * k : 2 * k + 2]
            half, rows = keep.shape[0] // 2, keep.shape[1]
            mine = (scal[2] >> bits[k]) & 1
            sides = []
            for side in (mine, 1 - mine):
                at = pl.ds(side * half, half)
                other = got[at, starts[k] : starts[k] + rows]
                sides.append((keep[at].astype(F32) + other.astype(F32)).astype(BF))
            keeps[k][...] = sides[0]
            out[:, start : start + rows] = sides[1]
            start += rows


def step_all(scal, groups, after=(), hold=()):
    sums = [one for group in groups for one in group]
    if sums[0].got is not None:
        bits = [one.order[0] for one in sums]
        places, ins, keeps, outs = [], [(scal, "s")], [], []
        for group in groups:
            places.append([sums.index(one) for one in group])
            half, rows = group[0].keep.shape[0] // 2, 0
            for one in group:
                ins += [(one.keep, "v"), (one.got, "v")]
                keeps.append(((half,) + one.keep.shape[1:], BF))
                rows += one.keep.shape[1]
            outs.append(((half, rows, one.keep.shape[2]), BF))
        parts = call(
            "img_step",
            functools.partial(step_kernel, bits, [one.at.start for one in sums], places),
            ins,
            keeps + outs,
            after=after,
            hold=hold,
        )
        for k, one in enumerate(sums):
            one.keep = parts[k]
        sent = parts[len(sums) :]
    else:
        sent = [group[0].sent for group in groups]
    for group, message in zip(groups, sent):
        got, start = swap(message, "img", 1 << group[0].order[0]), 0
        for one in group:
            rows = one.keep.shape[1]
            one.order.pop(0)
            one.sent, one.got = message, got
            one.at, start = slice(start, start + rows), start + rows


def load_kernel(blk, scal, *refs):
    sems = refs[-1]
    count = (len(refs) - 1) // 2
    copies = []
    for k, (source, target) in enumerate(zip(refs[:count], refs[count:-1])):
        copies.append(pltpu.make_async_copy(source.at[blk], target, sems.at[k]))
    for copy in copies:
        copy.start()
    for copy in copies:
        copy.wait()


def pick_kernel(blk, scal, upb, up_all, own_out, bias_out):
    step = own_out.shape[1] // 8
    for m in range(CYCLE):

        @pl.when(scal[0] == m)
        def _():
            for i in range(8):
                at = (CYCLE * i + m) * step
                own_out[:, i * step : (i + 1) * step] = up_all[:, at : at + step]
                bias_out[:, i * step : (i + 1) * step] = upb[blk : blk + 1, at : at + step]


def cut_kernel(blk, scal, upb, up_all, up, down, up_out, down_out, own_out, bias_out, sems):
    width = up_out.shape[1]
    mine = pl.ds(pl.multiple_of(scal[0] * width, 128), width)
    copies = [
        pltpu.make_async_copy(up.at[blk, :, mine], up_out, sems.at[0]),
        pltpu.make_async_copy(down.at[blk, mine], down_out, sems.at[1]),
    ]
    for copy in copies:
        copy.start()
    pick_kernel(blk, scal, upb, up_all, own_out, bias_out)
    for copy in copies:
        copy.wait()


def prep_kernel(scal, attn, up, vectors, attn_out, up_out, vec, w_out, b_out, sems):
    me = scal[0]
    share = w_out.shape[3]
    window = share + share % 128
    odd = me & 1
    start = pl.multiple_of(me * share - odd * (share % 128), 128)
    copies = [
        pltpu.make_async_copy(attn.at[blk], attn_out.at[blk], sems.at[blk]) for blk in range(2)
    ]
    copies.append(pltpu.make_async_copy(up.at[0], up_out, sems.at[2]))
    copies.append(pltpu.make_async_copy(vectors, vec, sems.at[3]))
    for copy in copies[::-1]:
        copy.start()
    copies[3].wait()
    for blk in range(2):
        copies[blk].wait()
        for m in range(3):
            for parity in range(2):
                shift = parity * (share % 128)

                @pl.when(odd == parity)
                def _():
                    part = attn_out[blk, m, :, pl.ds(start, window)]
                    w_out[blk, m] = part[:, shift : shift + share]
                    if m == 1:
                        b_out[blk, m] = jnp.zeros((1, share), F32)
                    else:
                        row = vec[2 + m // 2, blk : blk + 1, pl.ds(start, window)]
                        b_out[blk, m] = row[:, shift : shift + share]
    copies[2].wait()


def key_bias(me, rows, padded, limit):
    at = lax.broadcasted_iota(jnp.int32, (padded, 1), 0)
    parts = []
    for j in range(CYCLE):
        live = (at < rows) & (at + (me ^ j) * rows < limit)
        parts.append(jnp.where(live, 0.0, -1e30))
    return jnp.concatenate(parts, 0)


def own_live(me, rows, padded, limit):
    at = lax.broadcasted_iota(jnp.int32, (padded, 1), 0)
    return jnp.where((at < rows) & (at + me * rows < limit), 1.0, 0.0)


def probs_t(keys, queries, bias):
    scores = dot_nt(keys, queries) + bias
    exps = jnp.exp(scores - jnp.max(scores, 0, keepdims=True))
    return exps * (1.0 / jnp.sum(exps, 0, keepdims=True))


def attend_t(q, k, v, bias, out_ref):
    qs = (q.astype(F32) * HEAD**-0.5).astype(BF)
    vt = v.astype(F32).T.astype(BF)
    mixed = []
    for h in range(q.shape[1] // HEAD):
        c = slice(h * HEAD, (h + 1) * HEAD)
        p = probs_t(k[:, c], qs[:, c], bias).astype(BF)
        mixed.append(dot(vt[c], p))
    out_ref[...] = jnp.concatenate(mixed, 0).T.astype(BF)


def attend_back_t(q, k, v, do, bias):
    qs = (q.astype(F32) * HEAD**-0.5).astype(BF)
    kt = (k.astype(F32) * HEAD**-0.5).T.astype(BF)
    dq, dk, dv = [], [], []
    for h in range(q.shape[1] // HEAD):
        c = slice(h * HEAD, (h + 1) * HEAD)
        p = probs_t(k[:, c], qs[:, c], bias)
        dp = dot_nt(v[:, c], do[:, c])
        ds = (p * (dp - jnp.sum(p * dp, 0, keepdims=True))).astype(BF)
        dv.append(dot(p.astype(BF), do[:, c]))
        dk.append(dot(ds, qs[:, c]))
        dq.append(dot(kt[c], ds))
    return (
        jnp.concatenate(dq, 0).T.astype(BF),
        jnp.concatenate(dk, 1).astype(BF),
        jnp.concatenate(dv, 1).astype(BF),
    )


def enc_attend_kernel(vis, scal, x0, x1, x2, x3, w, b, vec, h_out, q_out, k_out, v_out, o_out):
    me, count = scal[0], scal[1]
    padded = h_out.shape[0] // CYCLE
    for j, ref in enumerate((x0, x1, x2, x3)):
        n, _ = norm(padded_rows(ref, padded))
        h_out[j * padded : (j + 1) * padded] = (n * vec[0, 0:1] + vec[1, 0:1]).astype(BF)
    h = h_out[...]
    q = (dot(h, w[0, 0]) + b[0, 0]).astype(BF)
    k = dot(h, w[0, 1]).astype(BF)
    v = (dot(h, w[0, 2]) + b[0, 2]).astype(BF)
    q_out[...], k_out[...], v_out[...] = q, k, v
    attend_t(q, k, v, key_bias(me, vis, padded, count), o_out)


def mask_project_kernel(x0, x1, x2, x3, w, b, vec, h_out, q_out, k_out, v_out):
    padded = h_out.shape[0] // CYCLE
    for j, ref in enumerate((x0, x1, x2, x3)):
        n, _ = norm(ref[x0.shape[0] - padded :].astype(F32))
        h_out[j * padded : (j + 1) * padded] = (n * vec[0, 1:2] + vec[1, 1:2]).astype(BF)
    h = h_out[...]
    q_out[...] = (dot(h, w[1, 0]) + b[1, 0]).astype(BF)
    k_out[...] = dot(h, w[1, 1]).astype(BF)
    v_out[...] = (dot(h, w[1, 2]) + b[1, 2]).astype(BF)


def reg_attend_kernel(
    vis, hid, scal, x0, x1, x2, x3, w, b, qm, km, vm, h_out, k_out, v_out, o_out
):
    me, count = scal[0], scal[1]
    padded = x0.shape[0]
    nv = CYCLE * padded
    for j, ref in enumerate((x0, x1, x2, x3)):
        h_out[j * padded : (j + 1) * padded] = ref[...]
    h = h_out[...]
    k_out[0:nv] = dot(h, w[1, 1]).astype(BF)
    v_out[0:nv] = (dot(h, w[1, 2]) + b[1, 2]).astype(BF)
    k_out[nv:] = km[...]
    v_out[nv:] = vm[...]
    bias = jnp.concatenate(
        [
            key_bias(me, vis, padded, count),
            key_bias(me, hid, qm.shape[0] // CYCLE, NPATCH - count),
        ],
        0,
    )
    attend_t(qm[...], k_out[...], v_out[...], bias, o_out)


def assemble(me, blocks, scratch, lane):
    share = blocks[0].shape[1] if lane is None else lane[1]
    rows = scratch.shape[0]
    for m in range(CYCLE):

        @pl.when(me == m)
        def _():
            for j, ref in enumerate(blocks):
                at = (m ^ j) * share
                value = ref[...] if lane is None else ref[0:rows, lane[0] : lane[0] + share]
                scratch[:, at : at + share] = value


def ffn_forward(blk, rows, mixed, vec, upb, attn, up, down, gp):
    r = dot(mixed, attn[blk, 3]) + vec[4, blk : blk + 1]
    y = rows + vec[5, blk : blk + 1] * r
    n, _ = norm(y)
    h2 = (n * vec[6, blk : blk + 1] + vec[7, blk : blk + 1]).astype(BF)
    width = up.shape[0]
    z = vec[8, blk : blk + 1]
    for c in range(up.shape[1] // width):
        cols = slice(c * width, (c + 1) * width)
        u = dot(h2, up[:, cols]) + upb[blk : blk + 1, cols]
        cdf, slope = gelu_parts(u)
        gp[:, cols] = slope
        a = (u * cdf).astype(BF)
        z = z + dot(a, down[cols, :])
    return r, y, h2, z


def ffn_backward(blk, grad, r, y, z, vec, up, down, gp, up_sum):
    n, inverse = norm(y)
    scale2 = col_sum(grad * z)
    dz = (grad * vec[9, blk : blk + 1]).astype(BF)
    width = up.shape[0]
    dh2 = 0.0
    for c in range(up.shape[1] // width):
        cols = slice(c * width, (c + 1) * width)
        da = dot_nt(dz, down[cols, :])
        du = (gp[:, cols] * da).astype(BF)
        up_sum[:, cols] = col_sum(du.astype(F32))
        dh2 = dh2 + dot_nt(du, up[:, cols])
    dy = grad + norm_back(dh2, vec[6, blk : blk + 1], n, inverse)
    dr = (dy * vec[5, blk : blk + 1]).astype(BF)
    small = [
        scale2,
        col_sum(dh2 * n),
        col_sum(dh2),
        col_sum(dy * r),
        col_sum(dz.astype(F32)),
        col_sum(dr.astype(F32)),
    ]
    return dz, dy, dr, small


def enc_ffn_kernel(
    vis, scal, o0, o1, o2, o3, x, vec, upb, attn, up, down,
    e_out, eb_out, he_out, h2_out, y_out, r_out, z_out, gp_out,
    mixed,
):
    me, count = scal[0], scal[1]
    assemble(me, (o0, o1, o2, o3), mixed, None)
    r, y, h2, z = ffn_forward(
        0, padded_rows(x, he_out.shape[0]), mixed[...], vec, upb, attn, up, down, gp_out
    )
    h2_out[...], y_out[...], r_out[...], z_out[...] = h2, y, r, z
    e = (y + vec[9, 0:1] * z) * own_live(me, vis, he_out.shape[0], count)
    e_out[...] = e
    eb_out[...] = e[0 : eb_out.shape[0]].astype(BF)
    n, _ = norm(e)
    he_out[...] = (n * vec[0, 1:2] + vec[1, 1:2]).astype(BF)


def reg_ffn_kernel(
    hid, scal, o0, o1, o2, o3, x, cot, vec, upb, attn, up, down,
    gb_out, pair_out, dr_out, dy_out, small_out, up_sum,
    mixed, gp,
):
    me, count = scal[0], scal[1]
    assemble(me, (o0, o1, o2, o3), mixed, None)
    r, y, h2, z = ffn_forward(
        1, x[x.shape[0] - dr_out.shape[0] :].astype(F32), mixed[...], vec, upb, attn, up, down, gp
    )
    padded = dr_out.shape[0]
    live = own_live(me, hid, padded, NPATCH - count)
    g = (y + vec[9, 1:2] * z) * live
    gb_out[...] = g[0 : gb_out.shape[0]].astype(BF)
    grad = cot[...].astype(F32) * live
    dz, dy, dr, small = ffn_backward(1, grad, r, y, z, vec, up, down, gp, up_sum)
    pair_out[0:padded] = h2
    pair_out[padded:] = dz
    dr_out[...] = dr
    dy_out[...] = dy
    for i, row in enumerate(small):
        small_out[i : i + 1] = row
    small_out[6:8] = jnp.zeros((2, small_out.shape[1]), F32)


def enc_ffn_back_kernel(
    vis, scal, g0, g1, g2, g3, e, cot, y, r, z, gp, h2, vec, attn, up, down,
    pair_out, dr_out, dy_out, small_out, up_sum,
    dk, dv,
):
    me, count = scal[0], scal[1]
    share = g0.shape[1] // 2
    assemble(me, (g0, g1, g2, g3), dk, (0, share))
    assemble(me, (g0, g1, g2, g3), dv, (share, share))
    n, inverse = norm(e[...])
    dh = dot_nt(dk[...], attn[1, 1]) + dot_nt(dv[...], attn[1, 2])
    grad_e = norm_back(dh, vec[0, 1:2], n, inverse)
    grad = (cot[...].astype(F32) + grad_e) * own_live(me, vis, cot.shape[0], count)
    dz, dy, dr, small = ffn_backward(
        0, grad, r[...], y[...], z[...], vec, up, down, gp, up_sum
    )
    pair_out[0 : dz.shape[0]] = h2[...]
    pair_out[dz.shape[0] :] = dz
    dy_out[...], dr_out[...] = dy, dr
    for i, row in enumerate(small + [col_sum(dh * n), col_sum(dh)]):
        small_out[i : i + 1] = row


def spread(place_of, keep, sent, place, order, rows, cols):
    first, second, third = order
    for i in range(8):
        t = 2 * ((i >> second) & 1) + ((i >> third) & 1)
        value = place_of(i)

        for side in range(2):
            target = keep if side == ((i >> first) & 1) else sent

            @pl.when(((place >> first) & 1) == side)
            def _():
                target[t, rows, cols] = value


def owner_piece(mat, i, share, parts):
    quarter, half = i >> 1, i & 1
    rows = mat.shape[0] // 2
    part = mat[half * rows : (half + 1) * rows, quarter * share : (quarter + 1) * share]
    rows = rows // parts
    return jnp.concatenate([part[k * rows : (k + 1) * rows] for k in range(parts)], 1)


def attn_pieces(h, dqkv, o, dr):
    share = dqkv[0].shape[1]
    results = [dot_tn(h, grad).astype(BF) for grad in dqkv]
    d_o = dot_tn(o, dr).astype(BF)
    step = h.shape[1] // 8

    def piece(i):
        parts = [result[i * step : (i + 1) * step] for result in results]
        return jnp.concatenate(parts + [owner_piece(d_o, i, share, 1)], 1)

    return results, d_o, piece


def norm_sums(rows, dqkv, w):
    dh = 0.0
    for m, grad in enumerate(dqkv):
        dh = dh + dot_nt(grad, w[m])
    n, _ = norm(rows.astype(F32))
    return col_sum(dh * n), col_sum(dh)


def store_attn(results, d_o, nats):
    share = d_o.shape[0]
    for m, result in enumerate(results):
        nats[0][:, m * share : (m + 1) * share] = result
    nats[1][...] = d_o


def reg_attend_back_kernel(
    vis, hid, scal, d0, d1, d2, d3, q, k, v, attn,
    e_out, m_out, qv_out,
    dr,
):
    me, count = scal[0], scal[1]
    share = q.shape[1]
    padded = d0.shape[0]
    for j, ref in enumerate((d0, d1, d2, d3)):
        dr[j * padded : (j + 1) * padded] = ref[...]
    do = dot_nt(dr[...], attn[1, 3, pl.ds(pl.multiple_of(me * share, 16), share), :]).astype(BF)
    nm = CYCLE * padded
    nv = k.shape[0] - nm
    bias = jnp.concatenate(
        [
            key_bias(me, vis, nv // CYCLE, count),
            key_bias(me, hid, padded, NPATCH - count),
        ],
        0,
    )
    dq, dk, dv = attend_back_t(q[...], k[...], v[...], do, bias)
    e_out[:, 0:share] = dk[0:nv]
    e_out[:, share:] = dv[0:nv]
    m_out[:, 0:share] = dq
    m_out[:, share : 2 * share] = dk[nv:]
    m_out[:, 2 * share :] = dv[nv:]
    qv_out[0:1] = col_sum(dq.astype(F32))
    qv_out[1:2] = col_sum(dv.astype(F32))
    qv_out[2:8] = jnp.zeros((6, share), F32)


def enc_attend_back_kernel(
    vis, order, natural, scal, d0, d1, d2, d3, h, q, k, v, o, gm, x0, x1, x2, x3, w,
    small0, small1, norm1, qv1, ups0, ups1, attn,
    g_out, vec_out, first, second, dr, qv0, norm0,
):
    me, count = scal[0], scal[1]
    share = q.shape[1]
    padded = d0.shape[0]
    for j, ref in enumerate((d0, d1, d2, d3)):
        dr[j * padded : (j + 1) * padded] = ref[...]
    do = dot_nt(dr[...], attn[0, 3, pl.ds(pl.multiple_of(me * share, 16), share), :]).astype(BF)
    dq, dk, dv = attend_back_t(
        q[...], k[...], v[...], do, key_bias(me, vis, padded, count)
    )
    for j in range(CYCLE):
        at = slice(j * padded, (j + 1) * padded)
        for m, grad in enumerate((dq, dk, dv)):
            g_out[j, 0:padded, m * share : (m + 1) * share] = grad[at]
        more = g_out.shape[1] - padded
        g_out[j, padded:] = gm[j * more : (j + 1) * more]
    qv0[0:1] = col_sum(dq.astype(F32))
    qv0[1:2] = col_sum(dv.astype(F32))
    x = jnp.concatenate([padded_rows(ref, padded) for ref in (x0, x1, x2, x3)], 0)
    norm0[0:1], norm0[1:2] = norm_sums(x, (dq, dk, dv), (w[0, 0], w[0, 1], w[0, 2]))
    vector_rows(
        natural, me, (small0, small1), (norm0, norm1), (qv0, qv1), (ups0, ups1), vec_out
    )
    results, d_o, piece = attn_pieces(h[...], (dq, dk, dv), o[...], dr[...])
    if natural:
        store_attn(results, d_o, (first, second))
        return
    step, cols = h.shape[1] // 8, slice(0, 4 * share)

    def vector_piece(i):
        mine = slice(i * step, (i + 1) * step)
        parts = [vec_out[0:16, mine], vec_out[16:32, mine]]
        parts.append(jnp.zeros((16, 4 * share - 2 * step), F32))
        return jnp.concatenate(parts, 1).astype(BF)

    spread(piece, first, second, scal[2], order, slice(0, step), cols)
    spread(vector_piece, first, second, scal[2], order, slice(step, step + 16), cols)


def ffn_pieces(blk, scal, pairs, upb, up, down, h2, dz, own=None, bias=None):
    me = scal[0]
    width = up.shape[0]
    cols = pl.ds(pl.multiple_of(me * width, 128), width)
    padded = pairs[0].shape[0] // 2
    for j, pair in enumerate(pairs):
        at = slice(j * padded, (j + 1) * padded)
        h2[at] = pair[0:padded]
        dz[at] = pair[padded:]
    whole = pl.ds(0, width) if up.shape[1] == width else cols
    u = dot(h2[...], up[:, whole]) + upb[blk : blk + 1, cols]
    cdf, slope = gelu_parts(u)
    du = (slope * dot_nt(dz[...], down[whole, :])).astype(BF)
    if own is not None:
        u = dot(h2[...], own[...]) + bias[...]
        cdf = gelu_cdf(u)
    a = (u * cdf).astype(BF)
    d_down = dot_tn(a, dz[...]).astype(BF)
    d_up = dot_tn(h2[...], du).astype(BF)
    step = width // 8
    return (
        d_down,
        d_up,
        lambda i: (
            d_down[i * step : (i + 1) * step]
            if own is not None
            else owner_piece(d_down, i, width // 4, 4)
        ),
        lambda i: d_up[i * step : (i + 1) * step],
    )


def vector_rows(natural, me, smalls, norms, qvs, ups, out):
    share, width = qvs[0].shape[1], out.shape[1]
    step = width // 8
    out[...] = jnp.zeros(out.shape, F32)
    for blk, (small, qv, up_sum) in enumerate(zip(smalls, qvs, ups)):
        at = 10 * blk
        gain, bias = norms[blk][0:1], norms[blk][1:2]
        if blk == 1:
            gain, bias = gain + smalls[0][6:7], bias + smalls[0][7:8]
        scale2, gain2, bias2, scale1, dzs, drs = [small[i : i + 1] for i in range(6)]
        rows = {0: gain, 1: bias, 4: drs, 5: scale1, 6: gain2, 7: bias2, 8: dzs, 9: scale2}
        for i, row in rows.items():
            out[at + i : at + i + 1] = row
        first = 20 + 4 * blk
        for k in range(4):
            if natural:
                out[first + k : first + k + 1] = up_sum[0:1, k * width : (k + 1) * width]
            else:
                parts = [
                    up_sum[0:1, (4 * i + k) * step : (4 * i + k + 1) * step] for i in range(8)
                ]
                out[first + k : first + k + 1] = jnp.concatenate(parts, 1)
        for m in range(CYCLE):

            @pl.when(me == m)
            def _():
                cols = slice(m * share, (m + 1) * share)
                out[at + 2 : at + 3, cols] = qv[0:1]
                out[at + 3 : at + 4, cols] = qv[1:2]


def enc_ffn_grad_kernel(
    orders, natural, scal, p0, p1, p2, p3, upb, own, bias, up, down, *refs
):
    outs, scratch = refs[:-2], refs[-2:]
    d_down, d_up, down_piece, up_piece = ffn_pieces(
        0, scal, (p0, p1, p2, p3), upb, up, down, *scratch, *(() if natural else (own, bias))
    )
    if natural:
        outs[0][...], outs[1][...] = d_down, d_up
        return
    here, cols = slice(0, d_up.shape[0] // 8), slice(0, d_up.shape[1])
    spread(down_piece, outs[0], outs[1], scal[2], orders[0], here, cols)
    spread(up_piece, outs[2], outs[3], scal[2], orders[1], here, cols)


def reg_attn_grad_kernel(
    orders, natural, scal, h_m, h_e, g_m, g_e, o, d0, d1, d2, d3, x0, x1, x2, x3, w, *refs
):
    outs, norm_out, dr = refs[:-2], refs[-2], refs[-1]
    share = g_e.shape[1] // 2
    padded = d0.shape[0]
    for j, ref in enumerate((d0, d1, d2, d3)):
        dr[j * padded : (j + 1) * padded] = ref[...]
    x = jnp.concatenate([ref[ref.shape[0] - padded :] for ref in (x0, x1, x2, x3)], 0)
    dqkv_m = [g_m[:, m * share : (m + 1) * share] for m in range(3)]
    norm_out[0:1], norm_out[1:2] = norm_sums(x, dqkv_m, (w[1, 0], w[1, 1], w[1, 2]))
    norm_out[2:8] = jnp.zeros((6, norm_out.shape[1]), F32)
    h = jnp.concatenate([h_e[...], h_m[...]], 0)
    none = jnp.zeros((h_e.shape[0], share), BF)
    grads = []
    for m in range(3):
        top = none if m == 0 else g_e[:, (m - 1) * share : m * share]
        grads.append(jnp.concatenate([top, dqkv_m[m]], 0))
    results, d_o, attn_piece = attn_pieces(h, grads, o[...], dr[...])
    if natural:
        store_attn(results, d_o, outs)
        return
    step, cols = h.shape[1] // 8, slice(0, h.shape[1])
    half = step // 2
    for k in range(2):
        spread(
            lambda i: attn_piece(i)[k * half : (k + 1) * half], outs[2 * k], outs[2 * k + 1],
            scal[2], orders[k], slice(step, step + half), cols,
        )


def reg_ffn_grad_kernel(
    orders, natural, scal, p0, p1, p2, p3, upb, own, bias, up, down, *refs
):
    outs, scratch = refs[-6:-2] if not natural else refs[-4:-2], refs[-2:]
    d_down, d_up, down_piece, up_piece = ffn_pieces(
        1, scal, (p0, p1, p2, p3), upb, up, down, *scratch, *(() if natural else (own, bias))
    )
    if natural:
        outs[0][...], outs[1][...] = d_down, d_up
        return
    step, cols = d_up.shape[0] // 8, slice(0, d_up.shape[1])
    for k, piece in enumerate((down_piece, up_piece)):
        spread(piece, outs[2 * k], outs[2 * k + 1], scal[2], orders[k], slice(0, step), cols)


def input_grad_kernel(
    scal, g0, g1, g2, g3, x, mq, dy0, dy1, vec, attn, out0, out1, dq, dk, dv
):
    share = g0.shape[1] // 3
    grads = (dq, dk, dv)
    for m, ref in enumerate(grads):
        assemble(scal[0], (g0, g1, g2, g3), ref, (m * share, share))
    first = dy0.shape[0]
    rows = (slice(0, first), slice(first, g0.shape[0]))
    for blk, (at, own, dy, out) in enumerate(
        ((rows[0], x, dy0, out0), (rows[1], mq, dy1, out1))
    ):
        n, inverse = norm(padded_rows(own, dy.shape[0]))
        dh = 0.0
        for m, ref in enumerate(grads):
            dh = dh + dot_nt(ref[at], attn[blk, m])
        dx = norm_back(dh, vec[0, blk : blk + 1], n, inverse) + dy[...]
        out[:, 0, :] = dx[0 : out.shape[0]]


def tail_kernel(parts, scal, *refs):
    count = max(part[2] for part in parts) + 1
    ins, downs, o_out = refs[:count], refs[count : count + CYCLE], refs[count + CYCLE :]

    def total(part, cols):
        keep, at, got, got_at = part
        return ins[keep][0, at, cols].astype(F32) + ins[got][0, got_at, cols].astype(F32)

    share = downs[0].shape[1]
    for m in range(CYCLE):

        @pl.when(scal[0] == m)
        def _():
            for j, ref in enumerate(downs):
                at = (m ^ j) * share
                ref[...] = total(parts[0], slice(at, at + share)).astype(BF)

    start = 0
    for part in parts[1:]:
        at = slice(start, start + part[1].stop - part[1].start)
        o_out[0][at] = total(part, slice(3 * share, 4 * share)).astype(BF)
        start = at.stop


def vector_total_kernel(at, keep, got, out, o_out):
    step = out.shape[1]
    for k in range(2):
        cols = slice(k * step, (k + 1) * step)
        out[16 * k : 16 * k + 16] = keep[0, at, cols].astype(F32) + got[0, at, cols].astype(F32)
    rows, cols = slice(0, o_out.shape[0]), slice(3 * o_out.shape[1], 4 * o_out.shape[1])
    o_out[...] = (keep[0, rows, cols].astype(F32) + got[0, rows, cols].astype(F32)).astype(BF)


def finish_kernel(scal, *refs):
    (up0, attn0, attn0_got, got0, o0), downs0 = refs[:5], refs[5 : 5 + CYCLE]
    refs = refs[5 + CYCLE :]
    (up1, down1, got1, o1), downs1 = refs[:4], refs[4 : 4 + CYCLE]
    rows, attn_out, up_out, down_out, vec_out, bias_out = refs[4 + CYCLE :]
    piece, share = attn_out.shape[2], attn_out.shape[3]
    half = piece // 2
    tail = slice(piece, 3 * half)
    moves = (
        (0, slice(0, piece), attn0, slice(0, piece), attn0_got, slice(0, piece)),
        (1, slice(0, half), down1, tail, got1, tail),
        (1, slice(half, piece), up1, tail, got1, slice(5 * half, 6 * half)),
    )
    for blk, to, keep, keep_at, got, got_at in moves:
        for m in range(3):
            cols = slice(m * share, (m + 1) * share)
            attn_out[blk, m, to] = keep[0, keep_at, cols].astype(F32) + got[
                0, got_at, cols
            ].astype(F32)
    for blk, o, downs in ((0, o0, downs0), (1, o1, downs1)):
        attn_out[blk, 3] = o[...].astype(F32)
        for m in range(CYCLE):

            @pl.when(scal[0] == m)
            def _():
                for j, ref in enumerate(downs):
                    at = (m ^ j) * piece
                    down_out[blk, :, at : at + piece] = ref[...].astype(F32).T

    for blk, keep, got, start in ((0, up0, got0, piece), (1, up1, got1, 3 * half)):
        up_out[blk] = keep[0, 0:piece].astype(F32) + got[0, start : start + piece].astype(F32)
        for k in range(10):
            vec_out[k, blk : blk + 1] = rows[10 * blk + k : 10 * blk + k + 1]
        for k in range(4):
            bias_out[blk : blk + 1, k * piece : (k + 1) * piece] = rows[
                20 + 4 * blk + k : 21 + 4 * blk + k
            ]


def body(
    visible,
    masked_queries,
    visible_counts,
    attention_matrices,
    up_projection_weights,
    down_projection_weights,
    vectors,
    up_projection_bias,
    encoder_cotangent,
    cot_regressor,
):
    vis, width = visible.shape[0], visible.shape[2]
    hid = masked_queries.shape[0]
    images = lax.axis_size("img")
    me = lax.axis_index("blk")
    place = lax.axis_index("img")
    pv, pm = round_up(vis, 16), round_up(hid, 16)
    nv, nm = CYCLE * pv, CYCLE * pm
    s = width // CYCLE
    ff = up_projection_weights.shape[2]
    ffb = ff // CYCLE
    natural = images != 8
    vec, upb = jnp.swapaxes(vectors, 0, 1), up_projection_bias
    dma = pltpu.SemaphoreType.DMA

    def pad(rows, to):
        return jnp.pad(rows[:, 0, :], ((0, to - rows.shape[0]), (0, 0)))

    def many(arrays, kind="v"):
        return [(a, kind) for a in arrays]

    scal = jnp.stack([me, visible_counts[0], place]).astype(jnp.int32)
    attn, up0, vec, w_own, b_own = call(
        "prep",
        prep_kernel,
        [(scal, "s"), (attention_matrices, "a"), (up_projection_weights, "a"), (vec, "a")],
        [(attention_matrices.shape, BF), ((width, ff), BF), (vec.shape, F32)]
        + [((2, 3, width, s), BF), ((2, 3, 1, s), F32)],
        [dma((4,))],
        keep=True,
    )

    def load(blk, sources, shapes, after, hold):
        return call(
            "load",
            functools.partial(load_kernel, blk),
            [(scal, "s")] + many(sources, "a"),
            [(shape, BF) for shape in shapes],
            [dma((len(sources),))],
            keep=True,
            after=after,
            hold=hold,
        )

    both_projections = [up_projection_weights, down_projection_weights]
    x, mq = visible[:, 0, :], pad(masked_queries, pm)
    xs = gather(x, None, b_own)
    cot_e, cot_g = pad(encoder_cotangent, pv), pad(cot_regressor, pm)

    h0, q0, k0, v0, o0 = call(
        "enc_attend",
        functools.partial(enc_attend_kernel, vis),
        [(scal, "s")] + many(xs) + many([w_own, b_own, vec]),
        [((nv, width), BF)] + [((nv, s), BF)] * 4,
        hold=[attn, up0],
    )
    (down0,) = load(0, [down_projection_weights], [(ff, width)], [o0], [attn, up0])
    mixed0 = exchange([o0[j * pv : (j + 1) * pv] for j in range(CYCLE)])
    e, e_b, he, h2_0, y0, r0, z0, gp0 = call(
        "enc_ffn",
        functools.partial(enc_ffn_kernel, vis),
        [(scal, "s")] + many(mixed0) + many([x, vec, upb]) + many([attn, up0, down0], "w"),
        [((pv, width), F32), ((vis, width), BF), ((pv, width), BF), ((pv, width), BF)]
        + [((pv, width), F32)] * 3
        + [((pv, ff), F32)],
        [pltpu.VMEM((pv, width), BF)],
    )

    up1, down1 = load(
        1, both_projections, [(width, ff), (ff, width)], [he], [attn, up0, down0]
    )
    mqs = gather(mq, xs[2], e)
    hm, qm, km, vm = call(
        "mask_project",
        mask_project_kernel,
        many(mqs) + many([w_own, b_own, vec]),
        [((nm, width), BF)] + [((nm, s), BF)] * 3,
        after=[up1],
        hold=[attn, up0, down0, up1, down1],
    )
    hes = gather(he, None, up1)
    h_vis, k1, v1, o1 = call(
        "reg_attend",
        functools.partial(reg_attend_kernel, vis, hid),
        [(scal, "s")] + many(hes) + many([w_own, b_own, qm, km, vm]),
        [((nv, width), BF), ((nv + nm, s), BF), ((nv + nm, s), BF), ((nm, s), BF)],
        hold=[attn, up0, down0, up1, down1],
    )
    mixed1 = exchange([o1[j * pm : (j + 1) * pm] for j in range(CYCLE)])
    g_b, pair1, dr1, dy1, small1, ups1 = call(
        "reg_ffn",
        functools.partial(reg_ffn_kernel, hid),
        [(scal, "s")] + many(mixed1) + many([mq, cot_g, vec, upb]) + many([attn, up1, down1], "w"),
        [((hid, width), BF), ((2 * pm, width), BF), ((pm, width), BF), ((pm, width), F32)]
        + [((8, width), F32), ((1, ff), F32)],
        [pltpu.VMEM((pm, width), BF), pltpu.VMEM((pm, ff), F32)],
        hold=[up0, down0],
    )

    piece = width // images
    m = images // CYCLE
    first_x, first_z = [0, 1, 2], [1, 0, 2]

    def message(rows):
        return [((images // 2, rows, width), BF)] * 2

    def by_owner(mat):
        count = mat.shape[0] // m
        cut = mat.reshape(m, count, CYCLE, s).transpose(2, 0, 1, 3)
        return reduce_whole(cut.reshape(images, count, s))

    def by_rows(mat):
        return reduce_whole(mat.reshape(images, piece, mat.shape[1]))

    ffn_whole = [((ffb, width), BF), ((width, ffb), BF)]
    attn_whole = [((width, 3 * s), BF), ((s, width), BF)]

    half = piece // 2

    def ffn_scratch(rows):
        return [pltpu.VMEM((rows, width), BF)] * 2

    up1_cut, down1_cut, own1, bias1 = call(
        "cut",
        functools.partial(cut_kernel, 1),
        [(scal, "s"), (upb, "v"), (up1, "w")] + many(both_projections, "a"),
        [((width, ffb), BF), ((ffb, width), BF), ((width, ffb), BF), ((1, ffb), F32)],
        [dma((2,))],
        keep=True,
        after=[dr1],
        hold=[attn, up0, down0],
    )
    dr1s = gather(dr1, None, up1_cut)
    ge, gm, qv1 = call(
        "reg_attend_back",
        functools.partial(reg_attend_back_kernel, vis, hid),
        [(scal, "s")] + many(dr1s) + many([qm, k1, v1]) + [(attn, "w")],
        [((nv, 2 * s), BF), ((nm, 3 * s), BF), ((8, s), F32)],
        [pltpu.VMEM((nm, width), BF)],
        limit=10,
        hold=[up0, down0, up1_cut, down1_cut],
    )
    ges = exchange([ge[j * pv : (j + 1) * pv] for j in range(CYCLE)])
    parts1 = call(
        "reg_attn_grad",
        functools.partial(reg_attn_grad_kernel, (first_x, first_z), natural),
        [(scal, "s")] + many([hm, h_vis, gm, ge, o1] + dr1s + mqs + [w_own]),
        (attn_whole if natural else message(piece + piece // 2) * 2) + [((8, width), F32)],
        [pltpu.VMEM((nm, width), BF)],
        after=[qv1],
        limit=10,
        hold=[attn, up0, down0, up1_cut, down1_cut],
    )
    norm1 = parts1[-1]
    pairs1 = gather(pair1, dr1s[2], norm1)
    buffers = [] if natural else list(parts1[:-1])
    first = 1 + CYCLE + 5
    out = call(
        "reg_ffn_grad",
        functools.partial(reg_ffn_grad_kernel, (first_x, first_z), natural),
        [(scal, "s")]
        + many(pairs1)
        + many([upb, own1, bias1])
        + many([up1_cut, down1_cut], "w")
        + many(buffers),
        ffn_whole if natural else message(piece + piece // 2) * 2,
        ffn_scratch(nm),
        after=[norm1],
        limit=10,
        hold=[attn, up0, down0],
        alias=[(first + k, k) for k in range(len(buffers))],
    )
    if natural:
        sums1 = [by_owner(out[0]), by_rows(out[1]), by_rows(parts1[0]), by_owner(parts1[1])]
    else:
        sums1 = [ImgSum(out[0], out[1], first_x), ImgSum(out[2], out[3], first_z)]

    def steps(groups, *after, hold=(attn,)):
        if natural:
            for group in groups:
                for one in group:
                    one.step()
        else:
            step_all(scal, groups, after, hold)

    for one in sums1:
        one.sent = later(one.sent, *ges[1:])
    steps([[one] for one in sums1])
    pair0, dr0, dy0, small0, ups0 = call(
        "enc_ffn_back",
        functools.partial(enc_ffn_back_kernel, vis),
        [(scal, "s")]
        + many(ges)
        + many([e, cot_e, y0, r0, z0, gp0, h2_0, vec])
        + many([attn, up0, down0], "w"),
        [((2 * pv, width), BF), ((pv, width), BF), ((pv, width), F32), ((8, width), F32)]
        + [((1, ff), F32)],
        [pltpu.VMEM((pv, width), BF)] * 2,
        after=[norm1],
    )

    own0, bias0 = call(
        "pick",
        functools.partial(pick_kernel, 0),
        [(scal, "s"), (upb, "v"), (up0, "w")],
        [((width, ffb), BF), ((1, ffb), F32)],
        after=[dr0],
        hold=[attn, down0],
    )
    dr0s = gather(dr0, None, own0)
    out = call(
        "enc_attend_back",
        functools.partial(enc_attend_back_kernel, vis, first_x, natural),
        [(scal, "s")]
        + many(dr0s)
        + many([h0, q0, k0, v0, o0, gm] + xs + [w_own])
        + many([small0, small1, norm1, qv1, ups0, ups1])
        + [(attn, "w")],
        [((CYCLE, pv + pm, 3 * s), BF), ((32, width), F32)]
        + (attn_whole if natural else message(piece + 16)),
        [pltpu.VMEM((nv, width), BF), pltpu.VMEM((8, s), F32), pltpu.VMEM((8, width), F32)],
        after=[small0],
        limit=10,
        hold=[up0, down0],
    )
    g, rows = out[:2]
    if natural:
        attn0, o0_sum = by_rows(out[2]), by_owner(out[3])
    else:
        attn0 = ImgSum(out[2], out[3], first_x)
    steps([[attn0]])
    steps([[one] for one in sums1], rows, hold=(attn, up0, down0))
    pairs0 = gather(pair0, dr0s[2], rows)
    out = call(
        "enc_ffn_grad",
        functools.partial(enc_ffn_grad_kernel, (first_z, first_x), natural),
        [(scal, "s")] + many(pairs0) + many([upb, own0, bias0]) + many([up0, down0], "w"),
        ffn_whole if natural else message(piece) * 2,
        ffn_scratch(nv),
        after=[sums1[0].sent],
        hold=[attn],
    )
    if natural:
        ffn0 = [by_owner(out[0]), by_rows(out[1])]
    else:
        ffn0 = [ImgSum(out[0], out[1], first_z), ImgSum(out[2], out[3], first_x)]
    steps([[one] for one in ffn0])
    steps([sums1], out[0])
    steps([[attn0]], sums1[0].sent)
    steps([[one] for one in ffn0 + [attn0]], sums1[0].got)
    g = later(g, ffn0[0].sent)
    gs = exchange([g[j] for j in range(CYCLE)])
    if not natural:
        got1 = later(sums1[0].got, ffn0[0].sent)
        parts1 = [
            (0, slice(0, piece), 2, slice(0, piece)),
            (0, slice(piece, 3 * half), 2, slice(piece, 3 * half)),
            (1, slice(piece, 3 * half), 2, slice(5 * half, 6 * half)),
        ]
        *downs1, o1_own = call(
            "tail",
            functools.partial(tail_kernel, parts1),
            [(scal, "s")] + many([sums1[0].keep, sums1[1].keep, got1]),
            [((piece, s), BF)] * (CYCLE + 1),
        )
        downs1, o1_own = exchange(downs1), transpose_owners(o1_own)
        steps([ffn0], attn0.got)

    grad_x, grad_m = call(
        "input_grad",
        input_grad_kernel,
        [(scal, "s")] + many(gs) + many([x, mq, dy0, dy1, vec]) + [(attn, "w")],
        [((vis, 1, width), F32), ((hid, 1, width), F32)],
        [pltpu.VMEM((pv + pm, width), BF)] * 3,
        after=[ffn0[0].sent],
    )

    if natural:

        def owned(sums):
            return transpose_owners(sums.finish().astype(BF)).astype(F32)

        ups, downs, attns = [], [], []
        for down_sum, up_sum, qkv, o_sum in (ffn0 + [attn0, o0_sum], sums1):
            ups.append(up_sum.finish())
            downs.append(owned(down_sum))
            got = qkv.finish()
            attns.append(
                jnp.stack([got[:, :s], got[:, s : 2 * s], got[:, 2 * s :], owned(o_sum)])
            )
        grad_attn, grad_up, grad_down = jnp.stack(attns), jnp.stack(ups), jnp.stack(downs)
        for axis in ("blk", "img"):
            j = 1
            while j < lax.axis_size(axis):
                rows = rows + swap(rows, axis, j)
                j *= 2
        vec_total = lax.dynamic_slice_in_dim(rows[:20], place * piece, piece, 1)
        vec_total = vec_total.reshape(2, 10, piece)
        bias_total = lax.dynamic_slice_in_dim(
            rows[20:28].reshape(2, ff), place * (ff // images), ff // images, 1
        )
    else:
        rows, o0_own = call(
            "vectors",
            functools.partial(vector_total_kernel, slice(piece, piece + 16)),
            many([attn0.keep, attn0.got]),
            [((32, piece), F32), ((piece, s), BF)],
        )
        o0_own = transpose_owners(o0_own)
        rows = rows + swap(rows, "blk", 1)
        rows = rows + swap(rows, "blk", 2)
        got0 = later(ffn0[0].got, grad_x, *downs1)
        downs0 = call(
            "tail",
            functools.partial(tail_kernel, [(0, slice(0, piece), 1, slice(0, piece))]),
            [(scal, "s")] + many([ffn0[0].keep, got0]),
            [((piece, s), BF)] * CYCLE,
        )
        downs0 = exchange(list(downs0))
        last = [ffn0[1].keep, attn0.keep, attn0.got, got0, o0_own] + downs0
        last += [sums1[1].keep, sums1[0].keep, got1, o1_own] + downs1
        grad_attn, grad_up, grad_down, vec_total, bias_total = call(
            "finish",
            finish_kernel,
            [(scal, "s")] + many(last + [rows]),
            [
                ((2, 4, piece, s), F32),
                ((2, piece, ffb), F32),
                ((2, s, ff // images), F32),
                ((10, 2, piece), F32),
                ((2, ff // images), F32),
            ],
        )
        grad_down, vec_total = jnp.swapaxes(grad_down, 1, 2), jnp.swapaxes(vec_total, 0, 1)

    return (
        e_b[:, None, :],
        g_b[:, None, :],
        grad_x,
        grad_m,
        grad_attn,
        grad_up,
        grad_down,
        vec_total,
        bias_total,
    )


def solution(mesh):
    rows = P("blk", "img", None)
    in_specs = (rows, rows, P("img"), P(), P(), P(), P(), P(), rows, rows)
    out_specs = (
        rows,
        rows,
        rows,
        rows,
        P(None, None, "img", "blk"),
        P(None, "img", "blk"),
        P(None, "img", "blk"),
        P(None, None, "img"),
        P(None, "img"),
    )
    return jax.shard_map(body, mesh=mesh, in_specs=in_specs, out_specs=out_specs, check_vma=False)
```
